32 devices in a mesh: expert: 8 (over z, core), hidden: 4 (over y, x).
Axes of the slice: x: 2, y: 2, z: 4, core: 2. Of those that a mesh axis runs over, the one named last changes fastest.
Arguments:
- tokens: bfloat16 [4096, 768], P('expert', 'hidden'), may hold values from -6 to 6
- routes: int32 [4096, 1], P('expert'), may hold values from 0 to 31; in each aligned block of 512 rows (0 to 511, 512 to 1023, ...) at most 32 rows name the same one
- gate_value: float32 [4096, 1], P('expert'), may hold values from 0.2 to 1
- weight_in: bfloat16 [32, 768, 3072], P('expert', None, 'hidden'), may hold values from -0.21875 to 0.21875
- weight_out: bfloat16 [32, 3072, 768], P('expert', 'hidden'), may hold values from -0.109375 to 0.109375
- cotangent: bfloat16 [4096, 768], P('expert', 'hidden'), may hold values from -6 to 6
Outputs:
- layer_out: bfloat16 [4096, 768], P('expert', 'hidden')
- grad_tokens: bfloat16 [4096, 768], P('expert', 'hidden')
- grad_weight_in: bfloat16 [32, 768, 3072], P('expert', None, 'hidden')
- grad_weight_out: bfloat16 [32, 3072, 768], P('expert', 'hidden')
The draws below stay inside these ranges and needn't reach their ends.
Inputs may be any that keep to these rules, and one draw needn't show every extreme that they name: `routes`: within each group of 512 consecutive tokens (the tokens of one index of the expert axis) no expert is chosen by more than 32 tokens; in some group some expert is chosen by exactly 32. Every expert is chosen by some token.
All inputs are finite; a program needn't handle non-finite values.
Results may differ from the reference program's by a relative error of at most 0.019.
Values may be sent and summed in bfloat16 or wider, within the bound.
No kernel may reach another device: no remote copies, remote signals or barrier semaphores. Data moves between devices by JAX's collectives and lax.ppermute only.
A program may use at most 64 MiB of HBM per device.

```python
import math
import jax
import jax.numpy as jnp
import numpy as np
from jax import lax

D = 768
H = 3072
TOK_DEV = 512
EXPERTS = 32
CAP = 32
TOKENS = 4096
N_EXPERT = 8
N_HIDDEN = 4


def level_of(stream_key, shape, cuts, smallest, largest):
    level, own = 1.0, jax.random.fold_in(stream_key, 6)
    for dim, blocks in cuts:
        draws = jnp.exp(jax.random.uniform(jax.random.fold_in(own, dim), (blocks,), jnp.float32, smallest / len(cuts), largest / len(cuts)))
        level = level * jnp.repeat(draws, shape[dim] // blocks).reshape([-1 if axis == dim else 1 for axis in range(len(shape))])
    return level


def routed_block(rng, own, number, rows, amount, top, limit, skew):
    sequence = jax.random.permutation(rng, amount)
    crowded, common = load_shares(amount, rows * top, limit, skew, True), load_shares(amount, rows * top, limit, skew, False)
    places = jnp.arange(amount)

    def named(tallies, rotation):
        used = int((tallies > 0).sum())
        fixed = max(1, used // 4)
        moved = fixed + (places - fixed + rotation * (used - fixed)) % max(1, amount - fixed)
        return jnp.zeros((amount,), jnp.int32).at[sequence[jnp.where(places < fixed, places, moved)]].set(jnp.asarray(tallies, jnp.int32))

    tallies = jnp.where(number % 4 == 0, named(crowded, number // 4), named(common, number - number // 4 - 1))
    mixed = jax.random.permutation(jax.random.fold_in(own, 3), amount)
    source_of, sink = mixed[0:amount // 2 * 2:2], mixed[1:amount // 2 * 2:2]
    margin = jnp.minimum(tallies[source_of] - 1, limit - tallies[sink]) // 2
    margin = jnp.where((source_of == sequence[0]) | (sink == sequence[0]) | (tallies[sink] == 0), 0, jnp.maximum(margin, 0))
    moved = jax.random.randint(jax.random.fold_in(own, 4), (amount // 2,), 0, 1 << 20) % (margin + 1)
    tallies = tallies.at[source_of].add(-moved).at[sink].add(moved)
    members = jnp.searchsorted(jnp.cumsum(tallies), jnp.arange(rows * top), side="right").astype(jnp.int32)
    table = members.reshape(top, rows).T
    table = table[jax.random.permutation(jax.random.fold_in(own, 1), rows)]
    rotation = jax.random.randint(jax.random.fold_in(own, 2), (rows, 1), 0, top)
    return jnp.take_along_axis(table, (jnp.arange(top)[None, :] + rotation) % top, axis=1)


def load_shares(count, total, bound, lean, full):
    weights = [(1 << 20) // math.isqrt(rank ** lean) + 1 for rank in range(1, count + 1)]
    largest = bound if full else min(bound, max(-(-total // count), total * weights[0] // sum(weights)))
    least = 1 if total - largest >= count - 1 else 0
    given, rest = [largest] + [least] * (count - 1), total - largest - least * (count - 1)
    while rest > 0:
        candidates = [i for i in range(1, count) if given[i] < largest] or [i for i in range(1, count) if given[i] < bound]
        mass, remaining = sum([weights[i] for i in candidates]), rest
        for i in candidates:
            extra = min(bound - given[i], max(1, remaining * weights[i] // mass), rest)
            given[i] = given[i] + extra
            rest = rest - extra
    return np.array(given)


def normal_values(own_key, extent, scale, bound, split=(), kind=jnp.bfloat16):
    drawn = scale * jax.random.normal(own_key, extent, jnp.float32)
    if split:
        drawn = drawn * level_of(own_key, extent, split, -0.22, 0.18)
    return jnp.clip(drawn, -bound, bound).astype(kind)


def setup_inputs(seed: int = 0) -> dict:
    key_of = jax.random.split(jax.random.key(seed), 7)
    tokens = normal_values(key_of[0], (TOKENS, D), 1.0, 6.0, ((0, 8), (1, 4)))
    routes_keys = jax.random.split(jax.random.fold_in(key_of[1], 1), TOKENS // TOK_DEV)
    routes_turns = jax.random.permutation(jax.random.fold_in(key_of[1], 3), TOKENS // TOK_DEV)
    routes = jax.vmap(lambda own, number: routed_block(jax.random.fold_in(key_of[1], 2), own, number, TOK_DEV, EXPERTS, 1, CAP, 2))(routes_keys, routes_turns).reshape((TOKENS, 1))
    gate_value = jnp.clip(0.2 + 0.8 * jax.random.uniform(key_of[2], (TOKENS, 1), jnp.float32) ** level_of(key_of[2], (TOKENS, 1), ((0, 8),), -0.2, 0.2), 0.2, 1.0)
    weight_in = normal_values(key_of[3], (EXPERTS, D, H), D ** -0.5, 0.21875, ((0, 8), (2, 4)))
    weight_out = normal_values(key_of[4], (EXPERTS, H, D), H ** -0.5, 0.109375, ((0, 8), (1, 4)))
    cotangent = normal_values(key_of[5], (TOKENS, D), 1.0, 6.0, ((0, 8), (1, 4)))
    return dict(tokens=tokens, routes=routes, gate_value=gate_value, weight_in=weight_in, weight_out=weight_out, cotangent=cotangent)


def gelu_tanh(values):
    return jax.nn.gelu(values, approximate=True)

def slot_places(routes):
    chosen = routes[:, 0].reshape(N_EXPERT, TOK_DEV)
    matches = (chosen[:, :, None] == jnp.arange(EXPERTS, dtype=jnp.int32)[None, None, :]).astype(jnp.int32)
    before = jnp.cumsum(matches, axis=1) - matches
    within = lax.optimization_barrier(jnp.sum(before * matches, axis=2))
    source = jnp.arange(N_EXPERT, dtype=jnp.int32)[:, None]
    return (chosen * (N_EXPERT * CAP) + source * CAP + within).reshape(TOKENS).astype(jnp.int32)

def shard_sum(partials):
    rounded = lax.optimization_barrier(partials.astype(jnp.bfloat16))
    return lax.optimization_barrier(jnp.sum(rounded.astype(jnp.float32), axis=0))

def one_expert(inputs):
    rows_in, rows_grad, first_weight, second_weight = inputs
    count = rows_in.shape[0]
    width = H // N_HIDDEN
    preact = jnp.dot(rows_in, first_weight, preferred_element_type=jnp.float32)
    activation, pullback = jax.vjp(gelu_tanh, preact)
    hidden_act = activation.astype(jnp.bfloat16)
    hidden_blocks = hidden_act.reshape(count, N_HIDDEN, width).astype(jnp.float32)
    second_blocks = second_weight.reshape(N_HIDDEN, width, D).astype(jnp.float32)
    expert_out = shard_sum(jnp.einsum('rnh,nhd->nrd', hidden_blocks, second_blocks)).astype(jnp.bfloat16)
    grad_hidden = jnp.dot(rows_grad, second_weight.T, preferred_element_type=jnp.float32)
    grad_pre = pullback(grad_hidden)[0].astype(jnp.bfloat16)
    grad_blocks = grad_pre.reshape(count, N_HIDDEN, width).astype(jnp.float32)
    first_blocks = first_weight.reshape(D, N_HIDDEN, width).astype(jnp.float32)
    expert_grad = shard_sum(jnp.einsum('rnh,dnh->nrd', grad_blocks, first_blocks)).astype(jnp.bfloat16)
    grad_first = jnp.dot(rows_in.T, grad_pre, preferred_element_type=jnp.float32).astype(jnp.bfloat16)
    grad_second = jnp.dot(hidden_act.T, rows_grad, preferred_element_type=jnp.float32).astype(jnp.bfloat16)
    return (expert_out, expert_grad, grad_first, grad_second)

def reference(tokens, routes, gate_value, weight_in, weight_out, cotangent):
    placed = slot_places(routes)
    total = EXPERTS * N_EXPERT * CAP
    scaled = (gate_value * cotangent.astype(jnp.float32)).astype(jnp.bfloat16)
    slot_in = jnp.zeros((total, D), jnp.bfloat16).at[placed].set(tokens).reshape(EXPERTS, N_EXPERT * CAP, D)
    slot_grad = jnp.zeros((total, D), jnp.bfloat16).at[placed].set(scaled).reshape(EXPERTS, N_EXPERT * CAP, D)
    expert_out, expert_grad, grad_weight_in, grad_weight_out = lax.map(one_expert, (slot_in, slot_grad, weight_in, weight_out))
    layer_out = (gate_value * expert_out.reshape(total, D)[placed].astype(jnp.float32)).astype(jnp.bfloat16)
    grad_tokens = expert_grad.reshape(total, D)[placed]
    return (layer_out, grad_tokens, grad_weight_in, grad_weight_out)
```

```python
import functools
import jax
import jax.numpy as jnp
from jax import lax
from jax.experimental import pallas as pl
from jax.experimental.pallas import tpu as pltpu
from jax.sharding import PartitionSpec as P

CHUNKS = 2
BF16 = jnp.bfloat16
F32 = jnp.float32


def gelu_tanh(values):
    return jax.nn.gelu(values, approximate=True)


def local_places(routes, experts, capacity):
    chosen = routes[:, 0]
    matches = (chosen[:, None] == jnp.arange(experts, dtype=jnp.int32)[None, :]).astype(jnp.int32)
    before = jnp.cumsum(matches, axis=0) - matches
    return chosen * capacity + jnp.sum(before * matches, axis=1)


def general(tokens, routes, gate_value, weight_in, weight_out, cotangent):
    owners = lax.axis_size("expert")
    blocks = lax.axis_size("hidden")
    exp_dev = weight_in.shape[0]
    experts = owners * exp_dev
    capacity = max(2, 2 * tokens.shape[0] // experts)
    slot_count = experts * capacity
    features = tokens.shape[1]
    full_width = weight_out.shape[2]
    units = weight_in.shape[2]
    line = exp_dev * capacity * features
    placed = local_places(routes, experts, capacity)
    scaled = (gate_value * cotangent.astype(F32)).astype(BF16)
    first_four = weight_in.reshape(exp_dev, blocks, features, units)
    second_four = weight_out.reshape(exp_dev, units, blocks, features)

    def to_slots(values):
        filled = jnp.zeros((slot_count, features), BF16).at[placed].set(values)
        return filled.reshape(owners, line)

    def rows_of(values):
        arrived = lax.all_to_all(to_slots(values), "expert", split_axis=0, concat_axis=0, tiled=True)
        gathered = lax.all_gather(arrived[None], "hidden", axis=0, tiled=True)
        return gathered.reshape(blocks, owners, exp_dev, capacity, features)

    def back(part):
        flat = part.reshape(blocks, owners, line).astype(BF16)
        total = lax.psum_scatter(flat, "hidden", scatter_dimension=0, tiled=True)
        total = total.astype(F32)[0].astype(BF16)
        returned = lax.all_to_all(total, "expert", split_axis=0, concat_axis=0, tiled=True)
        return returned.reshape(slot_count, features)[placed]

    rows_x = rows_of(tokens)
    rows_g = rows_of(scaled)
    preact = jnp.einsum("nsecf,enfh->sech", rows_x, first_four, preferred_element_type=F32)
    activation, pullback = jax.vjp(gelu_tanh, preact)
    hidden_act = activation.astype(BF16)
    out_part = jnp.einsum("sech,ehnf->nsecf", hidden_act, second_four, preferred_element_type=F32)
    grad_hidden = jnp.einsum("nsecf,ehnf->sech", rows_g, second_four, preferred_element_type=F32)
    grad_pre = pullback(grad_hidden)[0].astype(BF16)
    grad_part = jnp.einsum("sech,enfh->nsecf", grad_pre, first_four, preferred_element_type=F32)
    grad_weight_in = jnp.einsum("nsecf,sech->enfh", rows_x, grad_pre, preferred_element_type=F32)
    grad_weight_out = jnp.einsum("sech,nsecf->ehnf", hidden_act, rows_g, preferred_element_type=F32)
    layer_out = (gate_value * back(out_part).astype(F32)).astype(BF16)
    return (
        layer_out,
        back(grad_part),
        grad_weight_in.astype(BF16).reshape(exp_dev, full_width, units),
        grad_weight_out.astype(BF16).reshape(exp_dev, units, full_width),
    )


def column(row):
    return jnp.transpose(jnp.broadcast_to(row, (8, row.shape[1])))[:, :1]


def dispatch_kernel(exp_dev, capacity, routes_ref, gate_ref, tok_ref, cot_ref, place_ref, *chunk_refs):
    tokens = routes_ref.shape[1]
    owners = chunk_refs[0].shape[0]
    experts = owners * exp_dev
    chosen = routes_ref[...]
    matches = lax.broadcasted_iota(jnp.int32, (experts, tokens), 0) == chosen
    earlier = lax.broadcasted_iota(jnp.int32, (tokens, tokens), 0) < lax.broadcasted_iota(
        jnp.int32, (tokens, tokens), 1
    )
    before = jnp.dot(
        jnp.where(matches, 1.0, 0.0).astype(BF16),
        jnp.where(earlier, 1.0, 0.0).astype(BF16),
        preferred_element_type=F32,
    )
    within = jnp.sum(jnp.where(matches, before, 0.0), axis=0, keepdims=True).astype(jnp.int32)
    place = chosen * capacity + within
    place_ref[...] = place
    scaled = (column(gate_ref[...]) * cot_ref[...].astype(F32)).astype(BF16)
    both = jnp.concatenate([tok_ref[...], scaled], axis=1)
    for c, ref in enumerate(chunk_refs):
        rows = ref.shape[1]
        total = owners * rows
        index = lax.broadcasted_iota(jnp.int32, (total, tokens), 0)
        slot = (index // rows) * (exp_dev * capacity) + c * rows + index % rows
        hot = jnp.where(slot == place, 1.0, 0.0).astype(BF16)
        filled = jnp.dot(hot, both, preferred_element_type=F32).astype(BF16)
        ref[...] = filled.reshape(ref.shape)


def dispatch(routes, gate, tokens, cotangent, owners, exp_dev, capacity):
    count, features = tokens.shape
    rows = exp_dev // CHUNKS * capacity
    vmem = pl.BlockSpec(memory_space=pltpu.VMEM)
    return pl.pallas_call(
        functools.partial(dispatch_kernel, exp_dev, capacity),
        out_shape=[jax.ShapeDtypeStruct((1, count), jnp.int32)]
        + [jax.ShapeDtypeStruct((owners, rows, 2 * features), BF16)] * CHUNKS,
        in_specs=[vmem] * 4,
        out_specs=[vmem] * (1 + CHUNKS),
        compiler_params=pltpu.CompilerParams(vmem_limit_bytes=32 << 20),
        name="dispatch",
    )(routes.reshape(1, count), gate.reshape(1, count), tokens, cotangent)


def expert_kernel(features, h_ref, *refs):
    ins, (first_ref, second_ref), rest = refs[:4], refs[4:6], refs[6:]
    if len(rest) > 8:
        rest = rest[2:]
    outs, (grad_first_ref, grad_second_ref), (s_in, s_out) = rest[:4], rest[4:6], rest[6:8]
    mine = h_ref[0]
    rows = s_in.shape[1]
    for d, ref in enumerate(ins):
        s_in[mine ^ d] = ref[...].reshape(rows, 2 * features)
    x = jnp.concatenate([s_in[j, :, :features] for j in range(4)], axis=1)
    g = jnp.concatenate([s_in[j, :, features:] for j in range(4)], axis=1)
    first, second = first_ref[0], second_ref[0]
    nt = (((1,), (1,)), ((), ()))
    tn = (((0,), (0,)), ((), ()))
    v = jnp.dot(x, first, preferred_element_type=F32)
    root = 0.7978845608028654
    t = jnp.tanh(root * (v + 0.044715 * (v * v * v)))
    act = (0.5 * v * (1.0 + t)).astype(BF16)
    slope = 0.5 * (1.0 + t) + 0.5 * v * (1.0 - t * t) * (root * (1.0 + 3 * 0.044715 * (v * v)))
    out = jnp.dot(act, second, preferred_element_type=F32).astype(BF16)
    grad_hidden = lax.dot_general(g, second, nt, preferred_element_type=F32)
    grad_pre = (grad_hidden * slope).astype(BF16)
    grad = lax.dot_general(grad_pre, first, nt, preferred_element_type=F32).astype(BF16)
    for j in range(4):
        lanes = slice(j * features, (j + 1) * features)
        s_out[mine ^ j] = jnp.concatenate([out[:, lanes], grad[:, lanes]], axis=1)
    for d, ref in enumerate(outs):
        ref[...] = s_out[d].reshape(ref.shape)
    grad_first_ref[0] = lax.dot_general(x, grad_pre, tn, preferred_element_type=F32).astype(BF16)
    grad_second_ref[0] = lax.dot_general(act, g, tn, preferred_element_type=F32).astype(BF16)


def run_experts(chunk, mine, pieces, weight_in, weight_out, grads, capacity):
    owners, rows, wide = pieces[0].shape
    exp_dev, width, units = weight_in.shape
    per = rows // capacity
    piece = pl.BlockSpec((owners, capacity, wide), lambda e, h: (0, e, 0))
    weight = pl.BlockSpec((1, width, units), lambda e, h: (chunk * per + e, 0, 0))
    weight_2 = pl.BlockSpec((1, units, width), lambda e, h: (chunk * per + e, 0, 0))
    flops = 12 * per * owners * capacity * width * units
    return pl.pallas_call(
        functools.partial(expert_kernel, wide // 2),
        out_shape=[jax.ShapeDtypeStruct(pieces[0].shape, BF16)] * 4
        + [jax.ShapeDtypeStruct(weight_in.shape, BF16), jax.ShapeDtypeStruct(weight_out.shape, BF16)],
        grid_spec=pltpu.PrefetchScalarGridSpec(
            num_scalar_prefetch=1,
            grid=(per,),
            in_specs=[piece] * 4
            + [weight, weight_2]
            + [pl.BlockSpec(memory_space=pl.ANY)] * len(grads),
            out_specs=[piece] * 4 + [weight, weight_2],
            scratch_shapes=[pltpu.VMEM((4, owners * capacity, wide), BF16)] * 2,
        ),
        input_output_aliases={7: 4, 8: 5} if grads else {},
        compiler_params=pltpu.CompilerParams(vmem_limit_bytes=32 << 20),
        cost_estimate=pl.CostEstimate(
            flops=flops, bytes_accessed=8 * per * width * units, transcendentals=per * owners * capacity * units
        ),
        name="experts",
    )(mine, *pieces, weight_in, weight_out, *grads)


def combine_kernel(exp_dev, capacity, place_ref, gate_ref, *refs):
    chunk_refs, (out_ref, grad_ref) = refs[:-2], refs[-2:]
    tokens, features = out_ref.shape
    place = column(place_ref[...].astype(F32)).astype(jnp.int32)
    total = jnp.zeros((tokens, 2 * features), F32)
    for c, ref in enumerate(chunk_refs):
        owners, rows, wide = ref.shape
        index = lax.broadcasted_iota(jnp.int32, (tokens, owners * rows), 1)
        slot = (index // rows) * (exp_dev * capacity) + c * rows + index % rows
        hot = jnp.where(slot == place, 1.0, 0.0).astype(BF16)
        total += jnp.dot(hot, ref[...].reshape(owners * rows, wide), preferred_element_type=F32)
    out_ref[...] = (column(gate_ref[...]) * total[:, :features]).astype(BF16)
    grad_ref[...] = total[:, features:].astype(BF16)


def combine(place, gate, chunks, features, exp_dev, capacity):
    count = place.shape[1]
    vmem = pl.BlockSpec(memory_space=pltpu.VMEM)
    return pl.pallas_call(
        functools.partial(combine_kernel, exp_dev, capacity),
        out_shape=[jax.ShapeDtypeStruct((count, features), BF16)] * 2,
        in_specs=[vmem] * (2 + len(chunks)),
        out_specs=[vmem] * 2,
        compiler_params=pltpu.CompilerParams(vmem_limit_bytes=32 << 20),
        name="combine",
    )(place, gate.reshape(1, count), *chunks)


def swap(value, bit):
    return lax.ppermute(value, "hidden", [(i, i ^ bit) for i in range(4)])


def exchange(value):
    return lax.all_to_all(value, "expert", split_axis=0, concat_axis=0, tiled=True)


def add(first, *others):
    total = first.astype(F32)
    for other in others:
        total = total + other.astype(F32)
    return total.astype(BF16)


def local(tokens, routes, gate_value, weight_in, weight_out, cotangent):
    owners = lax.axis_size("expert")
    exp_dev = weight_in.shape[0]
    features = tokens.shape[1]
    capacity = max(2, 2 * tokens.shape[0] // (owners * exp_dev))
    mine = lax.axis_index("hidden").astype(jnp.int32).reshape(1)
    place, *chunks = dispatch(routes, gate_value, tokens, cotangent, owners, exp_dev, capacity)
    pieces = []
    for c, chunk in enumerate(chunks):
        own = exchange(chunk)
        near, far = (1, 2) if c % 2 == 0 else (2, 1)
        by_bit = {0: own, near: swap(own, near), far: swap(own, far)}
        by_bit[3] = swap(by_bit[near], far)
        pieces.append([by_bit[d] for d in range(4)])
    grads, returned = [], []
    for c, four in enumerate(pieces):
        *parts, grad_in, grad_out = run_experts(c, mine, four, weight_in, weight_out, grads, capacity)
        grads = [grad_in, grad_out]
        near, far = (1, 2) if c % 2 == 0 else (2, 1)
        corner = swap(parts[3], near)
        side = swap(parts[near], near)
        passed = swap(add(parts[far], corner), far)
        returned.append(exchange(add(parts[0], side, passed)))
    layer_out, grad_tokens = combine(place, gate_value, returned, features, exp_dev, capacity)
    return layer_out, grad_tokens, grads[0], grads[1]


def solution(mesh):
    in_specs = (
        P("expert", "hidden"),
        P("expert", None),
        P("expert", None),
        P("expert", None, "hidden"),
        P("expert", "hidden", None),
        P("expert", "hidden"),
    )
    out_specs = (
        P("expert", "hidden"),
        P("expert", "hidden"),
        P("expert", None, "hidden"),
        P("expert", "hidden", None),
    )

    def whole(*args):
        width, capacity = args[0].shape[1], 2 * args[0].shape[0] // args[3].shape[0]
        fits = mesh.shape["hidden"] == 4 and width % 512 == 256 and capacity % 16 == 0
        body = local if fits else general
        return jax.shard_map(body, mesh=mesh, in_specs=in_specs, out_specs=out_specs, check_vma=False)(*args)

    return whole
```

```python
import functools
import jax
import jax.numpy as jnp
from jax import lax
from jax.experimental import pallas as pl
from jax.experimental.pallas import tpu as pltpu
from jax.sharding import PartitionSpec as P

CHUNKS = 2
BF16 = jnp.bfloat16
F32 = jnp.float32


def gelu_tanh(values):
    return jax.nn.gelu(values, approximate=True)


def local_places(routes, experts, capacity):
    chosen = routes[:, 0]
    matches = (chosen[:, None] == jnp.arange(experts, dtype=jnp.int32)[None, :]).astype(jnp.int32)
    before = jnp.cumsum(matches, axis=0) - matches
    return chosen * capacity + jnp.sum(before * matches, axis=1)


def general(tokens, routes, gate_value, weight_in, weight_out, cotangent):
    owners = lax.axis_size("expert")
    blocks = lax.axis_size("hidden")
    exp_dev = weight_in.shape[0]
    experts = owners * exp_dev
    capacity = max(2, 2 * tokens.shape[0] // experts)
    slot_count = experts * capacity
    features = tokens.shape[1]
    full_width = weight_out.shape[2]
    units = weight_in.shape[2]
    line = exp_dev * capacity * features
    placed = local_places(routes, experts, capacity)
    scaled = (gate_value * cotangent.astype(F32)).astype(BF16)
    first_four = weight_in.reshape(exp_dev, blocks, features, units)
    second_four = weight_out.reshape(exp_dev, units, blocks, features)

    def to_slots(values):
        filled = jnp.zeros((slot_count, features), BF16).at[placed].set(values)
        return filled.reshape(owners, line)

    def rows_of(values):
        arrived = lax.all_to_all(to_slots(values), "expert", split_axis=0, concat_axis=0, tiled=True)
        gathered = lax.all_gather(arrived[None], "hidden", axis=0, tiled=True)
        return gathered.reshape(blocks, owners, exp_dev, capacity, features)

    def back(part):
        flat = part.reshape(blocks, owners, line).astype(BF16)
        total = lax.psum_scatter(flat, "hidden", scatter_dimension=0, tiled=True)
        total = total.astype(F32)[0].astype(BF16)
        returned = lax.all_to_all(total, "expert", split_axis=0, concat_axis=0, tiled=True)
        return returned.reshape(slot_count, features)[placed]

    rows_x = rows_of(tokens)
    rows_g = rows_of(scaled)
    preact = jnp.einsum("nsecf,enfh->sech", rows_x, first_four, preferred_element_type=F32)
    activation, pullback = jax.vjp(gelu_tanh, preact)
    hidden_act = activation.astype(BF16)
    out_part = jnp.einsum("sech,ehnf->nsecf", hidden_act, second_four, preferred_element_type=F32)
    grad_hidden = jnp.einsum("nsecf,ehnf->sech", rows_g, second_four, preferred_element_type=F32)
    grad_pre = pullback(grad_hidden)[0].astype(BF16)
    grad_part = jnp.einsum("sech,enfh->nsecf", grad_pre, first_four, preferred_element_type=F32)
    grad_weight_in = jnp.einsum("nsecf,sech->enfh", rows_x, grad_pre, preferred_element_type=F32)
    grad_weight_out = jnp.einsum("sech,nsecf->ehnf", hidden_act, rows_g, preferred_element_type=F32)
    layer_out = (gate_value * back(out_part).astype(F32)).astype(BF16)
    return (
        layer_out,
        back(grad_part),
        grad_weight_in.astype(BF16).reshape(exp_dev, full_width, units),
        grad_weight_out.astype(BF16).reshape(exp_dev, units, full_width),
    )


NT = (((1,), (1,)), ((), ()))
TN = (((0,), (0,)), ((), ()))
VMEM = pl.BlockSpec(memory_space=pltpu.VMEM)
HBM = pl.BlockSpec(memory_space=pltpu.HBM)
SMEM = pl.BlockSpec(memory_space=pltpu.SMEM)


def one_hot(place, first, count):
    rows = lax.broadcasted_iota(jnp.int32, (count, place.shape[1]), 0)
    return jnp.where(rows == place - first, 1.0, 0.0).astype(BF16)


def slot_blocks(me, offsets, exp_dev, capacity, chunk):
    per = exp_dev // CHUNKS * capacity
    return [(me ^ offset) * (exp_dev * capacity) + chunk * per for offset in offsets]


def dispatch_kernel(exp_dev, capacity, me_ref, routes_ref, gate_ref, tok_ref, cot_ref, place_ref, *refs):
    tokens = routes_ref.shape[1]
    owners = 2 * len(refs) // CHUNKS
    experts = owners * exp_dev
    per = exp_dev // CHUNKS * capacity
    chosen = routes_ref[...]
    matches = lax.broadcasted_iota(jnp.int32, (experts, tokens), 0) == chosen
    earlier = lax.broadcasted_iota(jnp.int32, (tokens, tokens), 0) < lax.broadcasted_iota(
        jnp.int32, (tokens, tokens), 1
    )
    before = jnp.dot(
        jnp.where(matches, 1.0, 0.0).astype(BF16),
        jnp.where(earlier, 1.0, 0.0).astype(BF16),
        preferred_element_type=F32,
    )
    within = jnp.sum(jnp.where(matches, before, 0.0), axis=0, keepdims=True).astype(jnp.int32)
    place = chosen * capacity + within
    place_ref[...] = place
    scaled = (gate_ref[...] * cot_ref[...].astype(F32)).astype(BF16)
    both = jnp.concatenate([tok_ref[...], scaled], axis=0)
    for i, ref in enumerate(refs):
        c, dz = divmod(i, owners // 2)
        firsts = slot_blocks(me_ref[0], (2 * dz, 2 * dz + 1), exp_dev, capacity, c)
        hot = jnp.concatenate([one_hot(place, first, per) for first in firsts], axis=0)
        filled = lax.dot_general(hot, both, NT, preferred_element_type=F32).astype(BF16)
        ref[...] = filled.reshape(ref.shape)


def dispatch(me, routes, gate, tokens, cotangent, owners, exp_dev, capacity):
    features, count = tokens.shape
    buffer = jax.ShapeDtypeStruct((2, exp_dev // CHUNKS, capacity, 2 * features), BF16)
    buffers = CHUNKS * owners // 2
    place, *buffers = pl.pallas_call(
        functools.partial(dispatch_kernel, exp_dev, capacity),
        out_shape=[jax.ShapeDtypeStruct((1, count), jnp.int32)] + [buffer] * buffers,
        in_specs=[SMEM] + [VMEM] * 4,
        out_specs=[VMEM] * (1 + buffers),
        compiler_params=pltpu.CompilerParams(vmem_limit_bytes=24 << 20),
        name="dispatch",
    )(me, routes, gate, tokens, cotangent)
    return place, [buffers[c * owners // 2 : (c + 1) * owners // 2] for c in range(CHUNKS)]


def pack_kernel(*refs):
    count = len(refs) // 2
    direct, passed, outs = refs[:-3], refs[-3], refs[-2:]
    for p, out in enumerate(outs):
        for dz, ref in enumerate(direct):
            out[dz] = ref[0, p]
            out[len(direct) + dz] = passed[dz, p]


def pack(direct, passed):
    _, per, capacity, wide = direct[0].shape
    return pl.pallas_call(
        pack_kernel,
        out_shape=[jax.ShapeDtypeStruct((2 * len(direct), capacity, wide), BF16)] * per,
        in_specs=[VMEM] * (1 + len(direct)),
        out_specs=[VMEM] * per,
        name="pack",
    )(*direct, passed)


def expert_kernel(chunk, features, h_ref, *refs):
    per = 2
    ins, (first_hbm, second_hbm) = refs[: 4 * per], refs[4 * per : 4 * per + 2]
    rest = refs[4 * per + 2 :] if chunk == 0 else refs[4 * per + 4 :]
    outs, (grad_first_hbm, grad_second_hbm) = rest[: 4 * per], rest[4 * per : 4 * per + 2]
    s_in, s_out, first_buf, second_buf, grad_first_buf, grad_second_buf, in_sem, out_sem = rest[4 * per + 2 :]
    mine = h_ref[0]
    rows = s_in.shape[1]
    loads = []
    for p in range(per):
        e = chunk * per + p
        loads.append(
            (
                pltpu.make_async_copy(first_hbm.at[e], first_buf.at[p], in_sem.at[p, 0]),
                pltpu.make_async_copy(second_hbm.at[e], second_buf.at[p], in_sem.at[p, 1]),
            )
        )
        for load in loads[-1]:
            load.start()
    stores = []
    for p in range(per):
        e = chunk * per + p
        for d in range(4):
            s_in[mine ^ d] = ins[4 * p + d][...].reshape(rows, 2 * features)
        x = jnp.concatenate([s_in[j, :, :features] for j in range(4)], axis=1)
        g = jnp.concatenate([s_in[j, :, features:] for j in range(4)], axis=1)
        loads[p][0].wait()
        first = first_buf[p]
        v = jnp.dot(x, first, preferred_element_type=F32)
        loads[p][1].wait()
        second = second_buf[p]
        grad_hidden = lax.dot_general(g, second, NT, preferred_element_type=F32)
        root = 0.7978845608028654
        square = v * v
        t = jnp.tanh(root * (v + 0.044715 * (v * square)))
        act = (0.5 * v * (1.0 + t)).astype(BF16)
        slope = 0.5 * (1.0 + t) + 0.5 * v * (1.0 - t * t) * (root * (1.0 + 3 * 0.044715 * square))
        grad_pre = (grad_hidden * slope).astype(BF16)
        out = jnp.dot(act, second, preferred_element_type=F32).astype(BF16)
        grad = lax.dot_general(grad_pre, first, NT, preferred_element_type=F32).astype(BF16)
        for j in range(4):
            lanes = slice(j * features, (j + 1) * features)
            s_out[mine ^ j] = jnp.concatenate([out[:, lanes], grad[:, lanes]], axis=1)
        for d in range(4):
            outs[4 * p + d][...] = s_out[d].reshape(outs[4 * p + d].shape)
        grad_first_buf[p] = lax.dot_general(x, grad_pre, TN, preferred_element_type=F32).astype(BF16)
        stores.append(pltpu.make_async_copy(grad_first_buf.at[p], grad_first_hbm.at[e], out_sem.at[p, 0]))
        stores[-1].start()
        grad_second_buf[p] = lax.dot_general(act, g, TN, preferred_element_type=F32).astype(BF16)
        stores.append(pltpu.make_async_copy(grad_second_buf.at[p], grad_second_hbm.at[e], out_sem.at[p, 1]))
        stores[-1].start()
    for store in stores:
        store.wait()


def run_experts(chunk, mine, pieces, weight_in, weight_out, grads):
    sources, capacity, wide = pieces[0].shape
    exp_dev, width, units = weight_in.shape
    per = exp_dev // CHUNKS
    rows = sources * capacity
    count = len(pieces)
    return pl.pallas_call(
        functools.partial(expert_kernel, chunk, wide // 2),
        out_shape=[jax.ShapeDtypeStruct(pieces[0].shape, BF16)] * count
        + [jax.ShapeDtypeStruct(weight_in.shape, BF16), jax.ShapeDtypeStruct(weight_out.shape, BF16)],
        in_specs=[SMEM] + [VMEM] * count + [HBM] * (2 + len(grads)),
        out_specs=[VMEM] * count + [HBM] * 2,
        scratch_shapes=[pltpu.VMEM((4, rows, wide), BF16)] * 2
        + [pltpu.VMEM((per, width, units), BF16), pltpu.VMEM((per, units, width), BF16)] * 2
        + [pltpu.SemaphoreType.DMA((per, 2))] * 2,
        input_output_aliases={count + 3: count, count + 4: count + 1} if grads else {},
        compiler_params=pltpu.CompilerParams(vmem_limit_bytes=32 << 20),
        cost_estimate=pl.CostEstimate(
            flops=12 * per * rows * width * units,
            bytes_accessed=8 * per * width * units,
            transcendentals=per * rows * units,
        ),
        name="experts",
    )(mine, *pieces, weight_in, weight_out, *grads)


def sum_kernel(*refs):
    per = (len(refs) - 1) // 3
    half = refs[0].shape[0] // 2
    terms, outs = refs[:6], refs[6:]
    for p in range(2):
        own, side, passed = (ref[...].astype(F32) for ref in terms[3 * p : 3 * p + 3])
        total = (own + side + passed).astype(BF16)
        for dz, out in enumerate(outs):
            out[0, p] = total[dz]
            out[1, p] = total[half + dz]


def sum_rows(terms):
    sources, capacity, wide = terms[0].shape
    return pl.pallas_call(
        sum_kernel,
        out_shape=[jax.ShapeDtypeStruct((2, 2, capacity, wide), BF16)] * (sources // 2),
        in_specs=[VMEM] * 6,
        out_specs=[VMEM] * (sources // 2),
        name="sum_rows",
    )(*terms)


def combine_kernel(exp_dev, capacity, me_ref, place_ref, gate_ref, *refs):
    ins, (out_ref, grad_ref) = refs[:-2], refs[-2:]
    features, tokens = out_ref.shape
    steps = len(ins) // CHUNKS - 1
    per = exp_dev // CHUNKS * capacity
    place = place_ref[...]
    total = jnp.zeros((2 * features, tokens), F32)
    for c in range(CHUNKS):
        *direct, passed = ins[c * (steps + 1) : (c + 1) * (steps + 1)]
        wide = passed.shape[-1]
        rows = [ref[0].reshape(per, wide) for ref in direct] + [passed[dz].reshape(per, wide) for dz in range(steps)]
        offsets = [2 * dz for dz in range(steps)] + [2 * dz + 1 for dz in range(steps)]
        firsts = slot_blocks(me_ref[0], offsets, exp_dev, capacity, c)
        hot = jnp.concatenate([one_hot(place, first, per) for first in firsts], axis=0)
        total += lax.dot_general(jnp.concatenate(rows, axis=0), hot, TN, preferred_element_type=F32)
    out_ref[...] = (gate_ref[...] * total[:features]).astype(BF16)
    grad_ref[...] = total[features:].astype(BF16)


def combine(me, place, gate, returned, features, exp_dev, capacity):
    count = place.shape[1]
    return pl.pallas_call(
        functools.partial(combine_kernel, exp_dev, capacity),
        out_shape=[jax.ShapeDtypeStruct((features, count), BF16)] * 2,
        in_specs=[SMEM] + [VMEM] * (2 + len(returned)),
        out_specs=[VMEM] * 2,
        compiler_params=pltpu.CompilerParams(vmem_limit_bytes=24 << 20),
        name="combine",
    )(me, place, gate, *returned)


def swap(value, axis, bits):
    size = lax.axis_size(axis)
    return lax.ppermute(value, axis, [(i, i ^ bits) for i in range(size)])


def exchange(buffers):
    direct = [buffers[0]] + [None] * (len(buffers) - 1)
    for dz in reversed(range(1, len(buffers))):
        direct[dz] = swap(buffers[dz], "expert", 2 * dz)
    passed = swap(jnp.stack([ref[1] for ref in direct]), "expert", 1)
    return direct, passed


def gather(own, near, far):
    by_bit = {0: own, near: swap(own, "hidden", near), far: swap(own, "hidden", far)}
    by_bit[3] = swap(by_bit[near], "hidden", far)
    return [by_bit[d] for d in range(4)]


def scatter_sum(parts, near, far):
    corner = swap(parts[3], "hidden", near)
    side = swap(parts[near], "hidden", near)
    both = (parts[far].astype(F32) + corner.astype(F32)).astype(BF16)
    return [parts[0], side, swap(both, "hidden", far)]


def local(tokens, routes, gate_value, weight_in, weight_out, cotangent):
    owners = lax.axis_size("expert")
    exp_dev = weight_in.shape[0]
    count, features = tokens.shape
    capacity = 2 * count // (owners * exp_dev)
    mine = lax.axis_index("hidden").astype(jnp.int32).reshape(1)
    me = lax.axis_index("expert").astype(jnp.int32).reshape(1)
    gate = gate_value.reshape(1, count)
    place, chunks = dispatch(
        me, routes.reshape(1, count), gate, tokens.T, cotangent.T, owners, exp_dev, capacity
    )
    ways = ((1, 2), (2, 1))
    pieces = []
    for buffers in chunks:
        if pieces:
            buffers, pieces[-1] = lax.optimization_barrier((buffers, pieces[-1]))
        halves = pack(*exchange(buffers))
        pieces.append(list(halves))
    pieces = [[piece for own, way in zip(halves, ways) for piece in gather(own, *way)] for halves in pieces]
    grads, returned = [], []
    for c, eight in enumerate(pieces):
        *parts, grad_in, grad_out = run_experts(c, mine, eight, weight_in, weight_out, grads)
        grads = [grad_in, grad_out]
        terms = [term for p, way in enumerate(ways) for term in scatter_sum(parts[4 * p : 4 * p + 4], *way)]
        direct, passed = exchange(sum_rows(terms))
        returned += [*direct, passed]
    layer_out, grad_tokens = combine(me, place, gate, returned, features, exp_dev, capacity)
    return layer_out.T, grad_tokens.T, grads[0], grads[1]


def solution(mesh):
    in_specs = (
        P("expert", "hidden"),
        P("expert", None),
        P("expert", None),
        P("expert", None, "hidden"),
        P("expert", "hidden", None),
        P("expert", "hidden"),
    )
    out_specs = (
        P("expert", "hidden"),
        P("expert", "hidden"),
        P("expert", None, "hidden"),
        P("expert", "hidden", None),
    )

    def whole(*args):
        wide = 2 * args[0].shape[1] // mesh.shape["hidden"]
        capacity = 2 * args[0].shape[0] // args[3].shape[0]
        four = mesh.shape["hidden"] == 4 and args[3].shape[0] == 4 * mesh.shape["expert"]
        fits = four and mesh.shape["expert"] in (2, 4, 8, 16) and wide % 128 == 0 and capacity % 16 == 0
        body = local if fits else general
        return jax.shard_map(body, mesh=mesh, in_specs=in_specs, out_specs=out_specs, check_vma=False)(*args)

    return whole
```

```python
import functools
import jax
import jax.numpy as jnp
from jax import lax
from jax.experimental import pallas as pl
from jax.experimental.pallas import tpu as pltpu
from jax.sharding import PartitionSpec as P

CHUNKS = 2
BF16 = jnp.bfloat16
F32 = jnp.float32


def gelu_tanh(values):
    return jax.nn.gelu(values, approximate=True)


def local_places(routes, experts, capacity):
    chosen = routes[:, 0]
    matches = (chosen[:, None] == jnp.arange(experts, dtype=jnp.int32)[None, :]).astype(jnp.int32)
    before = jnp.cumsum(matches, axis=0) - matches
    return chosen * capacity + jnp.sum(before * matches, axis=1)


def general(tokens, routes, gate_value, weight_in, weight_out, cotangent):
    owners = lax.axis_size("expert")
    blocks = lax.axis_size("hidden")
    exp_dev = weight_in.shape[0]
    experts = owners * exp_dev
    capacity = max(2, 2 * tokens.shape[0] // experts)
    slot_count = experts * capacity
    features = tokens.shape[1]
    full_width = weight_out.shape[2]
    units = weight_in.shape[2]
    line = exp_dev * capacity * features
    placed = local_places(routes, experts, capacity)
    scaled = (gate_value * cotangent.astype(F32)).astype(BF16)
    first_four = weight_in.reshape(exp_dev, blocks, features, units)
    second_four = weight_out.reshape(exp_dev, units, blocks, features)

    def to_slots(values):
        filled = jnp.zeros((slot_count, features), BF16).at[placed].set(values)
        return filled.reshape(owners, line)

    def rows_of(values):
        arrived = lax.all_to_all(to_slots(values), "expert", split_axis=0, concat_axis=0, tiled=True)
        gathered = lax.all_gather(arrived[None], "hidden", axis=0, tiled=True)
        return gathered.reshape(blocks, owners, exp_dev, capacity, features)

    def back(part):
        flat = part.reshape(blocks, owners, line).astype(BF16)
        total = lax.psum_scatter(flat, "hidden", scatter_dimension=0, tiled=True)
        total = total.astype(F32)[0].astype(BF16)
        returned = lax.all_to_all(total, "expert", split_axis=0, concat_axis=0, tiled=True)
        return returned.reshape(slot_count, features)[placed]

    rows_x = rows_of(tokens)
    rows_g = rows_of(scaled)
    preact = jnp.einsum("nsecf,enfh->sech", rows_x, first_four, preferred_element_type=F32)
    activation, pullback = jax.vjp(gelu_tanh, preact)
    hidden_act = activation.astype(BF16)
    out_part = jnp.einsum("sech,ehnf->nsecf", hidden_act, second_four, preferred_element_type=F32)
    grad_hidden = jnp.einsum("nsecf,ehnf->sech", rows_g, second_four, preferred_element_type=F32)
    grad_pre = pullback(grad_hidden)[0].astype(BF16)
    grad_part = jnp.einsum("sech,enfh->nsecf", grad_pre, first_four, preferred_element_type=F32)
    grad_weight_in = jnp.einsum("nsecf,sech->enfh", rows_x, grad_pre, preferred_element_type=F32)
    grad_weight_out = jnp.einsum("sech,nsecf->ehnf", hidden_act, rows_g, preferred_element_type=F32)
    layer_out = (gate_value * back(out_part).astype(F32)).astype(BF16)
    return (
        layer_out,
        back(grad_part),
        grad_weight_in.astype(BF16).reshape(exp_dev, full_width, units),
        grad_weight_out.astype(BF16).reshape(exp_dev, units, full_width),
    )


NT = (((1,), (1,)), ((), ()))
TN = (((0,), (0,)), ((), ()))
VMEM = pl.BlockSpec(memory_space=pltpu.VMEM)
HBM = pl.BlockSpec(memory_space=pltpu.HBM)
SMEM = pl.BlockSpec(memory_space=pltpu.SMEM)
WAYS = ((1, 2), (2, 1))


def one_hot(place, first, count):
    rows = lax.broadcasted_iota(jnp.int32, (count, place.shape[1]), 0)
    return jnp.where(rows == place - first, 1.0, 0.0).astype(BF16)


def slot_blocks(me, offsets, exp_dev, capacity, chunk):
    per = exp_dev // CHUNKS * capacity
    return [(me ^ offset) * (exp_dev * capacity) + chunk * per for offset in offsets]


def dispatch_kernel(exp_dev, capacity, me_ref, *refs):
    ins, place_ref, gate_ref, rest = refs[:4], refs[4], refs[5], refs[6:]
    buffers, (routes_buf, tok_buf, cot_buf, sems) = rest[:-4], rest[-4:]
    loads = [
        pltpu.make_async_copy(source, target, sems.at[i])
        for i, (source, target) in enumerate(zip(ins, (routes_buf, gate_ref, tok_buf, cot_buf)))
    ]
    for load in loads:
        load.start()
    tokens = routes_buf.shape[1]
    owners = 2 * len(buffers) // CHUNKS
    experts = owners * exp_dev
    per = exp_dev // CHUNKS * capacity
    earlier = lax.broadcasted_iota(jnp.int32, (tokens, tokens), 0) < lax.broadcasted_iota(
        jnp.int32, (tokens, tokens), 1
    )
    earlier = jnp.where(earlier, 1.0, 0.0).astype(BF16)
    loads[0].wait()
    chosen = routes_buf[...]
    matches = lax.broadcasted_iota(jnp.int32, (experts, tokens), 0) == chosen
    before = jnp.dot(jnp.where(matches, 1.0, 0.0).astype(BF16), earlier, preferred_element_type=F32)
    within = jnp.sum(jnp.where(matches, before, 0.0), axis=0, keepdims=True).astype(jnp.int32)
    place = chosen * capacity + within
    place_ref[...] = place
    for load in loads[1:]:
        load.wait()
    scaled = (gate_ref[...] * cot_buf[...].astype(F32)).astype(BF16)
    both = jnp.concatenate([tok_buf[...], scaled], axis=0)
    for i, ref in enumerate(buffers):
        c, dz = divmod(i, owners // 2)
        firsts = slot_blocks(me_ref[0], (2 * dz, 2 * dz + 1), exp_dev, capacity, c)
        hot = jnp.concatenate([one_hot(place, first, per) for first in firsts], axis=0)
        filled = lax.dot_general(hot, both, NT, preferred_element_type=F32).astype(BF16)
        ref[...] = filled.reshape(ref.shape)


def in_hbm(*arrays):
    return [pltpu.with_memory_space_constraint(array, pltpu.HBM) for array in arrays]


def dispatch(me, routes, gate, tokens, cotangent, owners, exp_dev, capacity):
    features, count = tokens.shape
    buffer = jax.ShapeDtypeStruct((2, exp_dev // CHUNKS, capacity, 2 * features), BF16)
    buffers = CHUNKS * owners // 2
    place, gate, *buffers = pl.pallas_call(
        functools.partial(dispatch_kernel, exp_dev, capacity),
        out_shape=[jax.ShapeDtypeStruct((1, count), jnp.int32), jax.ShapeDtypeStruct((1, count), F32)]
        + [buffer] * buffers,
        in_specs=[SMEM] + [HBM] * 4,
        out_specs=[VMEM] * (2 + buffers),
        scratch_shapes=[pltpu.VMEM((1, count), jnp.int32)]
        + [pltpu.VMEM((features, count), BF16)] * 2
        + [pltpu.SemaphoreType.DMA((4,))],
        compiler_params=pltpu.CompilerParams(vmem_limit_bytes=24 << 20),
        name="dispatch",
    )(me, *in_hbm(routes, gate, tokens, cotangent))
    return place, gate, [buffers[c * owners // 2 : (c + 1) * owners // 2] for c in range(CHUNKS)]


def pack_kernel(*refs):
    count = len(refs) // 2
    direct, passed, outs = refs[:-3], refs[-3], refs[-2:]
    for p, out in enumerate(outs):
        for dz, ref in enumerate(direct):
            out[dz] = ref[0, p]
            out[len(direct) + dz] = passed[dz, p]


def pack(direct, passed):
    _, per, capacity, wide = direct[0].shape
    return pl.pallas_call(
        pack_kernel,
        out_shape=[jax.ShapeDtypeStruct((2 * len(direct), capacity, wide), BF16)] * per,
        in_specs=[VMEM] * (1 + len(direct)),
        out_specs=[VMEM] * per,
        compiler_params=pltpu.CompilerParams(vmem_limit_bytes=8 << 20),
        name="pack",
    )(*direct, passed)


def expert_kernel(chunk, features, h_ref, *refs):
    per = len(WAYS)
    ins, (first_hbm, second_hbm) = refs[: 3 * per], refs[3 * per : 3 * per + 2]
    rest = refs[3 * per + 2 :] if chunk == 0 else refs[3 * per + 4 :]
    outs, (grad_first_hbm, grad_second_hbm) = rest[: 3 * per], rest[3 * per : 3 * per + 2]
    s_in, s_out, first_buf, second_buf, grad_first_buf, grad_second_buf, in_sem, out_sem = rest[3 * per + 2 :]
    mine = h_ref[0]
    rows = s_in.shape[1]
    loads = []
    for p in range(per):
        e = chunk * per + p
        loads.append(
            (
                pltpu.make_async_copy(first_hbm.at[e], first_buf.at[p], in_sem.at[p, 0]),
                pltpu.make_async_copy(second_hbm.at[e], second_buf.at[p], in_sem.at[p, 1]),
            )
        )
        for load in loads[-1]:
            load.start()
    stores = []
    for p in range(per):
        e = chunk * per + p
        near, far = WAYS[p]
        own_ref, near_ref, far_ref = ins[3 * p : 3 * p + 3]
        s_in[mine] = own_ref[...].reshape(rows, 2 * features)
        s_in[mine ^ near] = near_ref[...].reshape(rows, 2 * features)
        s_in[mine ^ far] = far_ref[0].reshape(rows, 2 * features)
        s_in[mine ^ 3] = far_ref[1].reshape(rows, 2 * features)
        x = jnp.concatenate([s_in[j, :, :features] for j in range(4)], axis=1)
        g = jnp.concatenate([s_in[j, :, features:] for j in range(4)], axis=1)
        loads[p][0].wait()
        first = first_buf[p]
        v = jnp.dot(x, first, preferred_element_type=F32)
        loads[p][1].wait()
        second = second_buf[p]
        grad_hidden = lax.dot_general(g, second, NT, preferred_element_type=F32)
        root = 0.7978845608028654
        square = v * v
        t = jnp.tanh(root * (v + 0.044715 * (v * square)))
        act = (0.5 * v * (1.0 + t)).astype(BF16)
        slope = 0.5 * (1.0 + t) + 0.5 * v * (1.0 - t * t) * (root * (1.0 + 3 * 0.044715 * square))
        grad_pre = (grad_hidden * slope).astype(BF16)
        out = jnp.dot(act, second, preferred_element_type=F32).astype(BF16)
        grad = lax.dot_general(grad_pre, first, NT, preferred_element_type=F32).astype(BF16)
        for j in range(4):
            lanes = slice(j * features, (j + 1) * features)
            s_out[mine ^ j] = jnp.concatenate([out[:, lanes], grad[:, lanes]], axis=1)
        own_ref, far_ref, near_ref = outs[3 * p : 3 * p + 3]
        own_ref[...] = s_out[0].reshape(own_ref.shape)
        far_ref[...] = s_out[far].reshape(own_ref.shape)
        near_ref[0] = s_out[near].reshape(own_ref.shape)
        near_ref[1] = s_out[3].reshape(own_ref.shape)
        grad_first_buf[p] = lax.dot_general(x, grad_pre, TN, preferred_element_type=F32).astype(BF16)
        stores.append(pltpu.make_async_copy(grad_first_buf.at[p], grad_first_hbm.at[e], out_sem.at[p, 0]))
        stores[-1].start()
        grad_second_buf[p] = lax.dot_general(act, g, TN, preferred_element_type=F32).astype(BF16)
        stores.append(pltpu.make_async_copy(grad_second_buf.at[p], grad_second_hbm.at[e], out_sem.at[p, 1]))
        stores[-1].start()
    for store in stores:
        store.wait()


def run_experts(chunk, mine, pieces, weight_in, weight_out, grads):
    sources, capacity, wide = pieces[0].shape
    exp_dev, width, units = weight_in.shape
    per = exp_dev // CHUNKS
    rows = sources * capacity
    count = len(pieces)
    return pl.pallas_call(
        functools.partial(expert_kernel, chunk, wide // 2),
        out_shape=[jax.ShapeDtypeStruct(piece.shape, BF16) for piece in pieces]
        + [jax.ShapeDtypeStruct(weight_in.shape, BF16), jax.ShapeDtypeStruct(weight_out.shape, BF16)],
        in_specs=[SMEM] + [VMEM] * count + [HBM] * (2 + len(grads)),
        out_specs=[VMEM] * count + [HBM] * 2,
        scratch_shapes=[pltpu.VMEM((4, rows, wide), BF16)] * 2
        + [pltpu.VMEM((per, width, units), BF16), pltpu.VMEM((per, units, width), BF16)] * 2
        + [pltpu.SemaphoreType.DMA((per, 2))] * 2,
        input_output_aliases={count + 3: count, count + 4: count + 1} if grads else {},
        compiler_params=pltpu.CompilerParams(vmem_limit_bytes=32 << 20),
        cost_estimate=pl.CostEstimate(
            flops=12 * per * rows * width * units,
            bytes_accessed=8 * per * width * units,
            transcendentals=per * rows * units,
        ),
        name="experts",
    )(mine, *pieces, *in_hbm(weight_in, weight_out), *grads)


def sum_kernel(*refs):
    half = refs[0].shape[0] // 2
    terms, outs = refs[:6], refs[6:]
    for p in range(2):
        own, side, passed = terms[3 * p : 3 * p + 3]
        total = own[...].astype(F32) + side[0].astype(F32) + passed[...].astype(F32)
        total = total.astype(BF16)
        for dz, out in enumerate(outs):
            out[0, p] = total[dz]
            out[1, p] = total[half + dz]


def sum_rows(terms):
    sources, capacity, wide = terms[0].shape
    return pl.pallas_call(
        sum_kernel,
        out_shape=[jax.ShapeDtypeStruct((2, 2, capacity, wide), BF16)] * (sources // 2),
        in_specs=[VMEM] * 6,
        out_specs=[VMEM] * (sources // 2),
        compiler_params=pltpu.CompilerParams(vmem_limit_bytes=8 << 20),
        name="sum_rows",
    )(*terms)


def combine_kernel(exp_dev, capacity, me_ref, place_ref, gate_ref, *refs):
    ins, (out_ref, grad_ref) = refs[:-2], refs[-2:]
    features, tokens = out_ref.shape
    steps = len(ins) // CHUNKS - 1
    per = exp_dev // CHUNKS * capacity
    place = place_ref[...]
    total = jnp.zeros((2 * features, tokens), F32)
    for c in range(CHUNKS):
        *direct, passed = ins[c * (steps + 1) : (c + 1) * (steps + 1)]
        wide = passed.shape[-1]
        rows = [ref[0].reshape(per, wide) for ref in direct] + [passed[dz].reshape(per, wide) for dz in range(steps)]
        offsets = [2 * dz for dz in range(steps)] + [2 * dz + 1 for dz in range(steps)]
        firsts = slot_blocks(me_ref[0], offsets, exp_dev, capacity, c)
        hot = jnp.concatenate([one_hot(place, first, per) for first in firsts], axis=0)
        total += lax.dot_general(jnp.concatenate(rows, axis=0), hot, TN, preferred_element_type=F32)
    out_ref[...] = (gate_ref[...] * total[:features]).astype(BF16)
    grad_ref[...] = total[features:].astype(BF16)


def combine(me, place, gate, returned, features, exp_dev, capacity):
    count = place.shape[1]
    return pl.pallas_call(
        functools.partial(combine_kernel, exp_dev, capacity),
        out_shape=[jax.ShapeDtypeStruct((features, count), BF16)] * 2,
        in_specs=[SMEM] + [VMEM] * (2 + len(returned)),
        out_specs=[VMEM] * 2,
        compiler_params=pltpu.CompilerParams(vmem_limit_bytes=24 << 20),
        name="combine",
    )(me, place, gate, *returned)


def swap(value, axis, bits):
    size = lax.axis_size(axis)
    return lax.ppermute(value, axis, [(i, i ^ bits) for i in range(size)])


def along_z(buffers):
    direct = [buffers[0]] + [None] * (len(buffers) - 1)
    for dz in reversed(range(1, len(buffers))):
        direct[dz] = swap(buffers[dz], "expert", 2 * dz)
    return direct


def between_cores(direct, *earlier):
    return swap(after(jnp.stack([rows[1] for rows in direct]), *earlier), "expert", 1)


def after(values, *earlier):
    return lax.optimization_barrier((values, earlier))[0]


def local(tokens, routes, gate_value, weight_in, weight_out, cotangent):
    owners = lax.axis_size("expert")
    exp_dev = weight_in.shape[0]
    count, features = tokens.shape
    capacity = 2 * count // (owners * exp_dev)
    mine = lax.axis_index("hidden").astype(jnp.int32).reshape(1)
    me = lax.axis_index("expert").astype(jnp.int32).reshape(1)
    place, gate, chunks = dispatch(
        me, routes.reshape(1, count), gate_value.reshape(1, count), tokens.T, cotangent.T, owners, exp_dev, capacity
    )
    own, near, far = [], [], []
    for c in range(CHUNKS):
        buffers = after(chunks[c], own[c - 1]) if c else chunks[c]
        direct = along_z(buffers)
        own.append(pack(direct, between_cores(direct, *near[:c])))
        near.append([swap(rows, "hidden", way[0]) for rows, way in zip(own[c], WAYS)])
    for c in range(CHUNKS):
        pairs = [jnp.stack(pair) for pair in zip(own[c], near[c])]
        far.append([swap(pair, "hidden", way[1]) for pair, way in zip(pairs, WAYS)])
    grads, returned, landed = [], [], []
    for c in range(CHUNKS):
        pieces = [piece for three in zip(own[c], near[c], far[c]) for piece in three]
        if c + 1 < CHUNKS:
            pieces = after(pieces, near[c + 1])
        parts = run_experts(c, mine, pieces, weight_in, weight_out, grads)
        parts, grads = parts[:-2], parts[-2:]
        ahead = far[c + 1] if c + 1 < CHUNKS else landed
        pairs = after([parts[2], parts[5]], ahead)
        landed = [swap(pair, "hidden", way[0]) for pair, way in zip(pairs, WAYS)]
        both = [
            (parts[3 * p + 1].astype(F32) + landed[p][1].astype(F32)).astype(BF16) for p in range(len(WAYS))
        ]
        passed = [swap(rows, "hidden", way[1]) for rows, way in zip(both, WAYS)]
        totals = sum_rows([parts[0], landed[0], passed[0], parts[3], landed[1], passed[1]])
        if returned:
            returned[-1].append(between_cores(returned[-1], totals))
        returned.append(along_z(totals))
    returned[-1].append(between_cores(returned[-1]))
    returned = [rows for chunk in returned for rows in chunk]
    layer_out, grad_tokens = combine(me, place, gate, returned, features, exp_dev, capacity)
    return layer_out.T, grad_tokens.T, grads[0], grads[1]


def solution(mesh):
    in_specs = (
        P("expert", "hidden"),
        P("expert", None),
        P("expert", None),
        P("expert", None, "hidden"),
        P("expert", "hidden", None),
        P("expert", "hidden"),
    )
    out_specs = (
        P("expert", "hidden"),
        P("expert", "hidden"),
        P("expert", None, "hidden"),
        P("expert", "hidden", None),
    )

    def whole(*args):
        wide = 2 * args[0].shape[1] // mesh.shape["hidden"]
        capacity = 2 * args[0].shape[0] // args[3].shape[0]
        four = mesh.shape["hidden"] == 4 and args[3].shape[0] == 4 * mesh.shape["expert"]
        fits = four and mesh.shape["expert"] in (2, 4, 8, 16) and wide % 128 == 0 and capacity % 16 == 0
        body = local if fits else general
        return jax.shard_map(body, mesh=mesh, in_specs=in_specs, out_specs=out_specs, check_vma=False)(*args)

    return whole
```

```python
import functools
import jax
import jax.numpy as jnp
from jax import lax
from jax.experimental import pallas as pl
from jax.experimental.pallas import tpu as pltpu
from jax.sharding import PartitionSpec as P

CHUNKS = 2
BF16 = jnp.bfloat16
F32 = jnp.float32


def gelu_tanh(values):
    return jax.nn.gelu(values, approximate=True)


def local_places(routes, experts, capacity):
    chosen = routes[:, 0]
    matches = (chosen[:, None] == jnp.arange(experts, dtype=jnp.int32)[None, :]).astype(jnp.int32)
    before = jnp.cumsum(matches, axis=0) - matches
    return chosen * capacity + jnp.sum(before * matches, axis=1)


def general(tokens, routes, gate_value, weight_in, weight_out, cotangent):
    owners = lax.axis_size("expert")
    blocks = lax.axis_size("hidden")
    exp_dev = weight_in.shape[0]
    experts = owners * exp_dev
    capacity = max(2, 2 * tokens.shape[0] // experts)
    slot_count = experts * capacity
    features = tokens.shape[1]
    full_width = weight_out.shape[2]
    units = weight_in.shape[2]
    line = exp_dev * capacity * features
    placed = local_places(routes, experts, capacity)
    scaled = (gate_value * cotangent.astype(F32)).astype(BF16)
    first_four = weight_in.reshape(exp_dev, blocks, features, units)
    second_four = weight_out.reshape(exp_dev, units, blocks, features)

    def to_slots(values):
        filled = jnp.zeros((slot_count, features), BF16).at[placed].set(values)
        return filled.reshape(owners, line)

    def rows_of(values):
        arrived = lax.all_to_all(to_slots(values), "expert", split_axis=0, concat_axis=0, tiled=True)
        gathered = lax.all_gather(arrived[None], "hidden", axis=0, tiled=True)
        return gathered.reshape(blocks, owners, exp_dev, capacity, features)

    def back(part):
        flat = part.reshape(blocks, owners, line).astype(BF16)
        total = lax.psum_scatter(flat, "hidden", scatter_dimension=0, tiled=True)
        total = total.astype(F32)[0].astype(BF16)
        returned = lax.all_to_all(total, "expert", split_axis=0, concat_axis=0, tiled=True)
        return returned.reshape(slot_count, features)[placed]

    rows_x = rows_of(tokens)
    rows_g = rows_of(scaled)
    preact = jnp.einsum("nsecf,enfh->sech", rows_x, first_four, preferred_element_type=F32)
    activation, pullback = jax.vjp(gelu_tanh, preact)
    hidden_act = activation.astype(BF16)
    out_part = jnp.einsum("sech,ehnf->nsecf", hidden_act, second_four, preferred_element_type=F32)
    grad_hidden = jnp.einsum("nsecf,ehnf->sech", rows_g, second_four, preferred_element_type=F32)
    grad_pre = pullback(grad_hidden)[0].astype(BF16)
    grad_part = jnp.einsum("sech,enfh->nsecf", grad_pre, first_four, preferred_element_type=F32)
    grad_weight_in = jnp.einsum("nsecf,sech->enfh", rows_x, grad_pre, preferred_element_type=F32)
    grad_weight_out = jnp.einsum("sech,nsecf->ehnf", hidden_act, rows_g, preferred_element_type=F32)
    layer_out = (gate_value * back(out_part).astype(F32)).astype(BF16)
    return (
        layer_out,
        back(grad_part),
        grad_weight_in.astype(BF16).reshape(exp_dev, full_width, units),
        grad_weight_out.astype(BF16).reshape(exp_dev, units, full_width),
    )


NT = (((1,), (1,)), ((), ()))
TN = (((0,), (0,)), ((), ()))
VMEM = pl.BlockSpec(memory_space=pltpu.VMEM)
HBM = pl.BlockSpec(memory_space=pltpu.HBM)
SMEM = pl.BlockSpec(memory_space=pltpu.SMEM)
WAYS = ((1, 2), (2, 1))


def one_hot(place, first, count):
    rows = lax.broadcasted_iota(jnp.int32, (count, place.shape[1]), 0)
    return jnp.where(rows == place - first, 1.0, 0.0).astype(BF16)


def slot_blocks(me, offsets, line, skip=0):
    return [(me ^ offset) * line + skip for offset in offsets]


def dispatch_kernel(exp_dev, capacity, me_ref, *refs):
    ins, place_ref, gate_ref, rest = refs[:4], refs[4], refs[5], refs[6:]
    buffers, (routes_buf, tok_buf, cot_buf, sems) = rest[:-4], rest[-4:]
    loads = [
        pltpu.make_async_copy(source, target, sems.at[i])
        for i, (source, target) in enumerate(zip(ins, (routes_buf, gate_ref, tok_buf, cot_buf)))
    ]
    for load in loads:
        load.start()
    tokens = routes_buf.shape[1]
    experts = 2 * len(buffers) * exp_dev
    line = exp_dev * capacity
    earlier = lax.broadcasted_iota(jnp.int32, (tokens, tokens), 0) < lax.broadcasted_iota(
        jnp.int32, (tokens, tokens), 1
    )
    earlier = jnp.where(earlier, 1.0, 0.0).astype(BF16)
    loads[0].wait()
    chosen = routes_buf[...]
    matches = lax.broadcasted_iota(jnp.int32, (experts, tokens), 0) == chosen
    before = jnp.dot(jnp.where(matches, 1.0, 0.0).astype(BF16), earlier, preferred_element_type=F32)
    within = jnp.sum(jnp.where(matches, before, 0.0), axis=0, keepdims=True).astype(jnp.int32)
    place = chosen * capacity + within
    place_ref[...] = place
    for load in loads[1:]:
        load.wait()
    scaled = (gate_ref[...] * cot_buf[...].astype(F32)).astype(BF16)
    both = jnp.concatenate([tok_buf[...], scaled], axis=0)
    for dz, ref in enumerate(buffers):
        firsts = slot_blocks(me_ref[0], (2 * dz, 2 * dz + 1), line)
        hot = jnp.concatenate([one_hot(place, first, line) for first in firsts], axis=0)
        filled = lax.dot_general(hot, both, NT, preferred_element_type=F32).astype(BF16)
        ref[...] = filled.reshape(ref.shape)


def in_hbm(*arrays):
    return [pltpu.with_memory_space_constraint(array, pltpu.HBM) for array in arrays]


def dispatch(me, routes, gate, tokens, cotangent, owners, exp_dev, capacity):
    features, count = tokens.shape
    buffer = jax.ShapeDtypeStruct((2, exp_dev, capacity, 2 * features), BF16)
    buffers = owners // 2
    place, gate, *buffers = pl.pallas_call(
        functools.partial(dispatch_kernel, exp_dev, capacity),
        out_shape=[jax.ShapeDtypeStruct((1, count), jnp.int32), jax.ShapeDtypeStruct((1, count), F32)]
        + [buffer] * buffers,
        in_specs=[SMEM] + [HBM] * 4,
        out_specs=[VMEM] * (2 + buffers),
        scratch_shapes=[pltpu.VMEM((1, count), jnp.int32)]
        + [pltpu.VMEM((features, count), BF16)] * 2
        + [pltpu.SemaphoreType.DMA((4,))],
        compiler_params=pltpu.CompilerParams(vmem_limit_bytes=24 << 20),
        name="dispatch",
    )(me, *in_hbm(routes, gate, tokens, cotangent))
    return place, gate, buffers


def pack_kernel(*refs):
    per = refs[0].shape[1]
    direct, passed, outs = refs[: -per - 1], refs[-per - 1], refs[-per:]
    for p, out in enumerate(outs):
        for dz, ref in enumerate(direct):
            out[dz] = ref[0, p]
            out[len(direct) + dz] = passed[dz, p]


def pack(direct, passed):
    _, per, capacity, wide = direct[0].shape
    return pl.pallas_call(
        pack_kernel,
        out_shape=[jax.ShapeDtypeStruct((2 * len(direct), capacity, wide), BF16)] * per,
        in_specs=[VMEM] * (1 + len(direct)),
        out_specs=[VMEM] * per,
        compiler_params=pltpu.CompilerParams(vmem_limit_bytes=8 << 20),
        name="pack",
    )(*direct, passed)


def load_kernel(*refs):
    count = (len(refs) - 1) // 2
    sems = refs[-1]
    loads = [pltpu.make_async_copy(refs[i], refs[count + i], sems.at[i]) for i in range(count)]
    for load in loads:
        load.start()
    for load in loads:
        load.wait()


def load(*arrays):
    return pl.pallas_call(
        load_kernel,
        out_shape=[jax.ShapeDtypeStruct(array.shape, array.dtype) for array in arrays],
        in_specs=[HBM] * len(arrays),
        out_specs=[VMEM] * len(arrays),
        scratch_shapes=[pltpu.SemaphoreType.DMA((len(arrays),))],
        compiler_params=pltpu.CompilerParams(vmem_limit_bytes=16 << 20),
        name="load",
    )(*in_hbm(*arrays))


def expert_kernel(expert, features, way, h_ref, *refs):
    ins, (first_ref, second_ref), outs, saved, (s_in, s_out) = refs[:3], refs[3:5], refs[5:8], refs[8:12], refs[12:]
    mine = h_ref[0]
    rows = s_in.shape[1]
    near, far = way
    own_ref, near_ref, far_ref = ins
    s_in[mine] = own_ref[...].reshape(rows, 2 * features)
    s_in[mine ^ near] = near_ref[...].reshape(rows, 2 * features)
    s_in[mine ^ far] = far_ref[0].reshape(rows, 2 * features)
    s_in[mine ^ 3] = far_ref[1].reshape(rows, 2 * features)
    x = jnp.concatenate([s_in[j, :, :features] for j in range(4)], axis=1)
    g = jnp.concatenate([s_in[j, :, features:] for j in range(4)], axis=1)
    first, second = first_ref[expert], second_ref[expert]
    v = jnp.dot(x, first, preferred_element_type=F32)
    grad_hidden = lax.dot_general(g, second, NT, preferred_element_type=F32)
    root = 0.7978845608028654
    square = v * v
    t = jnp.tanh(root * (v + 0.044715 * (v * square)))
    act = (0.5 * v * (1.0 + t)).astype(BF16)
    slope = 0.5 * (1.0 + t) + 0.5 * v * (1.0 - t * t) * (root * (1.0 + 3 * 0.044715 * square))
    grad_pre = (grad_hidden * slope).astype(BF16)
    out = jnp.dot(act, second, preferred_element_type=F32).astype(BF16)
    grad = lax.dot_general(grad_pre, first, NT, preferred_element_type=F32).astype(BF16)
    for j in range(4):
        lanes = slice(j * features, (j + 1) * features)
        s_out[mine ^ j] = jnp.concatenate([out[:, lanes], grad[:, lanes]], axis=1)
    own_ref, far_ref, near_ref = outs
    own_ref[...] = s_out[0].reshape(own_ref.shape)
    far_ref[...] = s_out[far].reshape(own_ref.shape)
    near_ref[0] = s_out[near].reshape(own_ref.shape)
    near_ref[1] = s_out[3].reshape(own_ref.shape)
    for ref, value in zip(saved, (x, g, act, grad_pre)):
        ref[...] = value


def run_expert(expert, way, mine, pieces, first, second):
    sources, capacity, wide = pieces[0].shape
    _, width, units = first.shape
    rows = sources * capacity
    results = pl.pallas_call(
        functools.partial(expert_kernel, expert, wide // 2, way),
        out_shape=[jax.ShapeDtypeStruct(piece.shape, BF16) for piece in pieces]
        + [jax.ShapeDtypeStruct((rows, n), BF16) for n in (width, width, units, units)],
        in_specs=[SMEM] + [VMEM] * 5,
        out_specs=[VMEM] * 7,
        scratch_shapes=[pltpu.VMEM((4, rows, wide), BF16)] * 2,
        compiler_params=pltpu.CompilerParams(vmem_limit_bytes=16 << 20),
        cost_estimate=pl.CostEstimate(
            flops=8 * rows * width * units, bytes_accessed=4 * width * units, transcendentals=rows * units
        ),
        name="expert",
    )(mine, *pieces, first, second)
    return results[:3], results[3:]


def weight_kernel(first_expert, per, *refs):
    saved, rest = refs[: 4 * per], refs[-6:]
    grad_first_hbm, grad_second_hbm, first_buf, second_buf, sems = rest[-5:]
    stores = []
    for p in range(per):
        x, g, act, grad_pre = (ref[...] for ref in saved[4 * p : 4 * p + 4])
        first_buf[p] = lax.dot_general(x, grad_pre, TN, preferred_element_type=F32).astype(BF16)
        stores.append(pltpu.make_async_copy(first_buf.at[p], grad_first_hbm.at[first_expert + p], sems.at[p, 0]))
        stores[-1].start()
        second_buf[p] = lax.dot_general(act, g, TN, preferred_element_type=F32).astype(BF16)
        stores.append(pltpu.make_async_copy(second_buf.at[p], grad_second_hbm.at[first_expert + p], sems.at[p, 1]))
        stores[-1].start()
    for store in stores:
        store.wait()


def weight_grads(chunk, saved, weight_in, weight_out, grads):
    per = len(saved) // 4
    rows, width = saved[0].shape
    units = weight_in.shape[2]
    count = 4 * per
    return pl.pallas_call(
        functools.partial(weight_kernel, chunk * per, per),
        out_shape=[jax.ShapeDtypeStruct(array.shape, BF16) for array in (weight_in, weight_out)],
        in_specs=[VMEM] * count + [HBM] * len(grads),
        out_specs=[HBM] * 2,
        scratch_shapes=[pltpu.VMEM((per, width, units), BF16), pltpu.VMEM((per, units, width), BF16)]
        + [pltpu.SemaphoreType.DMA((per, 2))],
        input_output_aliases={count: 0, count + 1: 1} if grads else {},
        compiler_params=pltpu.CompilerParams(vmem_limit_bytes=20 << 20),
        cost_estimate=pl.CostEstimate(
            flops=4 * per * rows * width * units, bytes_accessed=4 * per * width * units, transcendentals=0
        ),
        name="weight_grads",
    )(*saved, *grads)


def sum_kernel(*refs):
    half = refs[0].shape[0] // 2
    terms, outs = refs[:6], refs[6:]
    for p in range(2):
        own, side, passed = terms[3 * p : 3 * p + 3]
        total = own[...].astype(F32) + side[0].astype(F32) + passed[...].astype(F32)
        total = total.astype(BF16)
        for dz, out in enumerate(outs):
            out[0, p] = total[dz]
            out[1, p] = total[half + dz]


def sum_rows(terms):
    sources, capacity, wide = terms[0].shape
    return pl.pallas_call(
        sum_kernel,
        out_shape=[jax.ShapeDtypeStruct((2, 2, capacity, wide), BF16)] * (sources // 2),
        in_specs=[VMEM] * 6,
        out_specs=[VMEM] * (sources // 2),
        compiler_params=pltpu.CompilerParams(vmem_limit_bytes=8 << 20),
        name="sum_rows",
    )(*terms)


def combine_kernel(exp_dev, capacity, me_ref, place_ref, gate_ref, *refs):
    ins, (out_ref, grad_ref) = refs[:-2], refs[-2:]
    features, tokens = out_ref.shape
    steps = len(ins) // CHUNKS - 1
    per = exp_dev // CHUNKS * capacity
    place = place_ref[...]
    total = jnp.zeros((2 * features, tokens), F32)
    for c in range(CHUNKS):
        *direct, passed = ins[c * (steps + 1) : (c + 1) * (steps + 1)]
        wide = passed.shape[-1]
        rows = [ref[0].reshape(per, wide) for ref in direct] + [passed[dz].reshape(per, wide) for dz in range(steps)]
        offsets = [2 * dz for dz in range(steps)] + [2 * dz + 1 for dz in range(steps)]
        firsts = slot_blocks(me_ref[0], offsets, exp_dev * capacity, c * per)
        hot = jnp.concatenate([one_hot(place, first, per) for first in firsts], axis=0)
        total += lax.dot_general(jnp.concatenate(rows, axis=0), hot, TN, preferred_element_type=F32)
    out_ref[...] = (gate_ref[...] * total[:features]).astype(BF16)
    grad_ref[...] = total[features:].astype(BF16)


def combine(me, place, gate, returned, features, exp_dev, capacity):
    count = place.shape[1]
    return pl.pallas_call(
        functools.partial(combine_kernel, exp_dev, capacity),
        out_shape=[jax.ShapeDtypeStruct((features, count), BF16)] * 2,
        in_specs=[SMEM] + [VMEM] * (2 + len(returned)),
        out_specs=[VMEM] * 2,
        compiler_params=pltpu.CompilerParams(vmem_limit_bytes=24 << 20),
        name="combine",
    )(me, place, gate, *returned)


def swap(value, axis, bits):
    size = lax.axis_size(axis)
    return lax.ppermute(value, axis, [(i, i ^ bits) for i in range(size)])


def along_z(buffers):
    direct = [buffers[0]] + [None] * (len(buffers) - 1)
    for dz in reversed(range(1, len(buffers))):
        direct[dz] = swap(buffers[dz], "expert", 2 * dz)
    return direct


def between_cores(direct, *earlier):
    return swap(after(jnp.stack([rows[1] for rows in direct]), *earlier), "expert", 1)


def after(values, *earlier):
    return lax.optimization_barrier((values, earlier))[0]


def local(tokens, routes, gate_value, weight_in, weight_out, cotangent):
    owners = lax.axis_size("expert")
    exp_dev = weight_in.shape[0]
    count, features = tokens.shape
    capacity = 2 * count // (owners * exp_dev)
    mine = lax.axis_index("hidden").astype(jnp.int32).reshape(1)
    me = lax.axis_index("expert").astype(jnp.int32).reshape(1)
    place, gate, buffers = dispatch(
        me, routes.reshape(1, count), gate_value.reshape(1, count), tokens.T, cotangent.T, owners, exp_dev, capacity
    )
    first, second = load(weight_in, weight_out)
    direct = along_z(buffers)
    rows = pack(direct, between_cores(direct, first, second))
    per = exp_dev // CHUNKS
    own, near, far = [rows[per * c : per * (c + 1)] for c in range(CHUNKS)], [], []
    for c in range(CHUNKS):
        near.append([swap(rows, "hidden", way[0]) for rows, way in zip(own[c], WAYS)])
    for c in range(CHUNKS):
        pairs = [jnp.stack(pair) for pair in zip(own[c], near[c])]
        far.append([swap(pair, "hidden", way[1]) for pair, way in zip(pairs, WAYS)])
    parts, saved = [], []
    landed, both, passed = [], [], []
    for c in range(CHUNKS):
        parts.append([])
        for p, way in enumerate(WAYS):
            pieces = [own[c][p], near[c][p], far[c][p]]
            if c + 1 < CHUNKS:
                pieces = after(pieces, near[c + 1])
            part, save = run_expert(len(WAYS) * c + p, way, mine, pieces, first, second)
            parts[c].append(part)
            saved.append(save)
        ahead = far[c + 1] if c + 1 < CHUNKS else both[c - 1]
        pairs = after([part[2] for part in parts[c]], ahead)
        landed.append([swap(pair, "hidden", way[0]) for pair, way in zip(pairs, WAYS)])
        both.append([(part[1].astype(F32) + pair[1].astype(F32)).astype(BF16) for part, pair in zip(parts[c], landed[c])])
        passed.append([swap(rows, "hidden", way[1]) for rows, way in zip(both[c], WAYS)])
    grads, returned = [], []
    for c in range(CHUNKS):
        made_of = [rows for save in saved[len(WAYS) * c : len(WAYS) * (c + 1)] for rows in save]
        made_of = after(made_of, saved[-1])
        grads = weight_grads(c, made_of, weight_in, weight_out, grads)
        kept = after([part[0] for part in parts[c]], grads)
        totals = sum_rows([rows for three in zip(kept, landed[c], passed[c]) for rows in three])
        if returned:
            returned[-1].append(between_cores(returned[-1], totals))
        returned.append(along_z(totals))
    returned[-1].append(between_cores(returned[-1]))
    returned = [rows for chunk in returned for rows in chunk]
    layer_out, grad_tokens = combine(me, place, gate, returned, features, exp_dev, capacity)
    return layer_out.T, grad_tokens.T, grads[0], grads[1]


def solution(mesh):
    in_specs = (
        P("expert", "hidden"),
        P("expert", None),
        P("expert", None),
        P("expert", None, "hidden"),
        P("expert", "hidden", None),
        P("expert", "hidden"),
    )
    out_specs = (
        P("expert", "hidden"),
        P("expert", "hidden"),
        P("expert", None, "hidden"),
        P("expert", "hidden", None),
    )

    def whole(*args):
        wide = 2 * args[0].shape[1] // mesh.shape["hidden"]
        capacity = 2 * args[0].shape[0] // args[3].shape[0]
        four = mesh.shape["hidden"] == 4 and args[3].shape[0] == 4 * mesh.shape["expert"]
        fits = four and mesh.shape["expert"] in (2, 4, 8, 16) and wide % 128 == 0 and capacity % 16 == 0
        body = local if fits else general
        return jax.shard_map(body, mesh=mesh, in_specs=in_specs, out_specs=out_specs, check_vma=False)(*args)

    return whole
```

```python
import functools
import jax
import jax.numpy as jnp
from jax import lax
from jax.experimental import pallas as pl
from jax.experimental.pallas import tpu as pltpu
from jax.sharding import PartitionSpec as P

CHUNKS = 2
BF16 = jnp.bfloat16
F32 = jnp.float32


def gelu_tanh(values):
    return jax.nn.gelu(values, approximate=True)


def local_places(routes, experts, capacity):
    chosen = routes[:, 0]
    matches = (chosen[:, None] == jnp.arange(experts, dtype=jnp.int32)[None, :]).astype(jnp.int32)
    before = jnp.cumsum(matches, axis=0) - matches
    return chosen * capacity + jnp.sum(before * matches, axis=1)


def general(tokens, routes, gate_value, weight_in, weight_out, cotangent):
    owners = lax.axis_size("expert")
    blocks = lax.axis_size("hidden")
    exp_dev = weight_in.shape[0]
    experts = owners * exp_dev
    capacity = max(2, 2 * tokens.shape[0] // experts)
    slot_count = experts * capacity
    features = tokens.shape[1]
    full_width = weight_out.shape[2]
    units = weight_in.shape[2]
    line = exp_dev * capacity * features
    placed = local_places(routes, experts, capacity)
    scaled = (gate_value * cotangent.astype(F32)).astype(BF16)
    first_four = weight_in.reshape(exp_dev, blocks, features, units)
    second_four = weight_out.reshape(exp_dev, units, blocks, features)

    def to_slots(values):
        filled = jnp.zeros((slot_count, features), BF16).at[placed].set(values)
        return filled.reshape(owners, line)

    def rows_of(values):
        arrived = lax.all_to_all(to_slots(values), "expert", split_axis=0, concat_axis=0, tiled=True)
        gathered = lax.all_gather(arrived[None], "hidden", axis=0, tiled=True)
        return gathered.reshape(blocks, owners, exp_dev, capacity, features)

    def back(part):
        flat = part.reshape(blocks, owners, line).astype(BF16)
        total = lax.psum_scatter(flat, "hidden", scatter_dimension=0, tiled=True)
        total = total.astype(F32)[0].astype(BF16)
        returned = lax.all_to_all(total, "expert", split_axis=0, concat_axis=0, tiled=True)
        return returned.reshape(slot_count, features)[placed]

    rows_x = rows_of(tokens)
    rows_g = rows_of(scaled)
    preact = jnp.einsum("nsecf,enfh->sech", rows_x, first_four, preferred_element_type=F32)
    activation, pullback = jax.vjp(gelu_tanh, preact)
    hidden_act = activation.astype(BF16)
    out_part = jnp.einsum("sech,ehnf->nsecf", hidden_act, second_four, preferred_element_type=F32)
    grad_hidden = jnp.einsum("nsecf,ehnf->sech", rows_g, second_four, preferred_element_type=F32)
    grad_pre = pullback(grad_hidden)[0].astype(BF16)
    grad_part = jnp.einsum("sech,enfh->nsecf", grad_pre, first_four, preferred_element_type=F32)
    grad_weight_in = jnp.einsum("nsecf,sech->enfh", rows_x, grad_pre, preferred_element_type=F32)
    grad_weight_out = jnp.einsum("sech,nsecf->ehnf", hidden_act, rows_g, preferred_element_type=F32)
    layer_out = (gate_value * back(out_part).astype(F32)).astype(BF16)
    return (
        layer_out,
        back(grad_part),
        grad_weight_in.astype(BF16).reshape(exp_dev, full_width, units),
        grad_weight_out.astype(BF16).reshape(exp_dev, units, full_width),
    )


NT = (((1,), (1,)), ((), ()))
TN = (((0,), (0,)), ((), ()))
VMEM = pl.BlockSpec(memory_space=pltpu.VMEM)
HBM = pl.BlockSpec(memory_space=pltpu.HBM)
WAYS = ((1, 2), (2, 1))


def one_hot(place, first, count):
    rows = lax.broadcasted_iota(jnp.int32, (count, place.shape[1]), 0)
    return jnp.where(rows == place - first, 1.0, 0.0).astype(BF16)


def slot_blocks(me, offsets, line, skip=0):
    return [(me ^ offset) * line + skip for offset in offsets]


def dispatch_kernel(exp_dev, capacity, *refs):
    ins, place_ref, gate_ref, rest = refs[:4], refs[4], refs[5], refs[6:]
    buffers, (routes_buf, tok_buf, cot_buf, sems) = rest[:-4], rest[-4:]
    loads = [
        pltpu.make_async_copy(source, target, sems.at[i])
        for i, (source, target) in enumerate(zip(ins, (routes_buf, gate_ref, tok_buf, cot_buf)))
    ]
    for load in loads:
        load.start()
    tokens = routes_buf.shape[1]
    experts = 2 * len(buffers) * exp_dev
    line = exp_dev * capacity
    me = lax.axis_index("expert")
    earlier = lax.broadcasted_iota(jnp.int32, (tokens, tokens), 0) < lax.broadcasted_iota(
        jnp.int32, (tokens, tokens), 1
    )
    earlier = jnp.where(earlier, 1.0, 0.0).astype(BF16)
    loads[0].wait()
    chosen = routes_buf[...]
    matches = lax.broadcasted_iota(jnp.int32, (experts, tokens), 0) == chosen
    before = jnp.dot(jnp.where(matches, 1.0, 0.0).astype(BF16), earlier, preferred_element_type=F32)
    within = jnp.sum(jnp.where(matches, before, 0.0), axis=0, keepdims=True).astype(jnp.int32)
    place = chosen * capacity + within
    place_ref[...] = place
    for load in loads[1:]:
        load.wait()
    scaled = (gate_ref[...] * cot_buf[...].astype(F32)).astype(BF16)
    both = jnp.concatenate([tok_buf[...], scaled], axis=0)
    for dz, ref in enumerate(buffers):
        firsts = slot_blocks(me, (2 * dz, 2 * dz + 1), line)
        hot = jnp.concatenate([one_hot(place, first, line) for first in firsts], axis=0)
        filled = lax.dot_general(hot, both, NT, preferred_element_type=F32).astype(BF16)
        ref[...] = filled.reshape(ref.shape)


def in_hbm(*arrays):
    return [pltpu.with_memory_space_constraint(array, pltpu.HBM) for array in arrays]


def dispatch(routes, gate, tokens, cotangent, owners, exp_dev, capacity):
    features, count = tokens.shape
    buffer = jax.ShapeDtypeStruct((2, exp_dev, capacity, 2 * features), BF16)
    buffers = owners // 2
    place, gate, *buffers = pl.pallas_call(
        functools.partial(dispatch_kernel, exp_dev, capacity),
        out_shape=[jax.ShapeDtypeStruct((1, count), jnp.int32), jax.ShapeDtypeStruct((1, count), F32)]
        + [buffer] * buffers,
        in_specs=[HBM] * 4,
        out_specs=[VMEM] * (2 + buffers),
        scratch_shapes=[pltpu.VMEM((1, count), jnp.int32)]
        + [pltpu.VMEM((features, count), BF16)] * 2
        + [pltpu.SemaphoreType.DMA((4,))],
        compiler_params=pltpu.CompilerParams(vmem_limit_bytes=24 << 20),
        name="dispatch",
    )(*in_hbm(routes, gate, tokens, cotangent))
    return place, gate, buffers


def pack_kernel(*refs):
    per = refs[0].shape[1]
    direct, passed, outs = refs[: -per - 1], refs[-per - 1], refs[-per:]
    for p, out in enumerate(outs):
        for dz, ref in enumerate(direct):
            out[dz] = ref[0, p]
            out[len(direct) + dz] = passed[dz, p]


def pack(direct, passed):
    _, per, capacity, wide = direct[0].shape
    return pl.pallas_call(
        pack_kernel,
        out_shape=[jax.ShapeDtypeStruct((2 * len(direct), capacity, wide), BF16)] * per,
        in_specs=[VMEM] * (1 + len(direct)),
        out_specs=[VMEM] * per,
        compiler_params=pltpu.CompilerParams(vmem_limit_bytes=8 << 20),
        name="pack",
    )(*direct, passed)


def load_kernel(*refs):
    count = (len(refs) - 1) // 2
    sems = refs[-1]
    loads = [pltpu.make_async_copy(refs[i], refs[count + i], sems.at[i]) for i in range(count)]
    for load in loads:
        load.start()
    for load in loads:
        load.wait()


def load(*arrays):
    return pl.pallas_call(
        load_kernel,
        out_shape=[jax.ShapeDtypeStruct(array.shape, array.dtype) for array in arrays],
        in_specs=[HBM] * len(arrays),
        out_specs=[VMEM] * len(arrays),
        scratch_shapes=[pltpu.SemaphoreType.DMA((len(arrays),))],
        compiler_params=pltpu.CompilerParams(vmem_limit_bytes=16 << 20),
        name="load",
    )(*in_hbm(*arrays))


def expert_kernel(expert, features, way, *refs):
    ins, (first_ref, second_ref), outs, saved, (s_in, s_out) = refs[:3], refs[3:5], refs[5:8], refs[8:12], refs[12:]
    mine = lax.axis_index("hidden")
    rows = s_in.shape[1]
    near, far = way
    own_ref, near_ref, far_ref = ins
    s_in[mine] = own_ref[...].reshape(rows, 2 * features)
    s_in[mine ^ near] = near_ref[...].reshape(rows, 2 * features)
    s_in[mine ^ far] = far_ref[0].reshape(rows, 2 * features)
    s_in[mine ^ 3] = far_ref[1].reshape(rows, 2 * features)
    x = jnp.concatenate([s_in[j, :, :features] for j in range(4)], axis=1)
    g = jnp.concatenate([s_in[j, :, features:] for j in range(4)], axis=1)
    first, second = first_ref[expert], second_ref[expert]
    v = jnp.dot(x, first, preferred_element_type=F32)
    grad_hidden = lax.dot_general(g, second, NT, preferred_element_type=F32)
    root = 0.7978845608028654
    square = v * v
    t = jnp.tanh(root * (v + 0.044715 * (v * square)))
    act = (0.5 * v * (1.0 + t)).astype(BF16)
    slope = 0.5 * (1.0 + t) + 0.5 * v * (1.0 - t * t) * (root * (1.0 + 3 * 0.044715 * square))
    grad_pre = (grad_hidden * slope).astype(BF16)
    out = jnp.dot(act, second, preferred_element_type=F32).astype(BF16)
    grad = lax.dot_general(grad_pre, first, NT, preferred_element_type=F32).astype(BF16)
    for j in range(4):
        lanes = slice(j * features, (j + 1) * features)
        s_out[mine ^ j] = jnp.concatenate([out[:, lanes], grad[:, lanes]], axis=1)
    own_ref, far_ref, near_ref = outs
    own_ref[...] = s_out[0].reshape(own_ref.shape)
    far_ref[...] = s_out[far].reshape(own_ref.shape)
    near_ref[0] = s_out[near].reshape(own_ref.shape)
    near_ref[1] = s_out[3].reshape(own_ref.shape)
    for ref, value in zip(saved, (x, g, act, grad_pre)):
        ref[...] = value


def run_expert(expert, way, pieces, first, second):
    sources, capacity, wide = pieces[0].shape
    _, width, units = first.shape
    rows = sources * capacity
    results = pl.pallas_call(
        functools.partial(expert_kernel, expert, wide // 2, way),
        out_shape=[jax.ShapeDtypeStruct(piece.shape, BF16) for piece in pieces]
        + [jax.ShapeDtypeStruct((rows, n), BF16) for n in (width, width, units, units)],
        in_specs=[VMEM] * 5,
        out_specs=[VMEM] * 7,
        scratch_shapes=[pltpu.VMEM((4, rows, wide), BF16)] * 2,
        compiler_params=pltpu.CompilerParams(vmem_limit_bytes=16 << 20),
        cost_estimate=pl.CostEstimate(
            flops=8 * rows * width * units, bytes_accessed=4 * width * units, transcendentals=rows * units
        ),
        name="expert",
    )(*pieces, first, second)
    return results[:3], results[3:]


def weight_kernel(first_expert, per, *refs):
    saved, rest = refs[: 4 * per], refs[-6:]
    grad_first_hbm, grad_second_hbm, first_buf, second_buf, sems = rest[-5:]
    stores = []
    for p in range(per):
        x, g, act, grad_pre = (ref[...] for ref in saved[4 * p : 4 * p + 4])
        first_buf[p] = lax.dot_general(x, grad_pre, TN, preferred_element_type=F32).astype(BF16)
        stores.append(pltpu.make_async_copy(first_buf.at[p], grad_first_hbm.at[first_expert + p], sems.at[p, 0]))
        stores[-1].start()
        second_buf[p] = lax.dot_general(act, g, TN, preferred_element_type=F32).astype(BF16)
        stores.append(pltpu.make_async_copy(second_buf.at[p], grad_second_hbm.at[first_expert + p], sems.at[p, 1]))
        stores[-1].start()
    for store in stores:
        store.wait()


def weight_grads(chunk, saved, weight_in, weight_out, grads):
    per = len(saved) // 4
    rows, width = saved[0].shape
    units = weight_in.shape[2]
    count = 4 * per
    return pl.pallas_call(
        functools.partial(weight_kernel, chunk * per, per),
        out_shape=[jax.ShapeDtypeStruct(array.shape, BF16) for array in (weight_in, weight_out)],
        in_specs=[VMEM] * count + [HBM] * len(grads),
        out_specs=[HBM] * 2,
        scratch_shapes=[pltpu.VMEM((per, width, units), BF16), pltpu.VMEM((per, units, width), BF16)]
        + [pltpu.SemaphoreType.DMA((per, 2))],
        input_output_aliases={count: 0, count + 1: 1} if grads else {},
        compiler_params=pltpu.CompilerParams(vmem_limit_bytes=20 << 20),
        cost_estimate=pl.CostEstimate(
            flops=4 * per * rows * width * units, bytes_accessed=4 * per * width * units, transcendentals=0
        ),
        name="weight_grads",
    )(*saved, *grads)


def sum_kernel(*refs):
    half = refs[0].shape[0] // 2
    terms, outs = refs[:6], refs[6:]
    for p in range(2):
        own, side, passed = terms[3 * p : 3 * p + 3]
        total = own[...].astype(F32) + side[0].astype(F32) + passed[...].astype(F32)
        total = total.astype(BF16)
        for dz, out in enumerate(outs):
            out[0, p] = total[dz]
            out[1, p] = total[half + dz]


def sum_rows(terms):
    sources, capacity, wide = terms[0].shape
    return pl.pallas_call(
        sum_kernel,
        out_shape=[jax.ShapeDtypeStruct((2, 2, capacity, wide), BF16)] * (sources // 2),
        in_specs=[VMEM] * 6,
        out_specs=[VMEM] * (sources // 2),
        compiler_params=pltpu.CompilerParams(vmem_limit_bytes=8 << 20),
        name="sum_rows",
    )(*terms)


def combine_kernel(exp_dev, capacity, place_ref, gate_ref, *refs):
    ins, (out_ref, grad_ref) = refs[:-2], refs[-2:]
    features, tokens = out_ref.shape
    steps = len(ins) // CHUNKS - 1
    per = exp_dev // CHUNKS * capacity
    place = place_ref[...]
    total = jnp.zeros((2 * features, tokens), F32)
    for c in range(CHUNKS):
        *direct, passed = ins[c * (steps + 1) : (c + 1) * (steps + 1)]
        wide = passed.shape[-1]
        rows = [ref[0].reshape(per, wide) for ref in direct] + [passed[dz].reshape(per, wide) for dz in range(steps)]
        offsets = [2 * dz for dz in range(steps)] + [2 * dz + 1 for dz in range(steps)]
        firsts = slot_blocks(lax.axis_index("expert"), offsets, exp_dev * capacity, c * per)
        hot = jnp.concatenate([one_hot(place, first, per) for first in firsts], axis=0)
        total += lax.dot_general(jnp.concatenate(rows, axis=0), hot, TN, preferred_element_type=F32)
    out_ref[...] = (gate_ref[...] * total[:features]).astype(BF16)
    grad_ref[...] = total[features:].astype(BF16)


def combine(place, gate, returned, features, exp_dev, capacity):
    count = place.shape[1]
    return pl.pallas_call(
        functools.partial(combine_kernel, exp_dev, capacity),
        out_shape=[jax.ShapeDtypeStruct((features, count), BF16)] * 2,
        in_specs=[VMEM] * (2 + len(returned)),
        out_specs=[VMEM] * 2,
        compiler_params=pltpu.CompilerParams(vmem_limit_bytes=24 << 20),
        name="combine",
    )(place, gate, *returned)


def swap(value, axis, bits):
    size = lax.axis_size(axis)
    return lax.ppermute(value, axis, [(i, i ^ bits) for i in range(size)])


def along_z(buffers):
    direct = [buffers[0]] + [None] * (len(buffers) - 1)
    for dz in reversed(range(1, len(buffers))):
        direct[dz] = swap(buffers[dz], "expert", 2 * dz)
    return direct


def between_cores(direct, *earlier):
    return swap(jnp.stack([rows[1] for rows in after(direct, *earlier)]), "expert", 1)


def after(values, *earlier):
    return lax.optimization_barrier((values, earlier))[0]


def local(tokens, routes, gate_value, weight_in, weight_out, cotangent):
    owners = lax.axis_size("expert")
    exp_dev = weight_in.shape[0]
    count, features = tokens.shape
    capacity = 2 * count // (owners * exp_dev)
    place, gate, buffers = dispatch(
        routes.reshape(1, count), gate_value.reshape(1, count), tokens.T, cotangent.T, owners, exp_dev, capacity
    )
    first, second = load(weight_in, weight_out)
    direct = along_z(buffers)
    rows = pack(direct, between_cores(direct, first, second))
    per = exp_dev // CHUNKS
    own, near, far = [rows[per * c : per * (c + 1)] for c in range(CHUNKS)], [], []
    for c in range(CHUNKS):
        near.append([swap(rows, "hidden", way[0]) for rows, way in zip(own[c], WAYS)])
    for c in range(CHUNKS):
        pairs = [jnp.stack(pair) for pair in zip(own[c], near[c])]
        far.append([swap(pair, "hidden", way[1]) for pair, way in zip(pairs, WAYS)])
    parts, saved = [], []
    landed, both, passed = [], [], []
    for c in range(CHUNKS):
        parts.append([])
        for p, way in enumerate(WAYS):
            pieces = [own[c][p], near[c][p], far[c][p]]
            if c + 1 < CHUNKS:
                pieces = after(pieces, near[c + 1])
            part, save = run_expert(len(WAYS) * c + p, way, pieces, first, second)
            parts[c].append(part)
            saved.append(save)
        pairs = [part[2] for part in parts[c]]
        if c + 1 < CHUNKS:
            pairs = after(pairs, far[c + 1])
        landed.append([swap(pair, "hidden", way[0]) for pair, way in zip(pairs, WAYS)])
        both.append([(part[1].astype(F32) + pair[1].astype(F32)).astype(BF16) for part, pair in zip(parts[c], landed[c])])
    grads, returned = [], []
    for c in range(CHUNKS):
        made_of = [rows for save in saved[len(WAYS) * c : len(WAYS) * (c + 1)] for rows in save]
        made_of = after(made_of, saved[-1])
        grads = weight_grads(c, made_of, weight_in, weight_out, grads)
        kept = after([part[0] for part in parts[c]], grads)
        ready = after(both[c], *returned[-1:])
        passed.append([swap(rows, "hidden", way[1]) for rows, way in zip(ready, WAYS)])
        totals = sum_rows([rows for three in zip(kept, landed[c], passed[c]) for rows in three])
        returned.append(totals)
    last = returned[-1]
    returned = [along_z(totals) for totals in returned]
    returned = [rows for direct in returned for rows in (*direct, between_cores(direct, last))]
    layer_out, grad_tokens = combine(place, gate, returned, features, exp_dev, capacity)
    return layer_out.T, grad_tokens.T, grads[0], grads[1]


def solution(mesh):
    in_specs = (
        P("expert", "hidden"),
        P("expert", None),
        P("expert", None),
        P("expert", None, "hidden"),
        P("expert", "hidden", None),
        P("expert", "hidden"),
    )
    out_specs = (
        P("expert", "hidden"),
        P("expert", "hidden"),
        P("expert", None, "hidden"),
        P("expert", "hidden", None),
    )

    def whole(*args):
        wide = 2 * args[0].shape[1] // mesh.shape["hidden"]
        capacity = 2 * args[0].shape[0] // args[3].shape[0]
        four = mesh.shape["hidden"] == 4 and args[3].shape[0] == 4 * mesh.shape["expert"]
        fits = four and mesh.shape["expert"] in (2, 4, 8, 16) and wide % 128 == 0 and capacity % 16 == 0
        body = local if fits else general
        return jax.shard_map(body, mesh=mesh, in_specs=in_specs, out_specs=out_specs, check_vma=False)(*args)

    return whole
```

```python
import functools
import jax
import jax.numpy as jnp
from jax import lax
from jax.experimental import pallas as pl
from jax.experimental.pallas import tpu as pltpu
from jax.sharding import PartitionSpec as P

CHUNKS = 2
BF16 = jnp.bfloat16
F32 = jnp.float32


def gelu_tanh(values):
    return jax.nn.gelu(values, approximate=True)


def local_places(routes, experts, capacity):
    chosen = routes[:, 0]
    matches = (chosen[:, None] == jnp.arange(experts, dtype=jnp.int32)[None, :]).astype(jnp.int32)
    before = jnp.cumsum(matches, axis=0) - matches
    return chosen * capacity + jnp.sum(before * matches, axis=1)


def general(tokens, routes, gate_value, weight_in, weight_out, cotangent):
    owners = lax.axis_size("expert")
    blocks = lax.axis_size("hidden")
    exp_dev = weight_in.shape[0]
    experts = owners * exp_dev
    capacity = max(2, 2 * tokens.shape[0] // experts)
    slot_count = experts * capacity
    features = tokens.shape[1]
    full_width = weight_out.shape[2]
    units = weight_in.shape[2]
    line = exp_dev * capacity * features
    placed = local_places(routes, experts, capacity)
    scaled = (gate_value * cotangent.astype(F32)).astype(BF16)
    first_four = weight_in.reshape(exp_dev, blocks, features, units)
    second_four = weight_out.reshape(exp_dev, units, blocks, features)

    def to_slots(values):
        filled = jnp.zeros((slot_count, features), BF16).at[placed].set(values)
        return filled.reshape(owners, line)

    def rows_of(values):
        arrived = lax.all_to_all(to_slots(values), "expert", split_axis=0, concat_axis=0, tiled=True)
        gathered = lax.all_gather(arrived[None], "hidden", axis=0, tiled=True)
        return gathered.reshape(blocks, owners, exp_dev, capacity, features)

    def back(part):
        flat = part.reshape(blocks, owners, line).astype(BF16)
        total = lax.psum_scatter(flat, "hidden", scatter_dimension=0, tiled=True)
        total = total.astype(F32)[0].astype(BF16)
        returned = lax.all_to_all(total, "expert", split_axis=0, concat_axis=0, tiled=True)
        return returned.reshape(slot_count, features)[placed]

    rows_x = rows_of(tokens)
    rows_g = rows_of(scaled)
    preact = jnp.einsum("nsecf,enfh->sech", rows_x, first_four, preferred_element_type=F32)
    activation, pullback = jax.vjp(gelu_tanh, preact)
    hidden_act = activation.astype(BF16)
    out_part = jnp.einsum("sech,ehnf->nsecf", hidden_act, second_four, preferred_element_type=F32)
    grad_hidden = jnp.einsum("nsecf,ehnf->sech", rows_g, second_four, preferred_element_type=F32)
    grad_pre = pullback(grad_hidden)[0].astype(BF16)
    grad_part = jnp.einsum("sech,enfh->nsecf", grad_pre, first_four, preferred_element_type=F32)
    grad_weight_in = jnp.einsum("nsecf,sech->enfh", rows_x, grad_pre, preferred_element_type=F32)
    grad_weight_out = jnp.einsum("sech,nsecf->ehnf", hidden_act, rows_g, preferred_element_type=F32)
    layer_out = (gate_value * back(out_part).astype(F32)).astype(BF16)
    return (
        layer_out,
        back(grad_part),
        grad_weight_in.astype(BF16).reshape(exp_dev, full_width, units),
        grad_weight_out.astype(BF16).reshape(exp_dev, units, full_width),
    )


NT = (((1,), (1,)), ((), ()))
TN = (((0,), (0,)), ((), ()))
VMEM = pl.BlockSpec(memory_space=pltpu.VMEM)
HBM = pl.BlockSpec(memory_space=pltpu.HBM)
WAYS = ((1, 2), (2, 1))
UNITS = ((2, 1), (1, 2))
OFFSETS = ((0, 1), (2, 3))


def one_hot(place, first, count):
    rows = lax.broadcasted_iota(jnp.int32, (count, place.shape[1]), 0)
    return jnp.where(rows == place - first, 1.0, 0.0).astype(BF16)


def dispatch_kernel(exp_dev, capacity, *refs):
    ins, place_ref, gate_ref, rest = refs[:4], refs[4], refs[5], refs[6:]
    buffers, (routes_buf, tok_buf, cot_buf, sems) = rest[:-4], rest[-4:]
    loads = [
        pltpu.make_async_copy(source, target, sems.at[i])
        for i, (source, target) in enumerate(zip(ins, (routes_buf, gate_ref, tok_buf, cot_buf)))
    ]
    for load in loads:
        load.start()
    tokens = routes_buf.shape[1]
    experts = 2 * len(buffers) * exp_dev
    line = exp_dev * capacity
    me = lax.axis_index("expert")
    earlier = lax.broadcasted_iota(jnp.int32, (tokens, tokens), 0) < lax.broadcasted_iota(
        jnp.int32, (tokens, tokens), 1
    )
    earlier = jnp.where(earlier, 1.0, 0.0).astype(BF16)
    loads[0].wait()
    chosen = routes_buf[...]
    matches = lax.broadcasted_iota(jnp.int32, (experts, tokens), 0) == chosen
    before = jnp.dot(jnp.where(matches, 1.0, 0.0).astype(BF16), earlier, preferred_element_type=F32)
    within = jnp.sum(jnp.where(matches, before, 0.0), axis=0, keepdims=True).astype(jnp.int32)
    place = chosen * capacity + within
    place_ref[...] = place
    for load in loads[1:]:
        load.wait()
    scaled = (gate_ref[...] * cot_buf[...].astype(F32)).astype(BF16)
    both = jnp.concatenate([tok_buf[...], scaled], axis=0)
    for dz, ref in enumerate(buffers):
        firsts = [(me ^ offset) * line for offset in (2 * dz, 2 * dz + 1)]
        hot = jnp.concatenate([one_hot(place, first, line) for first in firsts], axis=0)
        filled = lax.dot_general(hot, both, NT, preferred_element_type=F32).astype(BF16)
        ref[...] = filled.reshape(ref.shape)


def in_hbm(*arrays):
    return [pltpu.with_memory_space_constraint(array, pltpu.HBM) for array in arrays]


def dispatch(routes, gate, tokens, cotangent, owners, exp_dev, capacity):
    features, count = tokens.shape
    buffer = jax.ShapeDtypeStruct((2, exp_dev, capacity, 2 * features), BF16)
    buffers = owners // 2
    place, gate, *buffers = pl.pallas_call(
        functools.partial(dispatch_kernel, exp_dev, capacity),
        out_shape=[jax.ShapeDtypeStruct((1, count), jnp.int32), jax.ShapeDtypeStruct((1, count), F32)]
        + [buffer] * buffers,
        in_specs=[HBM] * 4,
        out_specs=[VMEM] * (2 + buffers),
        scratch_shapes=[pltpu.VMEM((1, count), jnp.int32)]
        + [pltpu.VMEM((features, count), BF16)] * 2
        + [pltpu.SemaphoreType.DMA((4,))],
        compiler_params=pltpu.CompilerParams(vmem_limit_bytes=24 << 20),
        name="dispatch",
    )(*in_hbm(routes, gate, tokens, cotangent))
    return place, gate, buffers


def source_of(dz, other_core):
    return 4 * (dz // 2) + 2 * other_core + dz % 2


def pack_kernel(*refs):
    per = refs[0].shape[1]
    direct, passed, outs = refs[: -per - 1], refs[-per - 1], refs[-per:]
    for p, out in enumerate(outs):
        for dz, ref in enumerate(direct):
            out[source_of(dz, 0)] = ref[0, p]
            out[source_of(dz, 1)] = passed[dz, p]


def pack(direct, passed):
    _, per, capacity, wide = direct[0].shape
    return pl.pallas_call(
        pack_kernel,
        out_shape=[jax.ShapeDtypeStruct((2 * len(direct), capacity, wide), BF16)] * per,
        in_specs=[VMEM] * (1 + len(direct)),
        out_specs=[VMEM] * per,
        compiler_params=pltpu.CompilerParams(vmem_limit_bytes=8 << 20),
        name="pack",
    )(*direct, passed)


def load_kernel(*refs):
    count = (len(refs) - 1) // 2
    sems = refs[-1]
    loads = [pltpu.make_async_copy(refs[i], refs[count + i], sems.at[i]) for i in range(count)]
    for load in loads:
        load.start()
    for load in loads:
        load.wait()


def load(*arrays):
    return pl.pallas_call(
        load_kernel,
        out_shape=[jax.ShapeDtypeStruct(array.shape, array.dtype) for array in arrays],
        in_specs=[HBM] * len(arrays),
        out_specs=[VMEM] * len(arrays),
        scratch_shapes=[pltpu.SemaphoreType.DMA((len(arrays),))],
        compiler_params=pltpu.CompilerParams(vmem_limit_bytes=16 << 20),
        name="load",
    )(*in_hbm(*arrays))


def expert_kernel(first_expert, features, *refs):
    per = len(WAYS)
    ins, (first_ref, second_ref), refs = refs[: 3 * per], refs[3 * per : 3 * per + 2], refs[3 * per + 2 :]
    outs, saved, scratch = refs[: 3 * len(UNITS)], refs[3 * len(UNITS) : -2 * per], refs[-2 * per :]
    mine = lax.axis_index("hidden")
    rows = scratch[0].shape[1]
    for p, (near, far) in enumerate(WAYS):
        s_in, s_out = scratch[2 * p : 2 * p + 2]
        own_ref, near_ref, far_ref = ins[3 * p : 3 * p + 3]
        s_in[mine] = own_ref[...].reshape(rows, 2 * features)
        s_in[mine ^ near] = near_ref[...].reshape(rows, 2 * features)
        s_in[mine ^ far] = far_ref[0].reshape(rows, 2 * features)
        s_in[mine ^ 3] = far_ref[1].reshape(rows, 2 * features)
        x = jnp.concatenate([s_in[j, :, :features] for j in range(4)], axis=1)
        g = jnp.concatenate([s_in[j, :, features:] for j in range(4)], axis=1)
        first, second = first_ref[first_expert + p], second_ref[first_expert + p]
        v = jnp.dot(x, first, preferred_element_type=F32)
        grad_hidden = lax.dot_general(g, second, NT, preferred_element_type=F32)
        root = 0.7978845608028654
        square = v * v
        t = jnp.tanh(root * (v + 0.044715 * (v * square)))
        act = (0.5 * v * (1.0 + t)).astype(BF16)
        slope = 0.5 * (1.0 + t) + 0.5 * v * (1.0 - t * t) * (root * (1.0 + 3 * 0.044715 * square))
        grad_pre = (grad_hidden * slope).astype(BF16)
        out = jnp.dot(act, second, preferred_element_type=F32).astype(BF16)
        grad = lax.dot_general(grad_pre, first, NT, preferred_element_type=F32).astype(BF16)
        for j in range(4):
            lanes = slice(j * features, (j + 1) * features)
            s_out[mine ^ j] = jnp.concatenate([out[:, lanes], grad[:, lanes]], axis=1)
        for group, (near, far) in enumerate(UNITS):
            own_ref, far_ref, near_ref = outs[3 * group : 3 * group + 3]
            span = slice(group * rows // len(UNITS), (group + 1) * rows // len(UNITS))
            own_ref[p] = s_out[0, span].reshape(own_ref.shape[1:])
            far_ref[p] = s_out[far, span].reshape(own_ref.shape[1:])
            near_ref[0, p] = s_out[near, span].reshape(own_ref.shape[1:])
            near_ref[1, p] = s_out[3, span].reshape(own_ref.shape[1:])
        for ref, value in zip(saved[4 * p : 4 * p + 4], (x, g, act, grad_pre)):
            ref[...] = value


def run_experts(first_expert, pieces, first, second):
    sources, capacity, wide = pieces[0].shape
    _, width, units = first.shape
    rows = sources * capacity
    per = len(WAYS)
    part = (per, sources // len(UNITS), capacity, wide)
    results = pl.pallas_call(
        functools.partial(expert_kernel, first_expert, wide // 2),
        out_shape=[jax.ShapeDtypeStruct(shape, BF16) for shape in (part, part, (2, *part))] * len(UNITS)
        + [jax.ShapeDtypeStruct((rows, n), BF16) for n in (width, width, units, units)] * per,
        in_specs=[VMEM] * (len(pieces) + 2),
        out_specs=[VMEM] * (3 * len(UNITS) + 4 * per),
        scratch_shapes=[pltpu.VMEM((4, rows, wide), BF16)] * (2 * per),
        compiler_params=pltpu.CompilerParams(vmem_limit_bytes=16 << 20),
        cost_estimate=pl.CostEstimate(
            flops=8 * per * rows * width * units,
            bytes_accessed=4 * per * width * units,
            transcendentals=per * rows * units,
        ),
        name="experts",
    )(*pieces, first, second)
    parts = [results[3 * group : 3 * group + 3] for group in range(len(UNITS))]
    return parts, results[3 * len(UNITS) :]


def weight_kernel(first_expert, per, *refs):
    saved, rest = refs[: 4 * per], refs[-6:]
    grad_first_hbm, grad_second_hbm, first_buf, second_buf, sems = rest[-5:]
    stores = []
    for p in range(per):
        x, g, act, grad_pre = (ref[...] for ref in saved[4 * p : 4 * p + 4])
        first_buf[p] = lax.dot_general(x, grad_pre, TN, preferred_element_type=F32).astype(BF16)
        stores.append(pltpu.make_async_copy(first_buf.at[p], grad_first_hbm.at[first_expert + p], sems.at[p, 0]))
        stores[-1].start()
        second_buf[p] = lax.dot_general(act, g, TN, preferred_element_type=F32).astype(BF16)
        stores.append(pltpu.make_async_copy(second_buf.at[p], grad_second_hbm.at[first_expert + p], sems.at[p, 1]))
        stores[-1].start()
    for store in stores:
        store.wait()


def weight_grads(chunk, saved, weight_in, weight_out, grads):
    per = len(saved) // 4
    rows, width = saved[0].shape
    units = weight_in.shape[2]
    count = 4 * per
    return pl.pallas_call(
        functools.partial(weight_kernel, chunk * per, per),
        out_shape=[jax.ShapeDtypeStruct(array.shape, BF16) for array in (weight_in, weight_out)],
        in_specs=[VMEM] * count + [HBM] * len(grads),
        out_specs=[HBM] * 2,
        scratch_shapes=[pltpu.VMEM((per, width, units), BF16), pltpu.VMEM((per, units, width), BF16)]
        + [pltpu.SemaphoreType.DMA((per, 2))],
        input_output_aliases={count: 0, count + 1: 1} if grads else {},
        compiler_params=pltpu.CompilerParams(vmem_limit_bytes=20 << 20),
        cost_estimate=pl.CostEstimate(
            flops=4 * per * rows * width * units, bytes_accessed=4 * per * width * units, transcendentals=0
        ),
        name="weight_grads",
    )(*saved, *grads)


def sum_kernel(*refs):
    halves = (len(refs) - 2) // 3
    terms, outs = refs[: 3 * halves], refs[3 * halves :]
    for half in range(halves):
        own, side, passed = terms[3 * half : 3 * half + 3]
        total = own[...].astype(F32) + side[0].astype(F32) + passed[...].astype(F32)
        total = total.astype(BF16)
        for p in range(total.shape[0]):
            for dz, out in enumerate(outs):
                out[0, half * total.shape[0] + p] = total[p, source_of(dz, 0)]
                out[1, half * total.shape[0] + p] = total[p, source_of(dz, 1)]


def sum_rows(terms):
    per, _, capacity, wide = terms[0].shape
    return pl.pallas_call(
        sum_kernel,
        out_shape=[jax.ShapeDtypeStruct((2, len(terms) // 3 * per, capacity, wide), BF16)] * 2,
        in_specs=[VMEM] * len(terms),
        out_specs=[VMEM] * 2,
        compiler_params=pltpu.CompilerParams(vmem_limit_bytes=8 << 20),
        name="sum_rows",
    )(*terms)


def combine_kernel(capacity, exp_dev, picks, place_ref, gate_ref, *refs):
    ins, (out_ref, grad_ref) = refs[:-2], refs[-2:]
    me = lax.axis_index("expert")
    wide = ins[0].shape[-1]
    place = place_ref[...]
    rows, hot = [], []
    for array, index, offset, first_expert in picks:
        rows.append(ins[array][index].reshape(-1, wide))
        first = (me ^ offset) * (exp_dev * capacity) + first_expert * capacity
        hot.append(one_hot(place, first, rows[-1].shape[0]))
    total = lax.dot_general(jnp.concatenate(rows, axis=0), jnp.concatenate(hot, axis=0), TN, preferred_element_type=F32)
    features = out_ref.shape[0]
    out_ref[...] = (gate_ref[...] * total[:features]).astype(BF16)
    grad_ref[...] = total[features:].astype(BF16)


def combine(place, gate, returned, picks, features, exp_dev, capacity):
    count = place.shape[1]
    return pl.pallas_call(
        functools.partial(combine_kernel, capacity, exp_dev, picks),
        out_shape=[jax.ShapeDtypeStruct((features, count), BF16)] * 2,
        in_specs=[VMEM] * (2 + len(returned)),
        out_specs=[VMEM] * 2,
        compiler_params=pltpu.CompilerParams(vmem_limit_bytes=24 << 20),
        name="combine",
    )(place, gate, *returned)


def swap(value, axis, bits):
    size = lax.axis_size(axis)
    return lax.ppermute(value, axis, [(i, i ^ bits) for i in range(size)])


def along_z(buffers):
    direct = [buffers[0]] + [None] * (len(buffers) - 1)
    for dz in reversed(range(1, len(buffers))):
        direct[dz] = swap(buffers[dz], "expert", 2 * dz)
    return direct


def between_cores(direct, *earlier):
    return swap(jnp.stack([rows[1] for rows in after(direct, *earlier)]), "expert", 1)


def after(values, *earlier):
    return lax.optimization_barrier((values, earlier))[0]


def local(tokens, routes, gate_value, weight_in, weight_out, cotangent):
    owners = lax.axis_size("expert")
    exp_dev = weight_in.shape[0]
    count, features = tokens.shape
    capacity = 2 * count // (owners * exp_dev)
    place, gate, buffers = dispatch(
        routes.reshape(1, count), gate_value.reshape(1, count), tokens.T, cotangent.T, owners, exp_dev, capacity
    )
    first, second = load(weight_in, weight_out)
    direct = along_z(buffers)
    rows = pack(direct, between_cores(direct, first, second))
    per = exp_dev // CHUNKS
    own, near, far = [rows[per * c : per * (c + 1)] for c in range(CHUNKS)], [], []
    for c in range(CHUNKS):
        near.append([swap(rows, "hidden", way[0]) for rows, way in zip(own[c], WAYS)])
    for c in range(CHUNKS):
        pairs = [jnp.stack(pair) for pair in zip(own[c], near[c])]
        far.append([swap(pair, "hidden", way[1]) for pair, way in zip(pairs, WAYS)])
    parts, saved = [], []
    for c in range(CHUNKS):
        pieces = [piece for three in zip(own[c], near[c], far[c]) for piece in three]
        part, save = run_experts(per * c, pieces, first, second)
        parts.append(part)
        saved.append(save)

    def step_back(c, group):
        mine, other, pair = parts[c][group]
        landed = swap(pair, "hidden", UNITS[group][0])
        return [mine, landed, (other.astype(F32) + landed[1].astype(F32)).astype(BF16)]

    far_terms = [step_back(c, 1) for c in range(CHUNKS)]
    near_terms = [step_back(c, 0) for c in range(CHUNKS)]
    def finish(terms, group):
        passed = [swap(both, "hidden", UNITS[group][1]) for _, _, both in terms]
        totals = sum_rows([rows for (mine, landed, _), last in zip(terms, passed) for rows in (mine, landed, last)])
        return [swap(rows, "expert", 2 * dz) if dz else rows for dz, rows in zip(OFFSETS[group], totals)], totals

    grads = weight_grads(0, after(saved[0], saved[1]), weight_in, weight_out, [])
    near_terms[0][0] = after(near_terms[0][0], grads)
    homeward = [(1, per * c, *finish(far_terms[c : c + 1], 1)) for c in range(CHUNKS)]
    homeward.append((0, 0, *finish(near_terms, 0)))
    grads = weight_grads(1, after(saved[1], homeward[-1][-1]), weight_in, weight_out, grads)
    returned, picks = [], []
    for i, (group, first_expert, direct, _) in enumerate(homeward):
        for j, dz in enumerate(OFFSETS[group]):
            picks.append((len(returned) + j, (0,), 2 * dz, first_expert))
            picks.append((len(returned) + 2, (j,), 2 * dz + 1, first_expert))
        returned.extend([*direct, between_cores(direct, *(grads if i else []))])
    layer_out, grad_tokens = combine(place, gate, returned, picks, features, exp_dev, capacity)
    return layer_out.T, grad_tokens.T, grads[0], grads[1]


def solution(mesh):
    in_specs = (
        P("expert", "hidden"),
        P("expert", None),
        P("expert", None),
        P("expert", None, "hidden"),
        P("expert", "hidden", None),
        P("expert", "hidden"),
    )
    out_specs = (
        P("expert", "hidden"),
        P("expert", "hidden"),
        P("expert", None, "hidden"),
        P("expert", "hidden", None),
    )

    def whole(*args):
        wide = 2 * args[0].shape[1] // mesh.shape["hidden"]
        capacity = 2 * args[0].shape[0] // args[3].shape[0]
        four = mesh.shape["hidden"] == 4 and args[3].shape[0] == 4 * mesh.shape["expert"]
        fits = four and mesh.shape["expert"] == 8 and wide % 128 == 0 and capacity % 16 == 0
        body = local if fits else general
        return jax.shard_map(body, mesh=mesh, in_specs=in_specs, out_specs=out_specs, check_vma=False)(*args)

    return whole
```

```python
import functools
import jax
import jax.numpy as jnp
from jax import lax
from jax.experimental import pallas as pl
from jax.experimental.pallas import tpu as pltpu
from jax.sharding import PartitionSpec as P

CHUNKS = 2
BF16 = jnp.bfloat16
F32 = jnp.float32


def gelu_tanh(values):
    return jax.nn.gelu(values, approximate=True)


def local_places(routes, experts, capacity):
    chosen = routes[:, 0]
    matches = (chosen[:, None] == jnp.arange(experts, dtype=jnp.int32)[None, :]).astype(jnp.int32)
    before = jnp.cumsum(matches, axis=0) - matches
    return chosen * capacity + jnp.sum(before * matches, axis=1)


def general(tokens, routes, gate_value, weight_in, weight_out, cotangent):
    owners = lax.axis_size("expert")
    blocks = lax.axis_size("hidden")
    exp_dev = weight_in.shape[0]
    experts = owners * exp_dev
    capacity = max(2, 2 * tokens.shape[0] // experts)
    slot_count = experts * capacity
    features = tokens.shape[1]
    full_width = weight_out.shape[2]
    units = weight_in.shape[2]
    line = exp_dev * capacity * features
    placed = local_places(routes, experts, capacity)
    scaled = (gate_value * cotangent.astype(F32)).astype(BF16)
    first_four = weight_in.reshape(exp_dev, blocks, features, units)
    second_four = weight_out.reshape(exp_dev, units, blocks, features)

    def to_slots(values):
        filled = jnp.zeros((slot_count, features), BF16).at[placed].set(values)
        return filled.reshape(owners, line)

    def rows_of(values):
        arrived = lax.all_to_all(to_slots(values), "expert", split_axis=0, concat_axis=0, tiled=True)
        gathered = lax.all_gather(arrived[None], "hidden", axis=0, tiled=True)
        return gathered.reshape(blocks, owners, exp_dev, capacity, features)

    def back(part):
        flat = part.reshape(blocks, owners, line).astype(BF16)
        total = lax.psum_scatter(flat, "hidden", scatter_dimension=0, tiled=True)
        total = total.astype(F32)[0].astype(BF16)
        returned = lax.all_to_all(total, "expert", split_axis=0, concat_axis=0, tiled=True)
        return returned.reshape(slot_count, features)[placed]

    rows_x = rows_of(tokens)
    rows_g = rows_of(scaled)
    preact = jnp.einsum("nsecf,enfh->sech", rows_x, first_four, preferred_element_type=F32)
    activation, pullback = jax.vjp(gelu_tanh, preact)
    hidden_act = activation.astype(BF16)
    out_part = jnp.einsum("sech,ehnf->nsecf", hidden_act, second_four, preferred_element_type=F32)
    grad_hidden = jnp.einsum("nsecf,ehnf->sech", rows_g, second_four, preferred_element_type=F32)
    grad_pre = pullback(grad_hidden)[0].astype(BF16)
    grad_part = jnp.einsum("sech,enfh->nsecf", grad_pre, first_four, preferred_element_type=F32)
    grad_weight_in = jnp.einsum("nsecf,sech->enfh", rows_x, grad_pre, preferred_element_type=F32)
    grad_weight_out = jnp.einsum("sech,nsecf->ehnf", hidden_act, rows_g, preferred_element_type=F32)
    layer_out = (gate_value * back(out_part).astype(F32)).astype(BF16)
    return (
        layer_out,
        back(grad_part),
        grad_weight_in.astype(BF16).reshape(exp_dev, full_width, units),
        grad_weight_out.astype(BF16).reshape(exp_dev, units, full_width),
    )


NT = (((1,), (1,)), ((), ()))
TN = (((0,), (0,)), ((), ()))
VMEM = pl.BlockSpec(memory_space=pltpu.VMEM)
HBM = pl.BlockSpec(memory_space=pltpu.HBM)
WAYS = ((1, 2), (2, 1))
UNITS = ((2, 1), (1, 2))
OFFSETS = ((0, 1), (2, 3))


def one_hot(place, first, count):
    rows = lax.broadcasted_iota(jnp.int32, (count, place.shape[1]), 0)
    return jnp.where(rows == place - first, 1.0, 0.0).astype(BF16)


def dispatch_kernel(exp_dev, capacity, *refs):
    ins, place_ref, gate_ref, rest = refs[:4], refs[4], refs[5], refs[6:]
    buffers, (routes_buf, tok_buf, cot_buf, sems) = rest[:-4], rest[-4:]
    loads = [
        pltpu.make_async_copy(source, target, sems.at[i])
        for i, (source, target) in enumerate(zip(ins, (routes_buf, gate_ref, tok_buf, cot_buf)))
    ]
    for load in loads:
        load.start()
    tokens = routes_buf.shape[1]
    experts = 2 * len(buffers) * exp_dev
    line = exp_dev * capacity
    me = lax.axis_index("expert")
    earlier = lax.broadcasted_iota(jnp.int32, (tokens, tokens), 0) < lax.broadcasted_iota(
        jnp.int32, (tokens, tokens), 1
    )
    earlier = jnp.where(earlier, 1.0, 0.0).astype(BF16)
    loads[0].wait()
    chosen = routes_buf[...]
    matches = lax.broadcasted_iota(jnp.int32, (experts, tokens), 0) == chosen
    before = jnp.dot(jnp.where(matches, 1.0, 0.0).astype(BF16), earlier, preferred_element_type=F32)
    within = jnp.sum(jnp.where(matches, before, 0.0), axis=0, keepdims=True).astype(jnp.int32)
    place = chosen * capacity + within
    place_ref[...] = place
    for load in loads[1:]:
        load.wait()
    scaled = (gate_ref[...] * cot_buf[...].astype(F32)).astype(BF16)
    both = jnp.concatenate([tok_buf[...], scaled], axis=0)
    for dz, ref in enumerate(buffers):
        firsts = [(me ^ offset) * line for offset in (2 * dz, 2 * dz + 1)]
        hot = jnp.concatenate([one_hot(place, first, line) for first in firsts], axis=0)
        filled = lax.dot_general(hot, both, NT, preferred_element_type=F32).astype(BF16)
        ref[...] = filled.reshape(ref.shape)


def in_hbm(*arrays):
    return [pltpu.with_memory_space_constraint(array, pltpu.HBM) for array in arrays]


def dispatch(routes, gate, tokens, cotangent, owners, exp_dev, capacity):
    features, count = tokens.shape
    buffer = jax.ShapeDtypeStruct((2, exp_dev, capacity, 2 * features), BF16)
    buffers = owners // 2
    place, gate, *buffers = pl.pallas_call(
        functools.partial(dispatch_kernel, exp_dev, capacity),
        out_shape=[jax.ShapeDtypeStruct((1, count), jnp.int32), jax.ShapeDtypeStruct((1, count), F32)]
        + [buffer] * buffers,
        in_specs=[HBM] * 4,
        out_specs=[VMEM] * (2 + buffers),
        scratch_shapes=[pltpu.VMEM((1, count), jnp.int32)]
        + [pltpu.VMEM((features, count), BF16)] * 2
        + [pltpu.SemaphoreType.DMA((4,))],
        compiler_params=pltpu.CompilerParams(vmem_limit_bytes=24 << 20),
        name="dispatch",
    )(*in_hbm(routes, gate, tokens, cotangent))
    return place, gate, buffers


def source_of(dz, other_core):
    return 4 * (dz // 2) + 2 * other_core + dz % 2


def pack_kernel(*refs):
    per = refs[0].shape[1]
    direct, passed, outs = refs[: -per - 1], refs[-per - 1], refs[-per:]
    for p, out in enumerate(outs):
        for dz, ref in enumerate(direct):
            out[source_of(dz, 0)] = ref[0, p]
            out[source_of(dz, 1)] = passed[dz, p]


def pack(direct, passed):
    _, per, capacity, wide = direct[0].shape
    return pl.pallas_call(
        pack_kernel,
        out_shape=[jax.ShapeDtypeStruct((2 * len(direct), capacity, wide), BF16)] * per,
        in_specs=[VMEM] * (1 + len(direct)),
        out_specs=[VMEM] * per,
        compiler_params=pltpu.CompilerParams(vmem_limit_bytes=8 << 20),
        name="pack",
    )(*direct, passed)


def load_kernel(*refs):
    count = (len(refs) - 1) // 2
    sems = refs[-1]
    loads = [pltpu.make_async_copy(refs[i], refs[count + i], sems.at[i]) for i in range(count)]
    for load in loads:
        load.start()
    for load in loads:
        load.wait()


def load(*arrays):
    return pl.pallas_call(
        load_kernel,
        out_shape=[jax.ShapeDtypeStruct(array.shape, array.dtype) for array in arrays],
        in_specs=[HBM] * len(arrays),
        out_specs=[VMEM] * len(arrays),
        scratch_shapes=[pltpu.SemaphoreType.DMA((len(arrays),))],
        compiler_params=pltpu.CompilerParams(vmem_limit_bytes=16 << 20),
        name="load",
    )(*in_hbm(*arrays))


def expert_kernel(first_expert, features, *refs):
    per = len(WAYS)
    ins, (first_ref, second_ref), refs = refs[: 3 * per], refs[3 * per : 3 * per + 2], refs[3 * per + 2 :]
    outs, saved, scratch = refs[: 3 * len(UNITS)], refs[3 * len(UNITS) : -2 * per], refs[-2 * per :]
    mine = lax.axis_index("hidden")
    rows = scratch[0].shape[1]
    for p, (near, far) in enumerate(WAYS):
        s_in, s_out = scratch[2 * p : 2 * p + 2]
        own_ref, near_ref, far_ref = ins[3 * p : 3 * p + 3]
        s_in[mine] = own_ref[...].reshape(rows, 2 * features)
        s_in[mine ^ near] = near_ref[...].reshape(rows, 2 * features)
        s_in[mine ^ far] = far_ref[0].reshape(rows, 2 * features)
        s_in[mine ^ 3] = far_ref[1].reshape(rows, 2 * features)
        x = jnp.concatenate([s_in[j, :, :features] for j in range(4)], axis=1)
        g = jnp.concatenate([s_in[j, :, features:] for j in range(4)], axis=1)
        first, second = first_ref[first_expert + p], second_ref[first_expert + p]
        v = jnp.dot(x, first, preferred_element_type=F32)
        grad_hidden = lax.dot_general(g, second, NT, preferred_element_type=F32)
        root = 0.7978845608028654
        square = v * v
        t = jnp.tanh(root * (v + 0.044715 * (v * square)))
        act = (0.5 * v * (1.0 + t)).astype(BF16)
        slope = 0.5 * (1.0 + t) + 0.5 * v * (1.0 - t * t) * (root * (1.0 + 3 * 0.044715 * square))
        grad_pre = (grad_hidden * slope).astype(BF16)
        out = jnp.dot(act, second, preferred_element_type=F32).astype(BF16)
        grad = lax.dot_general(grad_pre, first, NT, preferred_element_type=F32).astype(BF16)
        for j in range(4):
            lanes = slice(j * features, (j + 1) * features)
            s_out[mine ^ j] = jnp.concatenate([out[:, lanes], grad[:, lanes]], axis=1)
        for group, (near, far) in enumerate(UNITS):
            own_ref, far_ref, near_ref = outs[3 * group : 3 * group + 3]
            span = slice(group * rows // len(UNITS), (group + 1) * rows // len(UNITS))
            own_ref[p] = s_out[0, span].reshape(own_ref.shape[1:])
            far_ref[p] = s_out[far, span].reshape(own_ref.shape[1:])
            near_ref[0, p] = s_out[near, span].reshape(own_ref.shape[1:])
            near_ref[1, p] = s_out[3, span].reshape(own_ref.shape[1:])
        for ref, value in zip(saved[4 * p : 4 * p + 4], (x, g, act, grad_pre)):
            ref[...] = value


def run_experts(first_expert, pieces, first, second):
    sources, capacity, wide = pieces[0].shape
    _, width, units = first.shape
    rows = sources * capacity
    per = len(WAYS)
    part = (per, sources // len(UNITS), capacity, wide)
    results = pl.pallas_call(
        functools.partial(expert_kernel, first_expert, wide // 2),
        out_shape=[jax.ShapeDtypeStruct(shape, BF16) for shape in (part, part, (2, *part))] * len(UNITS)
        + [jax.ShapeDtypeStruct((rows, n), BF16) for n in (width, width, units, units)] * per,
        in_specs=[VMEM] * (len(pieces) + 2),
        out_specs=[VMEM] * (3 * len(UNITS) + 4 * per),
        scratch_shapes=[pltpu.VMEM((4, rows, wide), BF16)] * (2 * per),
        compiler_params=pltpu.CompilerParams(vmem_limit_bytes=16 << 20),
        cost_estimate=pl.CostEstimate(
            flops=8 * per * rows * width * units,
            bytes_accessed=4 * per * width * units,
            transcendentals=per * rows * units,
        ),
        name="experts",
    )(*pieces, first, second)
    parts = [results[3 * group : 3 * group + 3] for group in range(len(UNITS))]
    return parts, results[3 * len(UNITS) :]


def weight_kernel(first_expert, per, *refs):
    saved, rest = refs[: 4 * per], refs[-6:]
    grad_first_hbm, grad_second_hbm, first_buf, second_buf, sems = rest[-5:]
    stores = []
    for p in range(per):
        x, g, act, grad_pre = (ref[...] for ref in saved[4 * p : 4 * p + 4])
        first_buf[p] = lax.dot_general(x, grad_pre, TN, preferred_element_type=F32).astype(BF16)
        stores.append(pltpu.make_async_copy(first_buf.at[p], grad_first_hbm.at[first_expert + p], sems.at[p, 0]))
        stores[-1].start()
        second_buf[p] = lax.dot_general(act, g, TN, preferred_element_type=F32).astype(BF16)
        stores.append(pltpu.make_async_copy(second_buf.at[p], grad_second_hbm.at[first_expert + p], sems.at[p, 1]))
        stores[-1].start()
    for store in stores:
        store.wait()


def weight_grads(chunk, saved, weight_in, weight_out, grads):
    per = len(saved) // 4
    rows, width = saved[0].shape
    units = weight_in.shape[2]
    count = 4 * per
    return pl.pallas_call(
        functools.partial(weight_kernel, chunk * per, per),
        out_shape=[jax.ShapeDtypeStruct(array.shape, BF16) for array in (weight_in, weight_out)],
        in_specs=[VMEM] * count + [HBM] * len(grads),
        out_specs=[HBM] * 2,
        scratch_shapes=[pltpu.VMEM((per, width, units), BF16), pltpu.VMEM((per, units, width), BF16)]
        + [pltpu.SemaphoreType.DMA((per, 2))],
        input_output_aliases={count: 0, count + 1: 1} if grads else {},
        compiler_params=pltpu.CompilerParams(vmem_limit_bytes=20 << 20),
        cost_estimate=pl.CostEstimate(
            flops=4 * per * rows * width * units, bytes_accessed=4 * per * width * units, transcendentals=0
        ),
        name="weight_grads",
    )(*saved, *grads)


def sum_kernel(*refs):
    halves = (len(refs) - 2) // 3
    terms, outs = refs[: 3 * halves], refs[3 * halves :]
    for half in range(halves):
        own, side, passed = terms[3 * half : 3 * half + 3]
        total = own[...].astype(F32) + side[0].astype(F32) + passed[...].astype(F32)
        total = total.astype(BF16)
        for p in range(total.shape[0]):
            for dz, out in enumerate(outs):
                out[0, half * total.shape[0] + p] = total[p, source_of(dz, 0)]
                out[1, half * total.shape[0] + p] = total[p, source_of(dz, 1)]


def sum_rows(terms):
    per, _, capacity, wide = terms[0].shape
    return pl.pallas_call(
        sum_kernel,
        out_shape=[jax.ShapeDtypeStruct((2, len(terms) // 3 * per, capacity, wide), BF16)] * 2,
        in_specs=[VMEM] * len(terms),
        out_specs=[VMEM] * 2,
        compiler_params=pltpu.CompilerParams(vmem_limit_bytes=8 << 20),
        name="sum_rows",
    )(*terms)


def combine_kernel(capacity, exp_dev, picks, place_ref, gate_ref, *refs):
    ins, (out_ref, grad_ref) = refs[:-2], refs[-2:]
    me = lax.axis_index("expert")
    wide = ins[0].shape[-1]
    place = place_ref[...]
    rows, hot = [], []
    for array, index, offset, first_expert in picks:
        rows.append(ins[array][index].reshape(-1, wide))
        first = (me ^ offset) * (exp_dev * capacity) + first_expert * capacity
        hot.append(one_hot(place, first, rows[-1].shape[0]))
    total = lax.dot_general(jnp.concatenate(rows, axis=0), jnp.concatenate(hot, axis=0), TN, preferred_element_type=F32)
    features = out_ref.shape[0]
    out_ref[...] = (gate_ref[...] * total[:features]).astype(BF16)
    grad_ref[...] = total[features:].astype(BF16)


def combine(place, gate, returned, picks, features, exp_dev, capacity):
    count = place.shape[1]
    return pl.pallas_call(
        functools.partial(combine_kernel, capacity, exp_dev, picks),
        out_shape=[jax.ShapeDtypeStruct((features, count), BF16)] * 2,
        in_specs=[VMEM] * (2 + len(returned)),
        out_specs=[VMEM] * 2,
        compiler_params=pltpu.CompilerParams(vmem_limit_bytes=24 << 20),
        name="combine",
    )(place, gate, *returned)


def swap(value, axis, bits):
    size = lax.axis_size(axis)
    return lax.ppermute(value, axis, [(i, i ^ bits) for i in range(size)])


def along_z(buffers):
    direct = [buffers[0]] + [None] * (len(buffers) - 1)
    for dz in reversed(range(1, len(buffers))):
        direct[dz] = swap(buffers[dz], "expert", 2 * dz)
    return direct


def between_cores(direct, *earlier):
    return swap(jnp.stack([rows[1] for rows in after(direct, *earlier)]), "expert", 1)


def after(values, *earlier):
    return lax.optimization_barrier((values, earlier))[0]


def local(tokens, routes, gate_value, weight_in, weight_out, cotangent):
    owners = lax.axis_size("expert")
    exp_dev = weight_in.shape[0]
    count, features = tokens.shape
    capacity = 2 * count // (owners * exp_dev)
    place, gate, buffers = dispatch(
        routes.reshape(1, count), gate_value.reshape(1, count), tokens.T, cotangent.T, owners, exp_dev, capacity
    )
    first, second = load(weight_in, weight_out)
    direct = along_z(buffers)
    rows = pack(direct, between_cores(direct, first, second))
    per = exp_dev // CHUNKS
    own, near, far = [rows[per * c : per * (c + 1)] for c in range(CHUNKS)], [], []
    for c in range(CHUNKS):
        near.append([swap(rows, "hidden", way[0]) for rows, way in zip(own[c], WAYS)])
    for c in range(CHUNKS):
        pairs = list(zip(own[c], near[c]))
        if c + 1 < CHUNKS:
            pairs[1] = after(pairs[1], near[c + 1])
        pairs = [jnp.stack(pair) for pair in pairs]
        far.append([swap(pair, "hidden", way[1]) for pair, way in zip(pairs, WAYS)])
    parts, saved = [], []
    for c in range(CHUNKS):
        pieces = [piece for three in zip(own[c], near[c], far[c]) for piece in three]
        part, save = run_experts(per * c, pieces, first, second)
        parts.append(part)
        saved.append(save)

    def step_back(c, group):
        mine, other, pair = parts[c][group]
        landed = swap(pair, "hidden", UNITS[group][0])
        return [mine, landed, (other.astype(F32) + landed[1].astype(F32)).astype(BF16)]

    far_terms = [step_back(c, 1) for c in range(CHUNKS)]
    near_terms = [step_back(c, 0) for c in range(CHUNKS)]
    def finish(terms, group):
        passed = [swap(both, "hidden", UNITS[group][1]) for _, _, both in terms]
        totals = sum_rows([rows for (mine, landed, _), last in zip(terms, passed) for rows in (mine, landed, last)])
        return [swap(rows, "expert", 2 * dz) if dz else rows for dz, rows in zip(OFFSETS[group], totals)], totals

    grads = weight_grads(0, saved[0], weight_in, weight_out, [])
    near_terms[1][2] = after(near_terms[1][2], grads)
    homeward = []
    for c in range(CHUNKS):
        if c:
            far_terms[c][2] = after(far_terms[c][2], homeward[-1][-1])
        homeward.append((1, per * c, *finish(far_terms[c : c + 1], 1)))
    near_terms[0][0] = after(near_terms[0][0], homeward[-1][-1])
    homeward.append((0, 0, *finish(near_terms, 0)))
    grads = weight_grads(1, after(saved[1], homeward[-1][-1]), weight_in, weight_out, grads)
    returned, picks = [], []
    for group, first_expert, direct, _ in homeward:
        for j, dz in enumerate(OFFSETS[group]):
            picks.append((len(returned) + j, (0,), 2 * dz, first_expert))
            picks.append((len(returned) + 2, (j,), 2 * dz + 1, first_expert))
        returned.extend([*direct, between_cores(direct, *grads)])
    layer_out, grad_tokens = combine(place, gate, returned, picks, features, exp_dev, capacity)
    return layer_out.T, grad_tokens.T, grads[0], grads[1]


def solution(mesh):
    in_specs = (
        P("expert", "hidden"),
        P("expert", None),
        P("expert", None),
        P("expert", None, "hidden"),
        P("expert", "hidden", None),
        P("expert", "hidden"),
    )
    out_specs = (
        P("expert", "hidden"),
        P("expert", "hidden"),
        P("expert", None, "hidden"),
        P("expert", "hidden", None),
    )

    def whole(*args):
        wide = 2 * args[0].shape[1] // mesh.shape["hidden"]
        capacity = 2 * args[0].shape[0] // args[3].shape[0]
        four = mesh.shape["hidden"] == 4 and args[3].shape[0] == 4 * mesh.shape["expert"]
        fits = four and mesh.shape["expert"] == 8 and wide % 128 == 0 and capacity % 16 == 0
        body = local if fits else general
        return jax.shard_map(body, mesh=mesh, in_specs=in_specs, out_specs=out_specs, check_vma=False)(*args)

    return whole
```

```python
import functools
import jax
import jax.numpy as jnp
from jax import lax
from jax.experimental import pallas as pl
from jax.experimental.pallas import tpu as pltpu
from jax.sharding import PartitionSpec as P

CHUNKS = 2
BF16 = jnp.bfloat16
F32 = jnp.float32


def gelu_tanh(values):
    return jax.nn.gelu(values, approximate=True)


def local_places(routes, experts, capacity):
    chosen = routes[:, 0]
    matches = (chosen[:, None] == jnp.arange(experts, dtype=jnp.int32)[None, :]).astype(jnp.int32)
    before = jnp.cumsum(matches, axis=0) - matches
    return chosen * capacity + jnp.sum(before * matches, axis=1)


def general(tokens, routes, gate_value, weight_in, weight_out, cotangent):
    owners = lax.axis_size("expert")
    blocks = lax.axis_size("hidden")
    exp_dev = weight_in.shape[0]
    experts = owners * exp_dev
    capacity = max(2, 2 * tokens.shape[0] // experts)
    slot_count = experts * capacity
    features = tokens.shape[1]
    full_width = weight_out.shape[2]
    units = weight_in.shape[2]
    line = exp_dev * capacity * features
    placed = local_places(routes, experts, capacity)
    scaled = (gate_value * cotangent.astype(F32)).astype(BF16)
    first_four = weight_in.reshape(exp_dev, blocks, features, units)
    second_four = weight_out.reshape(exp_dev, units, blocks, features)

    def to_slots(values):
        filled = jnp.zeros((slot_count, features), BF16).at[placed].set(values)
        return filled.reshape(owners, line)

    def rows_of(values):
        arrived = lax.all_to_all(to_slots(values), "expert", split_axis=0, concat_axis=0, tiled=True)
        gathered = lax.all_gather(arrived[None], "hidden", axis=0, tiled=True)
        return gathered.reshape(blocks, owners, exp_dev, capacity, features)

    def back(part):
        flat = part.reshape(blocks, owners, line).astype(BF16)
        total = lax.psum_scatter(flat, "hidden", scatter_dimension=0, tiled=True)
        total = total.astype(F32)[0].astype(BF16)
        returned = lax.all_to_all(total, "expert", split_axis=0, concat_axis=0, tiled=True)
        return returned.reshape(slot_count, features)[placed]

    rows_x = rows_of(tokens)
    rows_g = rows_of(scaled)
    preact = jnp.einsum("nsecf,enfh->sech", rows_x, first_four, preferred_element_type=F32)
    activation, pullback = jax.vjp(gelu_tanh, preact)
    hidden_act = activation.astype(BF16)
    out_part = jnp.einsum("sech,ehnf->nsecf", hidden_act, second_four, preferred_element_type=F32)
    grad_hidden = jnp.einsum("nsecf,ehnf->sech", rows_g, second_four, preferred_element_type=F32)
    grad_pre = pullback(grad_hidden)[0].astype(BF16)
    grad_part = jnp.einsum("sech,enfh->nsecf", grad_pre, first_four, preferred_element_type=F32)
    grad_weight_in = jnp.einsum("nsecf,sech->enfh", rows_x, grad_pre, preferred_element_type=F32)
    grad_weight_out = jnp.einsum("sech,nsecf->ehnf", hidden_act, rows_g, preferred_element_type=F32)
    layer_out = (gate_value * back(out_part).astype(F32)).astype(BF16)
    return (
        layer_out,
        back(grad_part),
        grad_weight_in.astype(BF16).reshape(exp_dev, full_width, units),
        grad_weight_out.astype(BF16).reshape(exp_dev, units, full_width),
    )


NT = (((1,), (1,)), ((), ()))
TN = (((0,), (0,)), ((), ()))
VMEM = pl.BlockSpec(memory_space=pltpu.VMEM)
HBM = pl.BlockSpec(memory_space=pltpu.HBM)
WAYS = ((1, 2), (2, 1))
UNITS = ((2, 1), (1, 2))
OFFSETS = ((0, 1), (2, 3))


def one_hot(place, first, count):
    rows = lax.broadcasted_iota(jnp.int32, (count, place.shape[1]), 0)
    return jnp.where(rows == place - first, 1.0, 0.0).astype(BF16)


def dispatch_kernel(exp_dev, capacity, *refs):
    ins, place_ref, gate_ref, rest = refs[:4], refs[4], refs[5], refs[6:]
    buffers, (routes_buf, tok_buf, cot_buf, sems) = rest[:-4], rest[-4:]
    loads = [
        pltpu.make_async_copy(source, target, sems.at[i])
        for i, (source, target) in enumerate(zip(ins, (routes_buf, gate_ref, tok_buf, cot_buf)))
    ]
    for load in loads:
        load.start()
    tokens = routes_buf.shape[1]
    experts = 2 * len(buffers) * exp_dev
    line = exp_dev * capacity
    me = lax.axis_index("expert")
    earlier = lax.broadcasted_iota(jnp.int32, (tokens, tokens), 0) < lax.broadcasted_iota(
        jnp.int32, (tokens, tokens), 1
    )
    earlier = jnp.where(earlier, 1.0, 0.0).astype(BF16)
    loads[0].wait()
    chosen = routes_buf[...]
    matches = lax.broadcasted_iota(jnp.int32, (experts, tokens), 0) == chosen
    before = jnp.dot(jnp.where(matches, 1.0, 0.0).astype(BF16), earlier, preferred_element_type=F32)
    within = jnp.sum(jnp.where(matches, before, 0.0), axis=0, keepdims=True).astype(jnp.int32)
    place = chosen * capacity + within
    place_ref[...] = place
    for load in loads[1:]:
        load.wait()
    scaled = (gate_ref[...] * cot_buf[...].astype(F32)).astype(BF16)
    both = jnp.concatenate([tok_buf[...], scaled], axis=0)
    for dz, ref in enumerate(buffers):
        firsts = [(me ^ offset) * line for offset in (2 * dz, 2 * dz + 1)]
        hot = jnp.concatenate([one_hot(place, first, line) for first in firsts], axis=0)
        filled = lax.dot_general(hot, both, NT, preferred_element_type=F32).astype(BF16)
        ref[...] = filled.reshape(ref.shape)


def in_hbm(*arrays):
    return [pltpu.with_memory_space_constraint(array, pltpu.HBM) for array in arrays]


def dispatch(routes, gate, tokens, cotangent, owners, exp_dev, capacity):
    features, count = tokens.shape
    buffer = jax.ShapeDtypeStruct((2, exp_dev, capacity, 2 * features), BF16)
    buffers = owners // 2
    place, gate, *buffers = pl.pallas_call(
        functools.partial(dispatch_kernel, exp_dev, capacity),
        out_shape=[jax.ShapeDtypeStruct((1, count), jnp.int32), jax.ShapeDtypeStruct((1, count), F32)]
        + [buffer] * buffers,
        in_specs=[HBM] * 4,
        out_specs=[VMEM] * (2 + buffers),
        scratch_shapes=[pltpu.VMEM((1, count), jnp.int32)]
        + [pltpu.VMEM((features, count), BF16)] * 2
        + [pltpu.SemaphoreType.DMA((4,))],
        compiler_params=pltpu.CompilerParams(vmem_limit_bytes=24 << 20),
        name="dispatch",
    )(*in_hbm(routes, gate, tokens, cotangent))
    return place, gate, buffers


def source_of(dz, other_core):
    return 2 * dz + other_core


def pack_kernel(*refs):
    per = refs[0].shape[1]
    direct, passed, outs = refs[: -per - 1], refs[-per - 1], refs[-per:]
    for p, out in enumerate(outs):
        for i, ref in enumerate(direct):
            out[source_of(i, 0)] = ref[0, p]
            out[source_of(i, 1)] = passed[i, p]


def pack(direct, passed):
    _, per, capacity, wide = direct[0].shape
    return pl.pallas_call(
        pack_kernel,
        out_shape=[jax.ShapeDtypeStruct((2 * len(direct), capacity, wide), BF16)] * per,
        in_specs=[VMEM] * (1 + len(direct)),
        out_specs=[VMEM] * per,
        compiler_params=pltpu.CompilerParams(vmem_limit_bytes=8 << 20),
        name="pack",
    )(*direct, passed)


def load_kernel(*refs):
    count = (len(refs) - 1) // 2
    sems = refs[-1]
    loads = [pltpu.make_async_copy(refs[i], refs[count + i], sems.at[i]) for i in range(count)]
    for load in loads:
        load.start()
    for load in loads:
        load.wait()


def load(*arrays):
    return pl.pallas_call(
        load_kernel,
        out_shape=[jax.ShapeDtypeStruct(array.shape, array.dtype) for array in arrays],
        in_specs=[HBM] * len(arrays),
        out_specs=[VMEM] * len(arrays),
        scratch_shapes=[pltpu.SemaphoreType.DMA((len(arrays),))],
        compiler_params=pltpu.CompilerParams(vmem_limit_bytes=16 << 20),
        name="load",
    )(*in_hbm(*arrays))


def expert_kernel(first_expert, features, *refs):
    per = len(WAYS)
    here, refs = refs[:4], refs[4:]
    ins, (first_ref, second_ref), refs = refs[: 3 * per], refs[3 * per : 3 * per + 2], refs[3 * per + 2 :]
    outs, saved, scratch = refs[: 3 * len(UNITS)], refs[3 * len(UNITS) : -2 * per], refs[-2 * per :]
    mine = lax.axis_index("hidden")
    rows = scratch[0].shape[1]
    for p, (near, far) in enumerate(WAYS):
        s_in, s_out = scratch[2 * p : 2 * p + 2]
        own_ref, near_ref, far_ref = ins[3 * p : 3 * p + 3]
        away = own_ref.shape[0] * own_ref.shape[1]
        for bits, ref in enumerate(here):
            s_in[mine ^ bits, : rows - away] = ref[:, first_expert + p].reshape(rows - away, 2 * features)
        s_in[mine, rows - away :] = own_ref[...].reshape(away, 2 * features)
        s_in[mine ^ near, rows - away :] = near_ref[...].reshape(away, 2 * features)
        s_in[mine ^ far, rows - away :] = far_ref[0].reshape(away, 2 * features)
        s_in[mine ^ 3, rows - away :] = far_ref[1].reshape(away, 2 * features)
        x = jnp.concatenate([s_in[j, :, :features] for j in range(4)], axis=1)
        g = jnp.concatenate([s_in[j, :, features:] for j in range(4)], axis=1)
        first, second = first_ref[first_expert + p], second_ref[first_expert + p]
        v = jnp.dot(x, first, preferred_element_type=F32)
        grad_hidden = lax.dot_general(g, second, NT, preferred_element_type=F32)
        root = 0.7978845608028654
        square = v * v
        t = jnp.tanh(root * (v + 0.044715 * (v * square)))
        act = (0.5 * v * (1.0 + t)).astype(BF16)
        slope = 0.5 * (1.0 + t) + 0.5 * v * (1.0 - t * t) * (root * (1.0 + 3 * 0.044715 * square))
        grad_pre = (grad_hidden * slope).astype(BF16)
        out = jnp.dot(act, second, preferred_element_type=F32).astype(BF16)
        grad = lax.dot_general(grad_pre, first, NT, preferred_element_type=F32).astype(BF16)
        for j in range(4):
            lanes = slice(j * features, (j + 1) * features)
            s_out[mine ^ j] = jnp.concatenate([out[:, lanes], grad[:, lanes]], axis=1)
        for group, (near, far) in enumerate(UNITS):
            own_ref, far_ref, near_ref = outs[3 * group : 3 * group + 3]
            span = slice(group * rows // len(UNITS), (group + 1) * rows // len(UNITS))
            own_ref[p] = s_out[0, span].reshape(own_ref.shape[1:])
            far_ref[p] = s_out[far, span].reshape(own_ref.shape[1:])
            near_ref[0, p] = s_out[near, span].reshape(own_ref.shape[1:])
            near_ref[1, p] = s_out[3, span].reshape(own_ref.shape[1:])
        for ref, value in zip(saved[4 * p : 4 * p + 4], (x, g, act, grad_pre)):
            ref[...] = value


def run_experts(first_expert, here, pieces, first, second):
    away, capacity, wide = pieces[0].shape
    sources = away + here[0].shape[0]
    _, width, units = first.shape
    rows = sources * capacity
    per = len(WAYS)
    part = (per, sources // len(UNITS), capacity, wide)
    results = pl.pallas_call(
        functools.partial(expert_kernel, first_expert, wide // 2),
        out_shape=[jax.ShapeDtypeStruct(shape, BF16) for shape in (part, part, (2, *part))] * len(UNITS)
        + [jax.ShapeDtypeStruct((rows, n), BF16) for n in (width, width, units, units)] * per,
        in_specs=[VMEM] * (len(here) + len(pieces) + 2),
        out_specs=[VMEM] * (3 * len(UNITS) + 4 * per),
        scratch_shapes=[pltpu.VMEM((4, rows, wide), BF16)] * (2 * per),
        compiler_params=pltpu.CompilerParams(vmem_limit_bytes=16 << 20),
        cost_estimate=pl.CostEstimate(
            flops=8 * per * rows * width * units,
            bytes_accessed=4 * per * width * units,
            transcendentals=per * rows * units,
        ),
        name="experts",
    )(*here, *pieces, first, second)
    parts = [results[3 * group : 3 * group + 3] for group in range(len(UNITS))]
    return parts, results[3 * len(UNITS) :]


def weight_kernel(first_expert, per, *refs):
    saved, rest = refs[: 4 * per], refs[-6:]
    grad_first_hbm, grad_second_hbm, first_buf, second_buf, sems = rest[-5:]
    stores = []
    for p in range(per):
        x, g, act, grad_pre = (ref[...] for ref in saved[4 * p : 4 * p + 4])
        first_buf[p] = lax.dot_general(x, grad_pre, TN, preferred_element_type=F32).astype(BF16)
        stores.append(pltpu.make_async_copy(first_buf.at[p], grad_first_hbm.at[first_expert + p], sems.at[p, 0]))
        stores[-1].start()
        second_buf[p] = lax.dot_general(act, g, TN, preferred_element_type=F32).astype(BF16)
        stores.append(pltpu.make_async_copy(second_buf.at[p], grad_second_hbm.at[first_expert + p], sems.at[p, 1]))
        stores[-1].start()
    for store in stores:
        store.wait()


def weight_grads(chunk, saved, weight_in, weight_out, grads):
    per = len(saved) // 4
    rows, width = saved[0].shape
    units = weight_in.shape[2]
    count = 4 * per
    return pl.pallas_call(
        functools.partial(weight_kernel, chunk * per, per),
        out_shape=[jax.ShapeDtypeStruct(array.shape, BF16) for array in (weight_in, weight_out)],
        in_specs=[VMEM] * count + [HBM] * len(grads),
        out_specs=[HBM] * 2,
        scratch_shapes=[pltpu.VMEM((per, width, units), BF16), pltpu.VMEM((per, units, width), BF16)]
        + [pltpu.SemaphoreType.DMA((per, 2))],
        input_output_aliases={count: 0, count + 1: 1} if grads else {},
        compiler_params=pltpu.CompilerParams(vmem_limit_bytes=20 << 20),
        cost_estimate=pl.CostEstimate(
            flops=4 * per * rows * width * units, bytes_accessed=4 * per * width * units, transcendentals=0
        ),
        name="weight_grads",
    )(*saved, *grads)


def sum_kernel(*refs):
    halves = (len(refs) - 2) // 3
    terms, outs = refs[: 3 * halves], refs[3 * halves :]
    for half in range(halves):
        own, side, passed = terms[3 * half : 3 * half + 3]
        total = own[...].astype(F32) + side[0].astype(F32) + passed[...].astype(F32)
        total = total.astype(BF16)
        for p in range(total.shape[0]):
            for dz, out in enumerate(outs):
                out[0, half * total.shape[0] + p] = total[p, source_of(dz, 0)]
                out[1, half * total.shape[0] + p] = total[p, source_of(dz, 1)]


def sum_rows(terms):
    per, _, capacity, wide = terms[0].shape
    return pl.pallas_call(
        sum_kernel,
        out_shape=[jax.ShapeDtypeStruct((2, len(terms) // 3 * per, capacity, wide), BF16)] * 2,
        in_specs=[VMEM] * len(terms),
        out_specs=[VMEM] * 2,
        compiler_params=pltpu.CompilerParams(vmem_limit_bytes=8 << 20),
        name="sum_rows",
    )(*terms)


def combine_kernel(capacity, exp_dev, picks, place_ref, gate_ref, *refs):
    ins, (out_ref, grad_ref) = refs[:-2], refs[-2:]
    me = lax.axis_index("expert")
    wide = ins[0].shape[-1]
    place = place_ref[...]
    rows, hot = [], []
    for array, index, offset, first_expert in picks:
        rows.append(ins[array][index].reshape(-1, wide))
        first = (me ^ offset) * (exp_dev * capacity) + first_expert * capacity
        hot.append(one_hot(place, first, rows[-1].shape[0]))
    total = lax.dot_general(jnp.concatenate(rows, axis=0), jnp.concatenate(hot, axis=0), TN, preferred_element_type=F32)
    features = out_ref.shape[0]
    out_ref[...] = (gate_ref[...] * total[:features]).astype(BF16)
    grad_ref[...] = total[features:].astype(BF16)


def combine(place, gate, returned, picks, features, exp_dev, capacity):
    count = place.shape[1]
    return pl.pallas_call(
        functools.partial(combine_kernel, capacity, exp_dev, picks),
        out_shape=[jax.ShapeDtypeStruct((features, count), BF16)] * 2,
        in_specs=[VMEM] * (2 + len(returned)),
        out_specs=[VMEM] * 2,
        compiler_params=pltpu.CompilerParams(vmem_limit_bytes=24 << 20),
        name="combine",
    )(place, gate, *returned)


def swap(value, axis, bits):
    size = lax.axis_size(axis)
    return lax.ppermute(value, axis, [(i, i ^ bits) for i in range(size)])


def along_z(buffers):
    direct = [buffers[0]] + [None] * (len(buffers) - 1)
    for dz in reversed(range(1, len(buffers))):
        direct[dz] = swap(buffers[dz], "expert", 2 * dz)
    return direct


def between_cores(direct, *earlier):
    return swap(jnp.stack([rows[1] for rows in after(direct, *earlier)]), "expert", 1)


def after(values, *earlier):
    return lax.optimization_barrier((values, earlier))[0]


def local(tokens, routes, gate_value, weight_in, weight_out, cotangent):
    owners = lax.axis_size("expert")
    exp_dev = weight_in.shape[0]
    count, features = tokens.shape
    capacity = 2 * count // (owners * exp_dev)
    place, gate, buffers = dispatch(
        routes.reshape(1, count), gate_value.reshape(1, count), tokens.T, cotangent.T, owners, exp_dev, capacity
    )
    first, second = load(weight_in, weight_out)
    same, other = buffers[0]
    here = jnp.stack([same, swap(other, "expert", 1)])
    here = [here] + [swap(here, "hidden", bits) for bits in (1, 2, 3)]
    direct = along_z(buffers)[1:]
    rows = pack(direct, between_cores(direct, first, second, *here[1:]))
    per = exp_dev // CHUNKS
    own, near, far = [rows[per * c : per * (c + 1)] for c in range(CHUNKS)], [], []
    for c in range(CHUNKS):
        near.append([swap(rows, "hidden", way[0]) for rows, way in zip(own[c], WAYS)])
    for c in range(CHUNKS):
        pairs = list(zip(own[c], near[c]))
        if c + 1 < CHUNKS:
            pairs[1] = after(pairs[1], near[c + 1])
        pairs = [jnp.stack(pair) for pair in pairs]
        far.append([swap(pair, "hidden", way[1]) for pair, way in zip(pairs, WAYS)])
    parts, saved = [], []
    for c in range(CHUNKS):
        pieces = [piece for three in zip(own[c], near[c], far[c]) for piece in three]
        part, save = run_experts(per * c, here, pieces, first, second)
        parts.append(part)
        saved.append(save)

    def step_back(c, group):
        mine, other, pair = parts[c][group]
        landed = swap(pair, "hidden", UNITS[group][0])
        return [mine, landed, (other.astype(F32) + landed[1].astype(F32)).astype(BF16)]

    far_terms = [step_back(c, 1) for c in range(CHUNKS)]
    near_terms = [step_back(c, 0) for c in range(CHUNKS)]
    def finish(terms, group):
        passed = [swap(both, "hidden", UNITS[group][1]) for _, _, both in terms]
        totals = sum_rows([rows for (mine, landed, _), last in zip(terms, passed) for rows in (mine, landed, last)])
        return [swap(rows, "expert", 2 * dz) if dz else rows for dz, rows in zip(OFFSETS[group], totals)], totals

    grads = weight_grads(0, saved[0], weight_in, weight_out, [])
    near_terms[1][2] = after(near_terms[1][2], grads)
    homeward = []
    for c in range(CHUNKS):
        if c:
            far_terms[c][2] = after(far_terms[c][2], homeward[-1][-1])
        homeward.append((1, per * c, *finish(far_terms[c : c + 1], 1)))
    near_terms[0][0] = after(near_terms[0][0], homeward[-1][-1])
    homeward.append((0, 0, *finish(near_terms, 0)))
    grads = weight_grads(1, after(saved[1], homeward[-1][-1]), weight_in, weight_out, grads)
    returned, picks = [], []
    for group, first_expert, direct, _ in homeward:
        for j, dz in enumerate(OFFSETS[group]):
            picks.append((len(returned) + j, (0,), 2 * dz, first_expert))
            picks.append((len(returned) + 2, (j,), 2 * dz + 1, first_expert))
        returned.extend([*direct, between_cores(direct, *grads)])
    layer_out, grad_tokens = combine(place, gate, returned, picks, features, exp_dev, capacity)
    return layer_out.T, grad_tokens.T, grads[0], grads[1]


def solution(mesh):
    in_specs = (
        P("expert", "hidden"),
        P("expert", None),
        P("expert", None),
        P("expert", None, "hidden"),
        P("expert", "hidden", None),
        P("expert", "hidden"),
    )
    out_specs = (
        P("expert", "hidden"),
        P("expert", "hidden"),
        P("expert", None, "hidden"),
        P("expert", "hidden", None),
    )

    def whole(*args):
        wide = 2 * args[0].shape[1] // mesh.shape["hidden"]
        capacity = 2 * args[0].shape[0] // args[3].shape[0]
        four = mesh.shape["hidden"] == 4 and args[3].shape[0] == 4 * mesh.shape["expert"]
        fits = four and mesh.shape["expert"] == 8 and wide % 128 == 0 and capacity % 16 == 0
        body = local if fits else general
        return jax.shard_map(body, mesh=mesh, in_specs=in_specs, out_specs=out_specs, check_vma=False)(*args)

    return whole
```

```python
import functools
import jax
import jax.numpy as jnp
from jax import lax
from jax.experimental import pallas as pl
from jax.experimental.pallas import tpu as pltpu
from jax.sharding import PartitionSpec as P

CHUNKS = 2
BF16 = jnp.bfloat16
F32 = jnp.float32


def gelu_tanh(values):
    return jax.nn.gelu(values, approximate=True)


def local_places(routes, experts, capacity):
    chosen = routes[:, 0]
    matches = (chosen[:, None] == jnp.arange(experts, dtype=jnp.int32)[None, :]).astype(jnp.int32)
    before = jnp.cumsum(matches, axis=0) - matches
    return chosen * capacity + jnp.sum(before * matches, axis=1)


def general(tokens, routes, gate_value, weight_in, weight_out, cotangent):
    owners = lax.axis_size("expert")
    blocks = lax.axis_size("hidden")
    exp_dev = weight_in.shape[0]
    experts = owners * exp_dev
    capacity = max(2, 2 * tokens.shape[0] // experts)
    slot_count = experts * capacity
    features = tokens.shape[1]
    full_width = weight_out.shape[2]
    units = weight_in.shape[2]
    line = exp_dev * capacity * features
    placed = local_places(routes, experts, capacity)
    scaled = (gate_value * cotangent.astype(F32)).astype(BF16)
    first_four = weight_in.reshape(exp_dev, blocks, features, units)
    second_four = weight_out.reshape(exp_dev, units, blocks, features)

    def to_slots(values):
        filled = jnp.zeros((slot_count, features), BF16).at[placed].set(values)
        return filled.reshape(owners, line)

    def rows_of(values):
        arrived = lax.all_to_all(to_slots(values), "expert", split_axis=0, concat_axis=0, tiled=True)
        gathered = lax.all_gather(arrived[None], "hidden", axis=0, tiled=True)
        return gathered.reshape(blocks, owners, exp_dev, capacity, features)

    def back(part):
        flat = part.reshape(blocks, owners, line).astype(BF16)
        total = lax.psum_scatter(flat, "hidden", scatter_dimension=0, tiled=True)
        total = total.astype(F32)[0].astype(BF16)
        returned = lax.all_to_all(total, "expert", split_axis=0, concat_axis=0, tiled=True)
        return returned.reshape(slot_count, features)[placed]

    rows_x = rows_of(tokens)
    rows_g = rows_of(scaled)
    preact = jnp.einsum("nsecf,enfh->sech", rows_x, first_four, preferred_element_type=F32)
    activation, pullback = jax.vjp(gelu_tanh, preact)
    hidden_act = activation.astype(BF16)
    out_part = jnp.einsum("sech,ehnf->nsecf", hidden_act, second_four, preferred_element_type=F32)
    grad_hidden = jnp.einsum("nsecf,ehnf->sech", rows_g, second_four, preferred_element_type=F32)
    grad_pre = pullback(grad_hidden)[0].astype(BF16)
    grad_part = jnp.einsum("sech,enfh->nsecf", grad_pre, first_four, preferred_element_type=F32)
    grad_weight_in = jnp.einsum("nsecf,sech->enfh", rows_x, grad_pre, preferred_element_type=F32)
    grad_weight_out = jnp.einsum("sech,nsecf->ehnf", hidden_act, rows_g, preferred_element_type=F32)
    layer_out = (gate_value * back(out_part).astype(F32)).astype(BF16)
    return (
        layer_out,
        back(grad_part),
        grad_weight_in.astype(BF16).reshape(exp_dev, full_width, units),
        grad_weight_out.astype(BF16).reshape(exp_dev, units, full_width),
    )


NT = (((1,), (1,)), ((), ()))
TN = (((0,), (0,)), ((), ()))
VMEM = pl.BlockSpec(memory_space=pltpu.VMEM)
HBM = pl.BlockSpec(memory_space=pltpu.HBM)
WAYS = ((1, 2), (2, 1))
UNITS = ((2, 1), (1, 2))
OFFSETS = ((0, 1), (2, 3))


def one_hot(place, first, count):
    rows = lax.broadcasted_iota(jnp.int32, (count, place.shape[1]), 0)
    return jnp.where(rows == place - first, 1.0, 0.0).astype(BF16)


def dispatch_kernel(exp_dev, capacity, *refs):
    ins, place_ref, gate_ref, rest = refs[:4], refs[4], refs[5], refs[6:]
    buffers, (routes_buf, tok_buf, cot_buf, sems) = rest[:-4], rest[-4:]
    loads = [
        pltpu.make_async_copy(source, target, sems.at[i])
        for i, (source, target) in enumerate(zip(ins, (routes_buf, gate_ref, tok_buf, cot_buf)))
    ]
    for load in loads:
        load.start()
    tokens = routes_buf.shape[1]
    experts = 2 * len(buffers) * exp_dev
    line = exp_dev * capacity
    me = lax.axis_index("expert")
    earlier = lax.broadcasted_iota(jnp.int32, (tokens, tokens), 0) < lax.broadcasted_iota(
        jnp.int32, (tokens, tokens), 1
    )
    earlier = jnp.where(earlier, 1.0, 0.0).astype(BF16)
    loads[0].wait()
    chosen = routes_buf[...]
    matches = lax.broadcasted_iota(jnp.int32, (experts, tokens), 0) == chosen
    before = jnp.dot(jnp.where(matches, 1.0, 0.0).astype(BF16), earlier, preferred_element_type=F32)
    within = jnp.sum(jnp.where(matches, before, 0.0), axis=0, keepdims=True).astype(jnp.int32)
    place = chosen * capacity + within
    place_ref[...] = place
    for load in loads[1:]:
        load.wait()
    scaled = (gate_ref[...] * cot_buf[...].astype(F32)).astype(BF16)
    both = jnp.concatenate([tok_buf[...], scaled], axis=0)
    for dz, ref in enumerate(buffers):
        firsts = [(me ^ offset) * line for offset in (2 * dz, 2 * dz + 1)]
        hot = jnp.concatenate([one_hot(place, first, line) for first in firsts], axis=0)
        filled = lax.dot_general(hot, both, NT, preferred_element_type=F32).astype(BF16)
        ref[...] = filled.reshape(ref.shape)


def in_hbm(*arrays):
    return [pltpu.with_memory_space_constraint(array, pltpu.HBM) for array in arrays]


def dispatch(routes, gate, tokens, cotangent, owners, exp_dev, capacity):
    features, count = tokens.shape
    buffer = jax.ShapeDtypeStruct((2, exp_dev, capacity, 2 * features), BF16)
    buffers = owners // 2
    place, gate, *buffers = pl.pallas_call(
        functools.partial(dispatch_kernel, exp_dev, capacity),
        out_shape=[jax.ShapeDtypeStruct((1, count), jnp.int32), jax.ShapeDtypeStruct((1, count), F32)]
        + [buffer] * buffers,
        in_specs=[HBM] * 4,
        out_specs=[VMEM] * (2 + buffers),
        scratch_shapes=[pltpu.VMEM((1, count), jnp.int32)]
        + [pltpu.VMEM((features, count), BF16)] * 2
        + [pltpu.SemaphoreType.DMA((4,))],
        compiler_params=pltpu.CompilerParams(vmem_limit_bytes=24 << 20),
        name="dispatch",
    )(*in_hbm(routes, gate, tokens, cotangent))
    return place, gate, buffers


def source_of(dz, other_core):
    return 2 * dz + other_core


def pack_kernel(*refs):
    per = refs[0].shape[1]
    direct, passed, outs = refs[: -per - 1], refs[-per - 1], refs[-per:]
    for p, out in enumerate(outs):
        for i, ref in enumerate(direct):
            out[source_of(i, 0)] = ref[0, p]
            out[source_of(i, 1)] = passed[i, p]


def pack(direct, passed):
    _, per, capacity, wide = direct[0].shape
    return pl.pallas_call(
        pack_kernel,
        out_shape=[jax.ShapeDtypeStruct((2 * len(direct), capacity, wide), BF16)] * per,
        in_specs=[VMEM] * (1 + len(direct)),
        out_specs=[VMEM] * per,
        compiler_params=pltpu.CompilerParams(vmem_limit_bytes=8 << 20),
        name="pack",
    )(*direct, passed)


def load_kernel(*refs):
    count = (len(refs) - 1) // 2
    sems = refs[-1]
    loads = [pltpu.make_async_copy(refs[i], refs[count + i], sems.at[i]) for i in range(count)]
    for load in loads:
        load.start()
    for load in loads:
        load.wait()


def load(*arrays):
    return pl.pallas_call(
        load_kernel,
        out_shape=[jax.ShapeDtypeStruct(array.shape, array.dtype) for array in arrays],
        in_specs=[HBM] * len(arrays),
        out_specs=[VMEM] * len(arrays),
        scratch_shapes=[pltpu.SemaphoreType.DMA((len(arrays),))],
        compiler_params=pltpu.CompilerParams(vmem_limit_bytes=16 << 20),
        name="load",
    )(*in_hbm(*arrays))


def expert_kernel(first_expert, features, *refs):
    per = len(WAYS)
    here, refs = refs[:4], refs[4:]
    ins, (first_ref, second_ref), refs = refs[: 3 * per], refs[3 * per : 3 * per + 2], refs[3 * per + 2 :]
    outs, saved, scratch = refs[: 3 * len(UNITS)], refs[3 * len(UNITS) : -2 * per], refs[-2 * per :]
    mine = lax.axis_index("hidden")
    rows = scratch[0].shape[1]
    for p, (near, far) in enumerate(WAYS):
        s_in, s_out = scratch[2 * p : 2 * p + 2]
        own_ref, near_ref, far_ref = ins[3 * p : 3 * p + 3]
        away = own_ref.shape[0] * own_ref.shape[1]
        for bits, ref in enumerate(here):
            s_in[mine ^ bits, : rows - away] = ref[:, first_expert + p].reshape(rows - away, 2 * features)
        s_in[mine, rows - away :] = own_ref[...].reshape(away, 2 * features)
        s_in[mine ^ near, rows - away :] = near_ref[...].reshape(away, 2 * features)
        s_in[mine ^ far, rows - away :] = far_ref[0].reshape(away, 2 * features)
        s_in[mine ^ 3, rows - away :] = far_ref[1].reshape(away, 2 * features)
        x = jnp.concatenate([s_in[j, :, :features] for j in range(4)], axis=1)
        g = jnp.concatenate([s_in[j, :, features:] for j in range(4)], axis=1)
        first, second = first_ref[first_expert + p], second_ref[first_expert + p]
        v = jnp.dot(x, first, preferred_element_type=F32)
        grad_hidden = lax.dot_general(g, second, NT, preferred_element_type=F32)
        root = 0.7978845608028654
        square = v * v
        t = jnp.tanh(root * (v + 0.044715 * (v * square)))
        act = (0.5 * v * (1.0 + t)).astype(BF16)
        slope = 0.5 * (1.0 + t) + 0.5 * v * (1.0 - t * t) * (root * (1.0 + 3 * 0.044715 * square))
        grad_pre = (grad_hidden * slope).astype(BF16)
        out = jnp.dot(act, second, preferred_element_type=F32).astype(BF16)
        grad = lax.dot_general(grad_pre, first, NT, preferred_element_type=F32).astype(BF16)
        for j in range(4):
            lanes = slice(j * features, (j + 1) * features)
            s_out[mine ^ j] = jnp.concatenate([out[:, lanes], grad[:, lanes]], axis=1)
        for group, (near, far) in enumerate(UNITS):
            own_ref, far_ref, near_ref = outs[3 * group : 3 * group + 3]
            span = slice(group * rows // len(UNITS), (group + 1) * rows // len(UNITS))
            own_ref[p] = s_out[0, span].reshape(own_ref.shape[1:])
            far_ref[p] = s_out[far, span].reshape(own_ref.shape[1:])
            near_ref[0, p] = s_out[near, span].reshape(own_ref.shape[1:])
            near_ref[1, p] = s_out[3, span].reshape(own_ref.shape[1:])
        for ref, value in zip(saved[4 * p : 4 * p + 4], (x, g, act, grad_pre)):
            ref[...] = value


def run_experts(first_expert, here, pieces, first, second):
    away, capacity, wide = pieces[0].shape
    sources = away + here[0].shape[0]
    _, width, units = first.shape
    rows = sources * capacity
    per = len(WAYS)
    part = (per, sources // len(UNITS), capacity, wide)
    results = pl.pallas_call(
        functools.partial(expert_kernel, first_expert, wide // 2),
        out_shape=[jax.ShapeDtypeStruct(shape, BF16) for shape in (part, part, (2, *part))] * len(UNITS)
        + [jax.ShapeDtypeStruct((rows, n), BF16) for n in (width, width, units, units)] * per,
        in_specs=[VMEM] * (len(here) + len(pieces) + 2),
        out_specs=[VMEM] * (3 * len(UNITS) + 4 * per),
        scratch_shapes=[pltpu.VMEM((4, rows, wide), BF16)] * (2 * per),
        compiler_params=pltpu.CompilerParams(vmem_limit_bytes=16 << 20),
        cost_estimate=pl.CostEstimate(
            flops=8 * per * rows * width * units,
            bytes_accessed=4 * per * width * units,
            transcendentals=per * rows * units,
        ),
        name="experts",
    )(*here, *pieces, first, second)
    parts = [results[3 * group : 3 * group + 3] for group in range(len(UNITS))]
    return parts, results[3 * len(UNITS) :]


def weight_kernel(first_expert, per, *refs):
    saved, rest = refs[: 4 * per], refs[-6:]
    grad_first_hbm, grad_second_hbm, first_buf, second_buf, sems = rest[-5:]
    stores = []
    for p in range(per):
        x, g, act, grad_pre = (ref[...] for ref in saved[4 * p : 4 * p + 4])
        first_buf[p] = lax.dot_general(x, grad_pre, TN, preferred_element_type=F32).astype(BF16)
        stores.append(pltpu.make_async_copy(first_buf.at[p], grad_first_hbm.at[first_expert + p], sems.at[p, 0]))
        stores[-1].start()
        second_buf[p] = lax.dot_general(act, g, TN, preferred_element_type=F32).astype(BF16)
        stores.append(pltpu.make_async_copy(second_buf.at[p], grad_second_hbm.at[first_expert + p], sems.at[p, 1]))
        stores[-1].start()
    for store in stores:
        store.wait()


def weight_grads(chunk, saved, weight_in, weight_out, grads):
    per = len(saved) // 4
    rows, width = saved[0].shape
    units = weight_in.shape[2]
    count = 4 * per
    return pl.pallas_call(
        functools.partial(weight_kernel, chunk * per, per),
        out_shape=[jax.ShapeDtypeStruct(array.shape, BF16) for array in (weight_in, weight_out)],
        in_specs=[VMEM] * count + [HBM] * len(grads),
        out_specs=[HBM] * 2,
        scratch_shapes=[pltpu.VMEM((per, width, units), BF16), pltpu.VMEM((per, units, width), BF16)]
        + [pltpu.SemaphoreType.DMA((per, 2))],
        input_output_aliases={count: 0, count + 1: 1} if grads else {},
        compiler_params=pltpu.CompilerParams(vmem_limit_bytes=20 << 20),
        cost_estimate=pl.CostEstimate(
            flops=4 * per * rows * width * units, bytes_accessed=4 * per * width * units, transcendentals=0
        ),
        name="weight_grads",
    )(*saved, *grads)


def sum_kernel(*refs):
    halves = (len(refs) - 2) // 3
    terms, outs = refs[: 3 * halves], refs[3 * halves :]
    for half in range(halves):
        own, side, passed = terms[3 * half : 3 * half + 3]
        total = own[...].astype(F32) + side[0].astype(F32) + passed[...].astype(F32)
        total = total.astype(BF16)
        for p in range(total.shape[0]):
            for dz, out in enumerate(outs):
                out[0, half * total.shape[0] + p] = total[p, source_of(dz, 0)]
                out[1, half * total.shape[0] + p] = total[p, source_of(dz, 1)]


def sum_rows(terms):
    per, _, capacity, wide = terms[0].shape
    return pl.pallas_call(
        sum_kernel,
        out_shape=[jax.ShapeDtypeStruct((2, len(terms) // 3 * per, capacity, wide), BF16)] * 2,
        in_specs=[VMEM] * len(terms),
        out_specs=[VMEM] * 2,
        compiler_params=pltpu.CompilerParams(vmem_limit_bytes=8 << 20),
        name="sum_rows",
    )(*terms)


def combine_kernel(capacity, exp_dev, picks, place_ref, gate_ref, *refs):
    ins, (out_ref, grad_ref) = refs[:-2], refs[-2:]
    me = lax.axis_index("expert")
    wide = ins[0].shape[-1]
    place = place_ref[...]
    rows, hot = [], []
    for array, index, offset, first_expert in picks:
        rows.append(ins[array][index].reshape(-1, wide))
        first = (me ^ offset) * (exp_dev * capacity) + first_expert * capacity
        hot.append(one_hot(place, first, rows[-1].shape[0]))
    total = lax.dot_general(jnp.concatenate(rows, axis=0), jnp.concatenate(hot, axis=0), TN, preferred_element_type=F32)
    features = out_ref.shape[0]
    out_ref[...] = (gate_ref[...] * total[:features]).astype(BF16)
    grad_ref[...] = total[features:].astype(BF16)


def combine(place, gate, returned, picks, features, exp_dev, capacity):
    count = place.shape[1]
    return pl.pallas_call(
        functools.partial(combine_kernel, capacity, exp_dev, picks),
        out_shape=[jax.ShapeDtypeStruct((features, count), BF16)] * 2,
        in_specs=[VMEM] * (2 + len(returned)),
        out_specs=[VMEM] * 2,
        compiler_params=pltpu.CompilerParams(vmem_limit_bytes=24 << 20),
        name="combine",
    )(place, gate, *returned)


def swap(value, axis, bits):
    size = lax.axis_size(axis)
    return lax.ppermute(value, axis, [(i, i ^ bits) for i in range(size)])


def along_z(buffers):
    direct = [buffers[0]] + [None] * (len(buffers) - 1)
    for dz in reversed(range(1, len(buffers))):
        direct[dz] = swap(buffers[dz], "expert", 2 * dz)
    return direct


def between_cores(direct, *earlier):
    return swap(jnp.stack([rows[1] for rows in after(direct, *earlier)]), "expert", 1)


def after(values, *earlier):
    return lax.optimization_barrier((values, earlier))[0]


def local(tokens, routes, gate_value, weight_in, weight_out, cotangent):
    owners = lax.axis_size("expert")
    exp_dev = weight_in.shape[0]
    count, features = tokens.shape
    capacity = 2 * count // (owners * exp_dev)
    place, gate, buffers = dispatch(
        routes.reshape(1, count), gate_value.reshape(1, count), tokens.T, cotangent.T, owners, exp_dev, capacity
    )
    first, second = load(weight_in, weight_out)
    same, other = buffers[0]
    here = jnp.stack([same, swap(other, "expert", 1)])
    here = [here] + [swap(here, "hidden", bits) for bits in (1, 2, 3)]
    direct = along_z(buffers)[1:]
    rows = pack(direct, between_cores(direct, first, second, *here[1:]))
    per = exp_dev // CHUNKS
    own, near, far = [rows[per * c : per * (c + 1)] for c in range(CHUNKS)], [], []
    for c in range(CHUNKS):
        near.append([swap(rows, "hidden", way[0]) for rows, way in zip(own[c], WAYS)])
    for c in range(CHUNKS):
        pairs = list(zip(own[c], near[c]))
        if c + 1 < CHUNKS:
            pairs[1] = after(pairs[1], near[c + 1])
        pairs = [jnp.stack(pair) for pair in pairs]
        far.append([swap(pair, "hidden", way[1]) for pair, way in zip(pairs, WAYS)])
    parts, saved = [], []
    for c in range(CHUNKS):
        pieces = [piece for three in zip(own[c], near[c], far[c]) for piece in three]
        part, save = run_experts(per * c, here, pieces, first, second)
        parts.append(part)
        saved.append(save)

    def step_back(c, group):
        mine, other, pair = parts[c][group]
        landed = swap(pair, "hidden", UNITS[group][0])
        return [mine, landed, (other.astype(F32) + landed[1].astype(F32)).astype(BF16)]

    far_terms = [step_back(c, 1) for c in range(CHUNKS)]
    near_terms = [step_back(c, 0) for c in range(CHUNKS)]
    def finish(terms, group):
        passed = [swap(both, "hidden", UNITS[group][1]) for _, _, both in terms]
        totals = sum_rows([rows for (mine, landed, _), last in zip(terms, passed) for rows in (mine, landed, last)])
        return [swap(rows, "expert", 2 * dz) if dz else rows for dz, rows in zip(OFFSETS[group], totals)], totals

    grads = weight_grads(0, after(saved[0], far_terms[0][2], near_terms[0][2]), weight_in, weight_out, [])
    far_terms[0][0] = after(far_terms[0][0], grads)
    homeward = []
    for c in range(CHUNKS):
        if c:
            far_terms[c][2] = after(far_terms[c][2], homeward[-1][-1])
        homeward.append((1, per * c, *finish(far_terms[c : c + 1], 1)))
    near_terms[0][0] = after(near_terms[0][0], homeward[-1][-1])
    homeward.append((0, 0, *finish(near_terms, 0)))
    grads = weight_grads(1, after(saved[1], homeward[-1][-1]), weight_in, weight_out, grads)
    returned, picks = [], []
    for group, first_expert, direct, _ in homeward:
        for j, dz in enumerate(OFFSETS[group]):
            picks.append((len(returned) + j, (0,), 2 * dz, first_expert))
            picks.append((len(returned) + 2, (j,), 2 * dz + 1, first_expert))
        returned.extend([*direct, between_cores(direct, *grads)])
    layer_out, grad_tokens = combine(place, gate, returned, picks, features, exp_dev, capacity)
    return layer_out.T, grad_tokens.T, grads[0], grads[1]


def solution(mesh):
    in_specs = (
        P("expert", "hidden"),
        P("expert", None),
        P("expert", None),
        P("expert", None, "hidden"),
        P("expert", "hidden", None),
        P("expert", "hidden"),
    )
    out_specs = (
        P("expert", "hidden"),
        P("expert", "hidden"),
        P("expert", None, "hidden"),
        P("expert", "hidden", None),
    )

    def whole(*args):
        wide = 2 * args[0].shape[1] // mesh.shape["hidden"]
        capacity = 2 * args[0].shape[0] // args[3].shape[0]
        four = mesh.shape["hidden"] == 4 and args[3].shape[0] == 4 * mesh.shape["expert"]
        fits = four and mesh.shape["expert"] == 8 and wide % 128 == 0 and capacity % 16 == 0
        body = local if fits else general
        return jax.shard_map(body, mesh=mesh, in_specs=in_specs, out_specs=out_specs, check_vma=False)(*args)

    return whole
```

```python
import functools
import jax
import jax.numpy as jnp
from jax import lax
from jax.experimental import pallas as pl
from jax.experimental.pallas import tpu as pltpu
from jax.sharding import PartitionSpec as P

CHUNKS = 2
BF16 = jnp.bfloat16
F32 = jnp.float32


def gelu_tanh(values):
    return jax.nn.gelu(values, approximate=True)


def local_places(routes, experts, capacity):
    chosen = routes[:, 0]
    matches = (chosen[:, None] == jnp.arange(experts, dtype=jnp.int32)[None, :]).astype(jnp.int32)
    before = jnp.cumsum(matches, axis=0) - matches
    return chosen * capacity + jnp.sum(before * matches, axis=1)


def general(tokens, routes, gate_value, weight_in, weight_out, cotangent):
    owners = lax.axis_size("expert")
    blocks = lax.axis_size("hidden")
    exp_dev = weight_in.shape[0]
    experts = owners * exp_dev
    capacity = max(2, 2 * tokens.shape[0] // experts)
    slot_count = experts * capacity
    features = tokens.shape[1]
    full_width = weight_out.shape[2]
    units = weight_in.shape[2]
    line = exp_dev * capacity * features
    placed = local_places(routes, experts, capacity)
    scaled = (gate_value * cotangent.astype(F32)).astype(BF16)
    first_four = weight_in.reshape(exp_dev, blocks, features, units)
    second_four = weight_out.reshape(exp_dev, units, blocks, features)

    def to_slots(values):
        filled = jnp.zeros((slot_count, features), BF16).at[placed].set(values)
        return filled.reshape(owners, line)

    def rows_of(values):
        arrived = lax.all_to_all(to_slots(values), "expert", split_axis=0, concat_axis=0, tiled=True)
        gathered = lax.all_gather(arrived[None], "hidden", axis=0, tiled=True)
        return gathered.reshape(blocks, owners, exp_dev, capacity, features)

    def back(part):
        flat = part.reshape(blocks, owners, line).astype(BF16)
        total = lax.psum_scatter(flat, "hidden", scatter_dimension=0, tiled=True)
        total = total.astype(F32)[0].astype(BF16)
        returned = lax.all_to_all(total, "expert", split_axis=0, concat_axis=0, tiled=True)
        return returned.reshape(slot_count, features)[placed]

    rows_x = rows_of(tokens)
    rows_g = rows_of(scaled)
    preact = jnp.einsum("nsecf,enfh->sech", rows_x, first_four, preferred_element_type=F32)
    activation, pullback = jax.vjp(gelu_tanh, preact)
    hidden_act = activation.astype(BF16)
    out_part = jnp.einsum("sech,ehnf->nsecf", hidden_act, second_four, preferred_element_type=F32)
    grad_hidden = jnp.einsum("nsecf,ehnf->sech", rows_g, second_four, preferred_element_type=F32)
    grad_pre = pullback(grad_hidden)[0].astype(BF16)
    grad_part = jnp.einsum("sech,enfh->nsecf", grad_pre, first_four, preferred_element_type=F32)
    grad_weight_in = jnp.einsum("nsecf,sech->enfh", rows_x, grad_pre, preferred_element_type=F32)
    grad_weight_out = jnp.einsum("sech,nsecf->ehnf", hidden_act, rows_g, preferred_element_type=F32)
    layer_out = (gate_value * back(out_part).astype(F32)).astype(BF16)
    return (
        layer_out,
        back(grad_part),
        grad_weight_in.astype(BF16).reshape(exp_dev, full_width, units),
        grad_weight_out.astype(BF16).reshape(exp_dev, units, full_width),
    )


NT = (((1,), (1,)), ((), ()))
TN = (((0,), (0,)), ((), ()))
VMEM = pl.BlockSpec(memory_space=pltpu.VMEM)
HBM = pl.BlockSpec(memory_space=pltpu.HBM)
WAYS = ((1, 2), (2, 1))
FAR = (((0,), 4, 4, WAYS[0]), ((1,), 4, 4, WAYS[1]))
UNITS = ((*FAR, ((0, 1), 0, 4, WAYS[0])), (*FAR, ((0, 1), 0, 4, WAYS[1])))


def one_hot(place, first, count):
    rows = lax.broadcasted_iota(jnp.int32, (count, place.shape[1]), 0)
    return jnp.where(rows == place - first, 1.0, 0.0).astype(BF16)


def dispatch_kernel(exp_dev, capacity, *refs):
    ins, place_ref, gate_ref, rest = refs[:4], refs[4], refs[5], refs[6:]
    buffers, (routes_buf, tok_buf, cot_buf, sems) = rest[:-4], rest[-4:]
    loads = [
        pltpu.make_async_copy(source, target, sems.at[i])
        for i, (source, target) in enumerate(zip(ins, (routes_buf, gate_ref, tok_buf, cot_buf)))
    ]
    for load in loads:
        load.start()
    tokens = routes_buf.shape[1]
    experts = 2 * len(buffers) * exp_dev
    line = exp_dev * capacity
    me = lax.axis_index("expert")
    earlier = lax.broadcasted_iota(jnp.int32, (tokens, tokens), 0) < lax.broadcasted_iota(
        jnp.int32, (tokens, tokens), 1
    )
    earlier = jnp.where(earlier, 1.0, 0.0).astype(BF16)
    loads[0].wait()
    chosen = routes_buf[...]
    matches = lax.broadcasted_iota(jnp.int32, (experts, tokens), 0) == chosen
    before = jnp.dot(jnp.where(matches, 1.0, 0.0).astype(BF16), earlier, preferred_element_type=F32)
    within = jnp.sum(jnp.where(matches, before, 0.0), axis=0, keepdims=True).astype(jnp.int32)
    place = chosen * capacity + within
    place_ref[...] = place
    for load in loads[1:]:
        load.wait()
    scaled = (gate_ref[...] * cot_buf[...].astype(F32)).astype(BF16)
    both = jnp.concatenate([tok_buf[...], scaled], axis=0)
    for dz, ref in enumerate(buffers):
        firsts = [(me ^ offset) * line for offset in (2 * dz, 2 * dz + 1)]
        hot = jnp.concatenate([one_hot(place, first, line) for first in firsts], axis=0)
        filled = lax.dot_general(hot, both, NT, preferred_element_type=F32).astype(BF16)
        ref[...] = filled.reshape(ref.shape)


def in_hbm(*arrays):
    return [pltpu.with_memory_space_constraint(array, pltpu.HBM) for array in arrays]


def dispatch(routes, gate, tokens, cotangent, owners, exp_dev, capacity):
    features, count = tokens.shape
    buffer = jax.ShapeDtypeStruct((2, exp_dev, capacity, 2 * features), BF16)
    buffers = owners // 2
    place, gate, *buffers = pl.pallas_call(
        functools.partial(dispatch_kernel, exp_dev, capacity),
        out_shape=[jax.ShapeDtypeStruct((1, count), jnp.int32), jax.ShapeDtypeStruct((1, count), F32)]
        + [buffer] * buffers,
        in_specs=[HBM] * 4,
        out_specs=[VMEM] * (2 + buffers),
        scratch_shapes=[pltpu.VMEM((1, count), jnp.int32)]
        + [pltpu.VMEM((features, count), BF16)] * 2
        + [pltpu.SemaphoreType.DMA((4,))],
        compiler_params=pltpu.CompilerParams(vmem_limit_bytes=24 << 20),
        name="dispatch",
    )(*in_hbm(routes, gate, tokens, cotangent))
    return place, gate, buffers


def source_of(dz, other_core):
    return 2 * dz + other_core


def pack_kernel(*refs):
    per = refs[0].shape[1]
    direct, passed, outs = refs[: -per - 1], refs[-per - 1], refs[-per:]
    for p, out in enumerate(outs):
        for i, ref in enumerate(direct):
            out[source_of(i, 0)] = ref[0, p]
            out[source_of(i, 1)] = passed[i, p]


def pack(direct, passed):
    _, per, capacity, wide = direct[0].shape
    return pl.pallas_call(
        pack_kernel,
        out_shape=[jax.ShapeDtypeStruct((2 * len(direct), capacity, wide), BF16)] * per,
        in_specs=[VMEM] * (1 + len(direct)),
        out_specs=[VMEM] * per,
        compiler_params=pltpu.CompilerParams(vmem_limit_bytes=8 << 20),
        name="pack",
    )(*direct, passed)


def load_kernel(*refs):
    count = (len(refs) - 1) // 2
    sems = refs[-1]
    loads = [pltpu.make_async_copy(refs[i], refs[count + i], sems.at[i]) for i in range(count)]
    for load in loads:
        load.start()
    for load in loads:
        load.wait()


def load(*arrays):
    return pl.pallas_call(
        load_kernel,
        out_shape=[jax.ShapeDtypeStruct(array.shape, array.dtype) for array in arrays],
        in_specs=[HBM] * len(arrays),
        out_specs=[VMEM] * len(arrays),
        scratch_shapes=[pltpu.SemaphoreType.DMA((len(arrays),))],
        compiler_params=pltpu.CompilerParams(vmem_limit_bytes=16 << 20),
        name="load",
    )(*in_hbm(*arrays))


def expert_kernel(first_expert, features, units, *refs):
    per = len(WAYS)
    here, refs = refs[:4], refs[4:]
    ins, (first_ref, second_ref), refs = refs[: 3 * per], refs[3 * per : 3 * per + 2], refs[3 * per + 2 :]
    outs, saved, scratch = refs[: 3 * len(units)], refs[3 * len(units) : -2 * per], refs[-2 * per :]
    mine = lax.axis_index("hidden")
    rows = scratch[0].shape[1]
    for p, (near, far) in enumerate(WAYS):
        s_in, s_out = scratch[2 * p : 2 * p + 2]
        own_ref, near_ref, far_ref = ins[3 * p : 3 * p + 3]
        away = own_ref.shape[0] * own_ref.shape[1]
        for bits, ref in enumerate(here):
            s_in[mine ^ bits, : rows - away] = ref[:, first_expert + p].reshape(rows - away, 2 * features)
        s_in[mine, rows - away :] = own_ref[...].reshape(away, 2 * features)
        s_in[mine ^ near, rows - away :] = near_ref[...].reshape(away, 2 * features)
        s_in[mine ^ far, rows - away :] = far_ref[0].reshape(away, 2 * features)
        s_in[mine ^ 3, rows - away :] = far_ref[1].reshape(away, 2 * features)
        x = jnp.concatenate([s_in[j, :, :features] for j in range(4)], axis=1)
        g = jnp.concatenate([s_in[j, :, features:] for j in range(4)], axis=1)
        first, second = first_ref[first_expert + p], second_ref[first_expert + p]
        v = jnp.dot(x, first, preferred_element_type=F32)
        grad_hidden = lax.dot_general(g, second, NT, preferred_element_type=F32)
        root = 0.7978845608028654
        square = v * v
        t = jnp.tanh(root * (v + 0.044715 * (v * square)))
        act = (0.5 * v * (1.0 + t)).astype(BF16)
        slope = 0.5 * (1.0 + t) + 0.5 * v * (1.0 - t * t) * (root * (1.0 + 3 * 0.044715 * square))
        grad_pre = (grad_hidden * slope).astype(BF16)
        out = jnp.dot(act, second, preferred_element_type=F32).astype(BF16)
        grad = lax.dot_general(grad_pre, first, NT, preferred_element_type=F32).astype(BF16)
        for j in range(4):
            lanes = slice(j * features, (j + 1) * features)
            s_out[mine ^ j] = jnp.concatenate([out[:, lanes], grad[:, lanes]], axis=1)
        for unit, (experts, source, count, (near, far)) in enumerate(units):
            if p not in experts:
                continue
            i = experts.index(p)
            own_ref, far_ref, near_ref = outs[3 * unit : 3 * unit + 3]
            capacity = own_ref.shape[2]
            span = slice(source * capacity, (source + count) * capacity)
            own_ref[i] = s_out[0, span].reshape(own_ref.shape[1:])
            far_ref[i] = s_out[far, span].reshape(own_ref.shape[1:])
            near_ref[0, i] = s_out[near, span].reshape(own_ref.shape[1:])
            near_ref[1, i] = s_out[3, span].reshape(own_ref.shape[1:])
        for ref, value in zip(saved[4 * p : 4 * p + 4], (x, g, act, grad_pre)):
            ref[...] = value


def run_experts(first_expert, here, pieces, first, second, units):
    away, capacity, wide = pieces[0].shape
    sources = away + here[0].shape[0]
    _, width, hidden = first.shape
    rows = sources * capacity
    per = len(WAYS)
    parts = [(len(experts), count, capacity, wide) for experts, _, count, _ in units]
    results = pl.pallas_call(
        functools.partial(expert_kernel, first_expert, wide // 2, units),
        out_shape=[jax.ShapeDtypeStruct(shape, BF16) for part in parts for shape in (part, part, (2, *part))]
        + [jax.ShapeDtypeStruct((rows, n), BF16) for n in (width, width, hidden, hidden)] * per,
        in_specs=[VMEM] * (len(here) + len(pieces) + 2),
        out_specs=[VMEM] * (3 * len(units) + 4 * per),
        scratch_shapes=[pltpu.VMEM((4, rows, wide), BF16)] * (2 * per),
        compiler_params=pltpu.CompilerParams(vmem_limit_bytes=16 << 20),
        cost_estimate=pl.CostEstimate(
            flops=8 * per * rows * width * hidden,
            bytes_accessed=4 * per * width * hidden,
            transcendentals=per * rows * hidden,
        ),
        name="experts",
    )(*here, *pieces, first, second)
    shares = [results[3 * unit : 3 * unit + 3] for unit in range(len(units))]
    return shares, results[3 * len(units) :]


def weight_kernel(first_expert, per, *refs):
    saved, rest = refs[: 4 * per], refs[-6:]
    grad_first_hbm, grad_second_hbm, first_buf, second_buf, sems = rest[-5:]
    stores = []
    for p in range(per):
        x, g, act, grad_pre = (ref[...] for ref in saved[4 * p : 4 * p + 4])
        first_buf[p] = lax.dot_general(x, grad_pre, TN, preferred_element_type=F32).astype(BF16)
        stores.append(pltpu.make_async_copy(first_buf.at[p], grad_first_hbm.at[first_expert + p], sems.at[p, 0]))
        stores[-1].start()
        second_buf[p] = lax.dot_general(act, g, TN, preferred_element_type=F32).astype(BF16)
        stores.append(pltpu.make_async_copy(second_buf.at[p], grad_second_hbm.at[first_expert + p], sems.at[p, 1]))
        stores[-1].start()
    for store in stores:
        store.wait()


def weight_grads(chunk, saved, weight_in, weight_out, grads):
    per = len(saved) // 4
    rows, width = saved[0].shape
    units = weight_in.shape[2]
    count = 4 * per
    return pl.pallas_call(
        functools.partial(weight_kernel, chunk * per, per),
        out_shape=[jax.ShapeDtypeStruct(array.shape, BF16) for array in (weight_in, weight_out)],
        in_specs=[VMEM] * count + [HBM] * len(grads),
        out_specs=[HBM] * 2,
        scratch_shapes=[pltpu.VMEM((per, width, units), BF16), pltpu.VMEM((per, units, width), BF16)]
        + [pltpu.SemaphoreType.DMA((per, 2))],
        input_output_aliases={count: 0, count + 1: 1} if grads else {},
        compiler_params=pltpu.CompilerParams(vmem_limit_bytes=20 << 20),
        cost_estimate=pl.CostEstimate(
            flops=4 * per * rows * width * units, bytes_accessed=4 * per * width * units, transcendentals=0
        ),
        name="weight_grads",
    )(*saved, *grads)


def sum_kernel(picks, *refs):
    terms, outs = refs[: -len(picks)], refs[-len(picks) :]
    for out, parts in zip(outs, picks):
        for half, (term, *sources) in enumerate(parts):
            own, side, passed = terms[3 * term : 3 * term + 3]
            per = own.shape[0]
            for other_core, source in enumerate(sources):
                total = own[:, source].astype(F32) + side[0, :, source].astype(F32) + passed[:, source].astype(F32)
                out[other_core, half * per : (half + 1) * per] = total.astype(BF16)


def sum_rows(terms, picks):
    per, _, capacity, wide = terms[0][0].shape
    return pl.pallas_call(
        functools.partial(sum_kernel, picks),
        out_shape=[jax.ShapeDtypeStruct((2, len(parts) * per, capacity, wide), BF16) for parts in picks],
        in_specs=[VMEM] * (3 * len(terms)),
        out_specs=[VMEM] * len(picks),
        compiler_params=pltpu.CompilerParams(vmem_limit_bytes=8 << 20),
        name="sum_rows",
    )(*[rows for three in terms for rows in three])


def combine_kernel(capacity, exp_dev, picks, place_ref, gate_ref, *refs):
    ins, (out_ref, grad_ref) = refs[:-2], refs[-2:]
    me = lax.axis_index("expert")
    wide = ins[0].shape[-1]
    place = place_ref[...]
    rows, hot = [], []
    for array, index, offset, first_expert in picks:
        rows.append(ins[array][index].reshape(-1, wide))
        first = (me ^ offset) * (exp_dev * capacity) + first_expert * capacity
        hot.append(one_hot(place, first, rows[-1].shape[0]))
    total = lax.dot_general(jnp.concatenate(rows, axis=0), jnp.concatenate(hot, axis=0), TN, preferred_element_type=F32)
    features = out_ref.shape[0]
    out_ref[...] = (gate_ref[...] * total[:features]).astype(BF16)
    grad_ref[...] = total[features:].astype(BF16)


def combine(place, gate, returned, picks, features, exp_dev, capacity):
    count = place.shape[1]
    return pl.pallas_call(
        functools.partial(combine_kernel, capacity, exp_dev, picks),
        out_shape=[jax.ShapeDtypeStruct((features, count), BF16)] * 2,
        in_specs=[VMEM] * (2 + len(returned)),
        out_specs=[VMEM] * 2,
        compiler_params=pltpu.CompilerParams(vmem_limit_bytes=24 << 20),
        name="combine",
    )(place, gate, *returned)


def swap(value, axis, bits):
    size = lax.axis_size(axis)
    return lax.ppermute(value, axis, [(i, i ^ bits) for i in range(size)])


def along_z(buffers):
    direct = [buffers[0]] + [None] * (len(buffers) - 1)
    for dz in reversed(range(1, len(buffers))):
        direct[dz] = swap(buffers[dz], "expert", 2 * dz)
    return direct


def between_cores(direct, *earlier):
    return swap(jnp.stack([rows[1] for rows in after(direct, *earlier)]), "expert", 1)


def after(values, *earlier):
    return lax.optimization_barrier((values, earlier))[0]


def local(tokens, routes, gate_value, weight_in, weight_out, cotangent):
    owners = lax.axis_size("expert")
    exp_dev = weight_in.shape[0]
    count, features = tokens.shape
    capacity = 2 * count // (owners * exp_dev)
    place, gate, buffers = dispatch(
        routes.reshape(1, count), gate_value.reshape(1, count), tokens.T, cotangent.T, owners, exp_dev, capacity
    )
    first, second = load(weight_in, weight_out)
    same, other = buffers[0]
    here = jnp.stack([same, swap(other, "expert", 1)])
    here = [here] + [swap(here, "hidden", bits) for bits in (1, 2, 3)]
    direct = along_z(buffers)[1:]
    rows = pack(direct, between_cores(direct, first, second, *here[1:]))
    per = exp_dev // CHUNKS
    own, near, far = [rows[per * c : per * (c + 1)] for c in range(CHUNKS)], [], []
    for c in range(CHUNKS):
        near.append([swap(rows, "hidden", way[0]) for rows, way in zip(own[c], WAYS)])
    for c in range(CHUNKS):
        pairs = list(zip(own[c], near[c]))
        pairs[1] = after(pairs[1], near)
        pairs = [jnp.stack(pair) for pair in pairs]
        far.append([swap(pair, "hidden", way[1]) for pair, way in zip(pairs, WAYS)])
    parts, saved = [], []
    for c in range(CHUNKS):
        pieces = [piece for three in zip(own[c], near[c], far[c]) for piece in three]
        part, save = run_experts(per * c, here, pieces, first, second, UNITS[c])
        parts.append(part)
        saved.append(save)

    def first_sum(c, unit):
        mine, other, pair = parts[c][unit]
        landed = swap(pair, "hidden", UNITS[c][unit][-1][0])
        return mine, landed, (other.astype(F32) + landed[1].astype(F32)).astype(BF16)

    def second_sum(c, unit, three, *earlier):
        mine, landed, both = three
        return mine, landed, swap(after(both, *earlier), "hidden", UNITS[c][unit][-1][1])

    far = [[first_sum(c, unit) for unit in range(len(FAR))] for c in range(CHUNKS)]
    near = [first_sum(c, len(FAR)) for c in range(CHUNKS)]
    distant, afloat = [], []
    for c in range(CHUNKS):
        terms = [second_sum(c, unit, three) for unit, three in enumerate(far[c])]
        distant.append(sum_rows(terms, [[(0, 0, 1), (1, 0, 1)], [(0, 2, 3), (1, 2, 3)]]))
        afloat.append([swap(rows, "expert", 2 * dz) for dz, rows in zip((2, 3), distant[c])])
    grads = weight_grads(0, saved[0], weight_in, weight_out, [])
    terms = [second_sum(c, len(FAR), three, grads, distant, afloat[0]) for c, three in enumerate(near)]
    beside = sum_rows(terms, [[(0, 0, 1), (1, 0, 1)], [(0, 2, 3), (1, 2, 3)]])
    grads = weight_grads(1, after(saved[1], beside), weight_in, weight_out, grads)
    returned, picks = [], []

    def home(first_expert, offsets, direct):
        for j, dz in enumerate(offsets):
            picks.append((len(returned) + j, (0,), 2 * dz, first_expert))
            picks.append((len(returned) + len(offsets), (j,), 2 * dz + 1, first_expert))
        returned.extend([*direct, between_cores(direct, grads)])

    for c in range(CHUNKS):
        home(per * c, (2, 3), afloat[c])
    home(0, (0, 1), [beside[0], swap(beside[1], "expert", 2)])
    layer_out, grad_tokens = combine(place, gate, returned, picks, features, exp_dev, capacity)
    return layer_out.T, grad_tokens.T, grads[0], grads[1]


def solution(mesh):
    in_specs = (
        P("expert", "hidden"),
        P("expert", None),
        P("expert", None),
        P("expert", None, "hidden"),
        P("expert", "hidden", None),
        P("expert", "hidden"),
    )
    out_specs = (
        P("expert", "hidden"),
        P("expert", "hidden"),
        P("expert", None, "hidden"),
        P("expert", "hidden", None),
    )

    def whole(*args):
        wide = 2 * args[0].shape[1] // mesh.shape["hidden"]
        capacity = 2 * args[0].shape[0] // args[3].shape[0]
        four = mesh.shape["hidden"] == 4 and args[3].shape[0] == 4 * mesh.shape["expert"]
        fits = four and mesh.shape["expert"] == 8 and wide % 128 == 0 and capacity % 16 == 0
        body = local if fits else general
        return jax.shard_map(body, mesh=mesh, in_specs=in_specs, out_specs=out_specs, check_vma=False)(*args)

    return whole
```

```python
import functools
import jax
import jax.numpy as jnp
from jax import lax
from jax.experimental import pallas as pl
from jax.experimental.pallas import tpu as pltpu
from jax.sharding import PartitionSpec as P

CHUNKS = 2
BF16 = jnp.bfloat16
F32 = jnp.float32


def gelu_tanh(values):
    return jax.nn.gelu(values, approximate=True)


def local_places(routes, experts, capacity):
    chosen = routes[:, 0]
    matches = (chosen[:, None] == jnp.arange(experts, dtype=jnp.int32)[None, :]).astype(jnp.int32)
    before = jnp.cumsum(matches, axis=0) - matches
    return chosen * capacity + jnp.sum(before * matches, axis=1)


def general(tokens, routes, gate_value, weight_in, weight_out, cotangent):
    owners = lax.axis_size("expert")
    blocks = lax.axis_size("hidden")
    exp_dev = weight_in.shape[0]
    experts = owners * exp_dev
    capacity = max(2, 2 * tokens.shape[0] // experts)
    slot_count = experts * capacity
    features = tokens.shape[1]
    full_width = weight_out.shape[2]
    units = weight_in.shape[2]
    line = exp_dev * capacity * features
    placed = local_places(routes, experts, capacity)
    scaled = (gate_value * cotangent.astype(F32)).astype(BF16)
    first_four = weight_in.reshape(exp_dev, blocks, features, units)
    second_four = weight_out.reshape(exp_dev, units, blocks, features)

    def to_slots(values):
        filled = jnp.zeros((slot_count, features), BF16).at[placed].set(values)
        return filled.reshape(owners, line)

    def rows_of(values):
        arrived = lax.all_to_all(to_slots(values), "expert", split_axis=0, concat_axis=0, tiled=True)
        gathered = lax.all_gather(arrived[None], "hidden", axis=0, tiled=True)
        return gathered.reshape(blocks, owners, exp_dev, capacity, features)

    def back(part):
        flat = part.reshape(blocks, owners, line).astype(BF16)
        total = lax.psum_scatter(flat, "hidden", scatter_dimension=0, tiled=True)
        total = total.astype(F32)[0].astype(BF16)
        returned = lax.all_to_all(total, "expert", split_axis=0, concat_axis=0, tiled=True)
        return returned.reshape(slot_count, features)[placed]

    rows_x = rows_of(tokens)
    rows_g = rows_of(scaled)
    preact = jnp.einsum("nsecf,enfh->sech", rows_x, first_four, preferred_element_type=F32)
    activation, pullback = jax.vjp(gelu_tanh, preact)
    hidden_act = activation.astype(BF16)
    out_part = jnp.einsum("sech,ehnf->nsecf", hidden_act, second_four, preferred_element_type=F32)
    grad_hidden = jnp.einsum("nsecf,ehnf->sech", rows_g, second_four, preferred_element_type=F32)
    grad_pre = pullback(grad_hidden)[0].astype(BF16)
    grad_part = jnp.einsum("sech,enfh->nsecf", grad_pre, first_four, preferred_element_type=F32)
    grad_weight_in = jnp.einsum("nsecf,sech->enfh", rows_x, grad_pre, preferred_element_type=F32)
    grad_weight_out = jnp.einsum("sech,nsecf->ehnf", hidden_act, rows_g, preferred_element_type=F32)
    layer_out = (gate_value * back(out_part).astype(F32)).astype(BF16)
    return (
        layer_out,
        back(grad_part),
        grad_weight_in.astype(BF16).reshape(exp_dev, full_width, units),
        grad_weight_out.astype(BF16).reshape(exp_dev, units, full_width),
    )


NT = (((1,), (1,)), ((), ()))
TN = (((0,), (0,)), ((), ()))
VMEM = pl.BlockSpec(memory_space=pltpu.VMEM)
HBM = pl.BlockSpec(memory_space=pltpu.HBM)
WAYS = ((1, 2), (2, 1))
NEAR, FAR = (0, 4, (2, 1)), (4, 4, (1, 2))
HERE, BESIDE = (0, 2, (1, 2)), (2, 2, (2, 1))
UNITS = ((NEAR, FAR), (HERE, BESIDE, FAR))


def one_hot(place, first, count):
    rows = lax.broadcasted_iota(jnp.int32, (count, place.shape[1]), 0)
    return jnp.where(rows == place - first, 1.0, 0.0).astype(BF16)


def dispatch_kernel(exp_dev, capacity, *refs):
    ins, place_ref, gate_ref, rest = refs[:4], refs[4], refs[5], refs[6:]
    buffers, (routes_buf, tok_buf, cot_buf, sems) = rest[:-4], rest[-4:]
    loads = [
        pltpu.make_async_copy(source, target, sems.at[i])
        for i, (source, target) in enumerate(zip(ins, (routes_buf, gate_ref, tok_buf, cot_buf)))
    ]
    for load in loads:
        load.start()
    tokens = routes_buf.shape[1]
    experts = 2 * len(buffers) * exp_dev
    line = exp_dev * capacity
    me = lax.axis_index("expert")
    earlier = lax.broadcasted_iota(jnp.int32, (tokens, tokens), 0) < lax.broadcasted_iota(
        jnp.int32, (tokens, tokens), 1
    )
    earlier = jnp.where(earlier, 1.0, 0.0).astype(BF16)
    loads[0].wait()
    chosen = routes_buf[...]
    matches = lax.broadcasted_iota(jnp.int32, (experts, tokens), 0) == chosen
    before = jnp.dot(jnp.where(matches, 1.0, 0.0).astype(BF16), earlier, preferred_element_type=F32)
    within = jnp.sum(jnp.where(matches, before, 0.0), axis=0, keepdims=True).astype(jnp.int32)
    place = chosen * capacity + within
    place_ref[...] = place
    for load in loads[1:]:
        load.wait()
    scaled = (gate_ref[...] * cot_buf[...].astype(F32)).astype(BF16)
    both = jnp.concatenate([tok_buf[...], scaled], axis=0)
    for dz, ref in enumerate(buffers):
        firsts = [(me ^ offset) * line for offset in (2 * dz, 2 * dz + 1)]
        hot = jnp.concatenate([one_hot(place, first, line) for first in firsts], axis=0)
        filled = lax.dot_general(hot, both, NT, preferred_element_type=F32).astype(BF16)
        ref[...] = filled.reshape(ref.shape)


def in_hbm(*arrays):
    return [pltpu.with_memory_space_constraint(array, pltpu.HBM) for array in arrays]


def dispatch(routes, gate, tokens, cotangent, owners, exp_dev, capacity):
    features, count = tokens.shape
    buffer = jax.ShapeDtypeStruct((2, exp_dev, capacity, 2 * features), BF16)
    buffers = owners // 2
    place, gate, *buffers = pl.pallas_call(
        functools.partial(dispatch_kernel, exp_dev, capacity),
        out_shape=[jax.ShapeDtypeStruct((1, count), jnp.int32), jax.ShapeDtypeStruct((1, count), F32)]
        + [buffer] * buffers,
        in_specs=[HBM] * 4,
        out_specs=[VMEM] * (2 + buffers),
        scratch_shapes=[pltpu.VMEM((1, count), jnp.int32)]
        + [pltpu.VMEM((features, count), BF16)] * 2
        + [pltpu.SemaphoreType.DMA((4,))],
        compiler_params=pltpu.CompilerParams(vmem_limit_bytes=24 << 20),
        name="dispatch",
    )(*in_hbm(routes, gate, tokens, cotangent))
    return place, gate, buffers


def source_of(dz, other_core):
    return 2 * dz + other_core


def pack_kernel(*refs):
    per = refs[0].shape[1]
    direct, passed, outs = refs[: -per - 1], refs[-per - 1], refs[-per:]
    for p, out in enumerate(outs):
        for i, ref in enumerate(direct):
            out[source_of(i, 0)] = ref[0, p]
            out[source_of(i, 1)] = passed[i, p]


def pack(direct, passed):
    _, per, capacity, wide = direct[0].shape
    return pl.pallas_call(
        pack_kernel,
        out_shape=[jax.ShapeDtypeStruct((2 * len(direct), capacity, wide), BF16)] * per,
        in_specs=[VMEM] * (1 + len(direct)),
        out_specs=[VMEM] * per,
        compiler_params=pltpu.CompilerParams(vmem_limit_bytes=8 << 20),
        name="pack",
    )(*direct, passed)


def load_kernel(*refs):
    count = (len(refs) - 1) // 2
    sems = refs[-1]
    loads = [pltpu.make_async_copy(refs[i], refs[count + i], sems.at[i]) for i in range(count)]
    for load in loads:
        load.start()
    for load in loads:
        load.wait()


def load(*arrays):
    return pl.pallas_call(
        load_kernel,
        out_shape=[jax.ShapeDtypeStruct(array.shape, array.dtype) for array in arrays],
        in_specs=[HBM] * len(arrays),
        out_specs=[VMEM] * len(arrays),
        scratch_shapes=[pltpu.SemaphoreType.DMA((len(arrays),))],
        compiler_params=pltpu.CompilerParams(vmem_limit_bytes=16 << 20),
        name="load",
    )(*in_hbm(*arrays))


def expert_kernel(first_expert, features, units, *refs):
    per = len(WAYS)
    here, refs = refs[:4], refs[4:]
    ins, (first_ref, second_ref), refs = refs[: 3 * per], refs[3 * per : 3 * per + 2], refs[3 * per + 2 :]
    outs, saved, scratch = refs[: 3 * len(units)], refs[3 * len(units) : -2 * per], refs[-2 * per :]
    mine = lax.axis_index("hidden")
    rows = scratch[0].shape[1]
    for p, (near, far) in enumerate(WAYS):
        s_in, s_out = scratch[2 * p : 2 * p + 2]
        own_ref, near_ref, far_ref = ins[3 * p : 3 * p + 3]
        away = own_ref.shape[0] * own_ref.shape[1]
        for bits, ref in enumerate(here):
            s_in[mine ^ bits, : rows - away] = ref[:, first_expert + p].reshape(rows - away, 2 * features)
        s_in[mine, rows - away :] = own_ref[...].reshape(away, 2 * features)
        s_in[mine ^ near, rows - away :] = near_ref[...].reshape(away, 2 * features)
        s_in[mine ^ far, rows - away :] = far_ref[0].reshape(away, 2 * features)
        s_in[mine ^ 3, rows - away :] = far_ref[1].reshape(away, 2 * features)
        x = jnp.concatenate([s_in[j, :, :features] for j in range(4)], axis=1)
        g = jnp.concatenate([s_in[j, :, features:] for j in range(4)], axis=1)
        first, second = first_ref[first_expert + p], second_ref[first_expert + p]
        v = jnp.dot(x, first, preferred_element_type=F32)
        grad_hidden = lax.dot_general(g, second, NT, preferred_element_type=F32)
        root = 0.7978845608028654
        square = v * v
        t = jnp.tanh(root * (v + 0.044715 * (v * square)))
        act = (0.5 * v * (1.0 + t)).astype(BF16)
        slope = 0.5 * (1.0 + t) + 0.5 * v * (1.0 - t * t) * (root * (1.0 + 3 * 0.044715 * square))
        grad_pre = (grad_hidden * slope).astype(BF16)
        out = jnp.dot(act, second, preferred_element_type=F32).astype(BF16)
        grad = lax.dot_general(grad_pre, first, NT, preferred_element_type=F32).astype(BF16)
        for j in range(4):
            lanes = slice(j * features, (j + 1) * features)
            s_out[mine ^ j] = jnp.concatenate([out[:, lanes], grad[:, lanes]], axis=1)
        for unit, (source, count, (near, far)) in enumerate(units):
            own_ref, far_ref, near_ref = outs[3 * unit : 3 * unit + 3]
            capacity = own_ref.shape[2]
            span = slice(source * capacity, (source + count) * capacity)
            own_ref[p] = s_out[0, span].reshape(own_ref.shape[1:])
            far_ref[p] = s_out[far, span].reshape(own_ref.shape[1:])
            near_ref[0, p] = s_out[near, span].reshape(own_ref.shape[1:])
            near_ref[1, p] = s_out[3, span].reshape(own_ref.shape[1:])
        for ref, value in zip(saved[4 * p : 4 * p + 4], (x, g, act, grad_pre)):
            ref[...] = value


def run_experts(first_expert, here, pieces, first, second, units):
    away, capacity, wide = pieces[0].shape
    sources = away + here[0].shape[0]
    _, width, hidden = first.shape
    rows = sources * capacity
    per = len(WAYS)
    parts = [(per, count, capacity, wide) for _, count, _ in units]
    results = pl.pallas_call(
        functools.partial(expert_kernel, first_expert, wide // 2, units),
        out_shape=[jax.ShapeDtypeStruct(shape, BF16) for part in parts for shape in (part, part, (2, *part))]
        + [jax.ShapeDtypeStruct((rows, n), BF16) for n in (width, width, hidden, hidden)] * per,
        in_specs=[VMEM] * (len(here) + len(pieces) + 2),
        out_specs=[VMEM] * (3 * len(units) + 4 * per),
        scratch_shapes=[pltpu.VMEM((4, rows, wide), BF16)] * (2 * per),
        compiler_params=pltpu.CompilerParams(vmem_limit_bytes=16 << 20),
        cost_estimate=pl.CostEstimate(
            flops=8 * per * rows * width * hidden,
            bytes_accessed=4 * per * width * hidden,
            transcendentals=per * rows * hidden,
        ),
        name="experts",
    )(*here, *pieces, first, second)
    shares = [results[3 * unit : 3 * unit + 3] for unit in range(len(units))]
    return shares, results[3 * len(units) :]


def weight_kernel(first_expert, per, *refs):
    saved, rest = refs[: 4 * per], refs[-6:]
    grad_first_hbm, grad_second_hbm, first_buf, second_buf, sems = rest[-5:]
    stores = []
    for p in range(per):
        x, g, act, grad_pre = (ref[...] for ref in saved[4 * p : 4 * p + 4])
        first_buf[p] = lax.dot_general(x, grad_pre, TN, preferred_element_type=F32).astype(BF16)
        stores.append(pltpu.make_async_copy(first_buf.at[p], grad_first_hbm.at[first_expert + p], sems.at[p, 0]))
        stores[-1].start()
        second_buf[p] = lax.dot_general(act, g, TN, preferred_element_type=F32).astype(BF16)
        stores.append(pltpu.make_async_copy(second_buf.at[p], grad_second_hbm.at[first_expert + p], sems.at[p, 1]))
        stores[-1].start()
    for store in stores:
        store.wait()


def weight_grads(chunk, saved, weight_in, weight_out, grads):
    per = len(saved) // 4
    rows, width = saved[0].shape
    units = weight_in.shape[2]
    count = 4 * per
    return pl.pallas_call(
        functools.partial(weight_kernel, chunk * per, per),
        out_shape=[jax.ShapeDtypeStruct(array.shape, BF16) for array in (weight_in, weight_out)],
        in_specs=[VMEM] * count + [HBM] * len(grads),
        out_specs=[HBM] * 2,
        scratch_shapes=[pltpu.VMEM((per, width, units), BF16), pltpu.VMEM((per, units, width), BF16)]
        + [pltpu.SemaphoreType.DMA((per, 2))],
        input_output_aliases={count: 0, count + 1: 1} if grads else {},
        compiler_params=pltpu.CompilerParams(vmem_limit_bytes=20 << 20),
        cost_estimate=pl.CostEstimate(
            flops=4 * per * rows * width * units, bytes_accessed=4 * per * width * units, transcendentals=0
        ),
        name="weight_grads",
    )(*saved, *grads)


def sum_kernel(picks, *refs):
    terms, outs = refs[: -len(picks)], refs[-len(picks) :]
    for out, parts in zip(outs, picks):
        for half, (term, *sources) in enumerate(parts):
            own, side, passed = terms[3 * term : 3 * term + 3]
            per = own.shape[0]
            for other_core, source in enumerate(sources):
                total = own[:, source].astype(F32) + side[0, :, source].astype(F32) + passed[:, source].astype(F32)
                out[other_core, half * per : (half + 1) * per] = total.astype(BF16)


def sum_rows(terms, picks):
    per, _, capacity, wide = terms[0][0].shape
    return pl.pallas_call(
        functools.partial(sum_kernel, picks),
        out_shape=[jax.ShapeDtypeStruct((2, len(parts) * per, capacity, wide), BF16) for parts in picks],
        in_specs=[VMEM] * (3 * len(terms)),
        out_specs=[VMEM] * len(picks),
        compiler_params=pltpu.CompilerParams(vmem_limit_bytes=8 << 20),
        name="sum_rows",
    )(*[rows for three in terms for rows in three])


def combine_kernel(capacity, exp_dev, picks, place_ref, gate_ref, *refs):
    ins, (out_ref, grad_ref) = refs[:-2], refs[-2:]
    me = lax.axis_index("expert")
    wide = ins[0].shape[-1]
    place = place_ref[...]
    rows, hot = [], []
    for array, index, offset, first_expert in picks:
        rows.append(ins[array][index].reshape(-1, wide))
        first = (me ^ offset) * (exp_dev * capacity) + first_expert * capacity
        hot.append(one_hot(place, first, rows[-1].shape[0]))
    total = lax.dot_general(jnp.concatenate(rows, axis=0), jnp.concatenate(hot, axis=0), TN, preferred_element_type=F32)
    features = out_ref.shape[0]
    out_ref[...] = (gate_ref[...] * total[:features]).astype(BF16)
    grad_ref[...] = total[features:].astype(BF16)


def combine(place, gate, returned, picks, features, exp_dev, capacity):
    count = place.shape[1]
    return pl.pallas_call(
        functools.partial(combine_kernel, capacity, exp_dev, picks),
        out_shape=[jax.ShapeDtypeStruct((features, count), BF16)] * 2,
        in_specs=[VMEM] * (2 + len(returned)),
        out_specs=[VMEM] * 2,
        compiler_params=pltpu.CompilerParams(vmem_limit_bytes=24 << 20),
        name="combine",
    )(place, gate, *returned)


def swap(value, axis, bits):
    size = lax.axis_size(axis)
    return lax.ppermute(value, axis, [(i, i ^ bits) for i in range(size)])


def along_z(buffers):
    direct = [buffers[0]] + [None] * (len(buffers) - 1)
    for dz in reversed(range(1, len(buffers))):
        direct[dz] = swap(buffers[dz], "expert", 2 * dz)
    return direct


def between_cores(direct, *earlier):
    return swap(jnp.stack([rows[1] for rows in after(direct, *earlier)]), "expert", 1)


def after(values, *earlier):
    return lax.optimization_barrier((values, earlier))[0]


def local(tokens, routes, gate_value, weight_in, weight_out, cotangent):
    owners = lax.axis_size("expert")
    exp_dev = weight_in.shape[0]
    count, features = tokens.shape
    capacity = 2 * count // (owners * exp_dev)
    place, gate, buffers = dispatch(
        routes.reshape(1, count), gate_value.reshape(1, count), tokens.T, cotangent.T, owners, exp_dev, capacity
    )
    first, second = load(weight_in, weight_out)
    same, other = buffers[0]
    here = jnp.stack([same, swap(other, "expert", 1)])
    here = [here] + [swap(here, "hidden", bits) for bits in (1, 2, 3)]
    direct = along_z(buffers)[1:]
    rows = pack(direct, between_cores(direct, first, second, *here[1:]))
    per = exp_dev // CHUNKS
    own, near, far = [rows[per * c : per * (c + 1)] for c in range(CHUNKS)], [], []
    for c in range(CHUNKS):
        near.append([swap(rows, "hidden", way[0]) for rows, way in zip(own[c], WAYS)])
    for c in range(CHUNKS):
        pairs = list(zip(own[c], near[c]))
        pairs[1] = after(pairs[1], near)
        pairs = [jnp.stack(pair) for pair in pairs]
        far.append([swap(pair, "hidden", way[1]) for pair, way in zip(pairs, WAYS)])
    parts, saved = [], []
    for c in range(CHUNKS):
        pieces = [piece for three in zip(own[c], near[c], far[c]) for piece in three]
        part, save = run_experts(per * c, here, pieces, first, second, UNITS[c])
        parts.append(part)
        saved.append(save)

    def first_sum(c, unit, earlier=(), ahead=()):
        mine, other, pair = parts[c][UNITS[c].index(unit)]
        landed = after(swap(after(pair, earlier), "hidden", unit[2][0]), ahead)
        return mine, landed, (other.astype(F32) + landed[1].astype(F32)).astype(BF16)

    def second_sum(three, unit, *earlier):
        mine, landed, both = three
        return mine, landed, swap(after(both, *earlier), "hidden", unit[2][1])

    def chip_pair(rows):
        return [swap(part, "expert", 2 * dz) for dz, part in zip((2, 3), rows)]

    near, far = first_sum(0, NEAR), [first_sum(0, FAR)]
    far.append(first_sum(1, FAR, far[0][1]))
    beside = first_sum(1, BESIDE, far[0][1])
    each_way = [[(0, 0, 1)], [(0, 2, 3)]]
    distant = [sum_rows([second_sum(three, FAR)], each_way) for three in far]
    afloat = [chip_pair(rows) for rows in distant]
    here = first_sum(1, HERE, far[1][1], distant[1])
    grads = weight_grads(0, after(saved[0], distant[0]), weight_in, weight_out, [])
    mine, *terms = second_sum(near, NEAR)
    near = (after(mine, grads, distant[1]), *terms)
    (next_door,) = sum_rows([near, second_sum(beside, BESIDE, distant[0])], [[(0, 2, 3), (1, 0, 1)]])
    grads = weight_grads(1, after(saved[1], distant[0]), weight_in, weight_out, grads)
    mine, *terms = second_sum(here, HERE, afloat[0])
    here = (after(mine, grads, afloat[1], next_door), *terms)
    (at_home,) = sum_rows([near, here], [[(0, 0, 1), (1, 0, 1)]])
    returned, picks = [], []

    def home(first_expert, offsets, direct):
        for j, dz in enumerate(offsets):
            picks.append((len(returned) + j, (0,), 2 * dz, first_expert))
            picks.append((len(returned) + len(offsets), (j,), 2 * dz + 1, first_expert))
        returned.extend([*direct, between_cores(direct, at_home)])

    for c in range(CHUNKS):
        home(per * c, (2, 3), afloat[c])
    home(0, (1,), [swap(next_door, "expert", 2)])
    home(0, (0,), [at_home])
    layer_out, grad_tokens = combine(place, gate, returned, picks, features, exp_dev, capacity)
    return layer_out.T, grad_tokens.T, grads[0], grads[1]


def solution(mesh):
    in_specs = (
        P("expert", "hidden"),
        P("expert", None),
        P("expert", None),
        P("expert", None, "hidden"),
        P("expert", "hidden", None),
        P("expert", "hidden"),
    )
    out_specs = (
        P("expert", "hidden"),
        P("expert", "hidden"),
        P("expert", None, "hidden"),
        P("expert", "hidden", None),
    )

    def whole(*args):
        wide = 2 * args[0].shape[1] // mesh.shape["hidden"]
        capacity = 2 * args[0].shape[0] // args[3].shape[0]
        four = mesh.shape["hidden"] == 4 and args[3].shape[0] == 4 * mesh.shape["expert"]
        fits = four and mesh.shape["expert"] == 8 and wide % 128 == 0 and capacity % 16 == 0
        body = local if fits else general
        return jax.shard_map(body, mesh=mesh, in_specs=in_specs, out_specs=out_specs, check_vma=False)(*args)

    return whole
```

```python
import functools
import jax
import jax.numpy as jnp
from jax import lax
from jax.experimental import pallas as pl
from jax.experimental.pallas import tpu as pltpu
from jax.sharding import PartitionSpec as P

CHUNKS = 2
BF16 = jnp.bfloat16
F32 = jnp.float32


def gelu_tanh(values):
    return jax.nn.gelu(values, approximate=True)


def local_places(routes, experts, capacity):
    chosen = routes[:, 0]
    matches = (chosen[:, None] == jnp.arange(experts, dtype=jnp.int32)[None, :]).astype(jnp.int32)
    before = jnp.cumsum(matches, axis=0) - matches
    return chosen * capacity + jnp.sum(before * matches, axis=1)


def general(tokens, routes, gate_value, weight_in, weight_out, cotangent):
    owners = lax.axis_size("expert")
    blocks = lax.axis_size("hidden")
    exp_dev = weight_in.shape[0]
    experts = owners * exp_dev
    capacity = max(2, 2 * tokens.shape[0] // experts)
    slot_count = experts * capacity
    features = tokens.shape[1]
    full_width = weight_out.shape[2]
    units = weight_in.shape[2]
    line = exp_dev * capacity * features
    placed = local_places(routes, experts, capacity)
    scaled = (gate_value * cotangent.astype(F32)).astype(BF16)
    first_four = weight_in.reshape(exp_dev, blocks, features, units)
    second_four = weight_out.reshape(exp_dev, units, blocks, features)

    def to_slots(values):
        filled = jnp.zeros((slot_count, features), BF16).at[placed].set(values)
        return filled.reshape(owners, line)

    def rows_of(values):
        arrived = lax.all_to_all(to_slots(values), "expert", split_axis=0, concat_axis=0, tiled=True)
        gathered = lax.all_gather(arrived[None], "hidden", axis=0, tiled=True)
        return gathered.reshape(blocks, owners, exp_dev, capacity, features)

    def back(part):
        flat = part.reshape(blocks, owners, line).astype(BF16)
        total = lax.psum_scatter(flat, "hidden", scatter_dimension=0, tiled=True)
        total = total.astype(F32)[0].astype(BF16)
        returned = lax.all_to_all(total, "expert", split_axis=0, concat_axis=0, tiled=True)
        return returned.reshape(slot_count, features)[placed]

    rows_x = rows_of(tokens)
    rows_g = rows_of(scaled)
    preact = jnp.einsum("nsecf,enfh->sech", rows_x, first_four, preferred_element_type=F32)
    activation, pullback = jax.vjp(gelu_tanh, preact)
    hidden_act = activation.astype(BF16)
    out_part = jnp.einsum("sech,ehnf->nsecf", hidden_act, second_four, preferred_element_type=F32)
    grad_hidden = jnp.einsum("nsecf,ehnf->sech", rows_g, second_four, preferred_element_type=F32)
    grad_pre = pullback(grad_hidden)[0].astype(BF16)
    grad_part = jnp.einsum("sech,enfh->nsecf", grad_pre, first_four, preferred_element_type=F32)
    grad_weight_in = jnp.einsum("nsecf,sech->enfh", rows_x, grad_pre, preferred_element_type=F32)
    grad_weight_out = jnp.einsum("sech,nsecf->ehnf", hidden_act, rows_g, preferred_element_type=F32)
    layer_out = (gate_value * back(out_part).astype(F32)).astype(BF16)
    return (
        layer_out,
        back(grad_part),
        grad_weight_in.astype(BF16).reshape(exp_dev, full_width, units),
        grad_weight_out.astype(BF16).reshape(exp_dev, units, full_width),
    )


NT = (((1,), (1,)), ((), ()))
TN = (((0,), (0,)), ((), ()))
VMEM = pl.BlockSpec(memory_space=pltpu.VMEM)
HBM = pl.BlockSpec(memory_space=pltpu.HBM)
WAYS = ((1, 2), (2, 1))
UNITS = ((2, 1), (1, 2))
OFFSETS = ((0, 1), (2, 3))


def one_hot(place, first, count):
    rows = lax.broadcasted_iota(jnp.int32, (count, place.shape[1]), 0)
    return jnp.where(rows == place - first, 1.0, 0.0).astype(BF16)


def dispatch_kernel(exp_dev, capacity, *refs):
    ins, place_ref, gate_ref, rest = refs[:4], refs[4], refs[5], refs[6:]
    buffers, (routes_buf, tok_buf, cot_buf, sems) = rest[:-4], rest[-4:]
    loads = [
        pltpu.make_async_copy(source, target, sems.at[i])
        for i, (source, target) in enumerate(zip(ins, (routes_buf, gate_ref, tok_buf, cot_buf)))
    ]
    for load in loads:
        load.start()
    tokens = routes_buf.shape[1]
    experts = 2 * len(buffers) * exp_dev
    line = exp_dev * capacity
    me = lax.axis_index("expert")
    earlier = lax.broadcasted_iota(jnp.int32, (tokens, tokens), 0) < lax.broadcasted_iota(
        jnp.int32, (tokens, tokens), 1
    )
    earlier = jnp.where(earlier, 1.0, 0.0).astype(BF16)
    loads[0].wait()
    chosen = routes_buf[...]
    matches = lax.broadcasted_iota(jnp.int32, (experts, tokens), 0) == chosen
    before = jnp.dot(jnp.where(matches, 1.0, 0.0).astype(BF16), earlier, preferred_element_type=F32)
    within = jnp.sum(jnp.where(matches, before, 0.0), axis=0, keepdims=True).astype(jnp.int32)
    place = chosen * capacity + within
    place_ref[...] = place
    for load in loads[1:]:
        load.wait()
    scaled = (gate_ref[...] * cot_buf[...].astype(F32)).astype(BF16)
    both = jnp.concatenate([tok_buf[...], scaled], axis=0)
    for dz, ref in enumerate(buffers):
        firsts = [(me ^ offset) * line for offset in (2 * dz, 2 * dz + 1)]
        hot = jnp.concatenate([one_hot(place, first, line) for first in firsts], axis=0)
        filled = lax.dot_general(hot, both, NT, preferred_element_type=F32).astype(BF16)
        ref[...] = filled.reshape(ref.shape)


def in_hbm(*arrays):
    return [pltpu.with_memory_space_constraint(array, pltpu.HBM) for array in arrays]


def dispatch(routes, gate, tokens, cotangent, owners, exp_dev, capacity):
    features, count = tokens.shape
    buffer = jax.ShapeDtypeStruct((2, exp_dev, capacity, 2 * features), BF16)
    buffers = owners // 2
    place, gate, *buffers = pl.pallas_call(
        functools.partial(dispatch_kernel, exp_dev, capacity),
        out_shape=[jax.ShapeDtypeStruct((1, count), jnp.int32), jax.ShapeDtypeStruct((1, count), F32)]
        + [buffer] * buffers,
        in_specs=[HBM] * 4,
        out_specs=[VMEM] * (2 + buffers),
        scratch_shapes=[pltpu.VMEM((1, count), jnp.int32)]
        + [pltpu.VMEM((features, count), BF16)] * 2
        + [pltpu.SemaphoreType.DMA((4,))],
        compiler_params=pltpu.CompilerParams(vmem_limit_bytes=24 << 20),
        name="dispatch",
    )(*in_hbm(routes, gate, tokens, cotangent))
    return place, gate, buffers


def source_of(dz, other_core):
    return 2 * dz + other_core


def pack_kernel(*refs):
    per = refs[0].shape[1]
    direct, passed, outs = refs[: -per - 1], refs[-per - 1], refs[-per:]
    for p, out in enumerate(outs):
        for i, ref in enumerate(direct):
            out[source_of(i, 0)] = ref[0, p]
            out[source_of(i, 1)] = passed[i, p]


def pack(direct, passed):
    _, per, capacity, wide = direct[0].shape
    return pl.pallas_call(
        pack_kernel,
        out_shape=[jax.ShapeDtypeStruct((2 * len(direct), capacity, wide), BF16)] * per,
        in_specs=[VMEM] * (1 + len(direct)),
        out_specs=[VMEM] * per,
        compiler_params=pltpu.CompilerParams(vmem_limit_bytes=8 << 20),
        name="pack",
    )(*direct, passed)


def load_kernel(*refs):
    count = (len(refs) - 1) // 2
    sems = refs[-1]
    loads = [pltpu.make_async_copy(refs[i], refs[count + i], sems.at[i]) for i in range(count)]
    for load in loads:
        load.start()
    for load in loads:
        load.wait()


def load(*arrays):
    return pl.pallas_call(
        load_kernel,
        out_shape=[jax.ShapeDtypeStruct(array.shape, array.dtype) for array in arrays],
        in_specs=[HBM] * len(arrays),
        out_specs=[VMEM] * len(arrays),
        scratch_shapes=[pltpu.SemaphoreType.DMA((len(arrays),))],
        compiler_params=pltpu.CompilerParams(vmem_limit_bytes=16 << 20),
        name="load",
    )(*in_hbm(*arrays))


def expert_kernel(first_expert, features, *refs):
    per = len(WAYS)
    here, refs = refs[:4], refs[4:]
    ins, (first_ref, second_ref), refs = refs[: 3 * per], refs[3 * per : 3 * per + 2], refs[3 * per + 2 :]
    outs, saved, scratch = refs[: 3 * len(UNITS)], refs[3 * len(UNITS) : -2 * per], refs[-2 * per :]
    mine = lax.axis_index("hidden")
    rows = scratch[0].shape[1]
    for p, (near, far) in enumerate(WAYS):
        s_in, s_out = scratch[2 * p : 2 * p + 2]
        own_ref, near_ref, far_ref = ins[3 * p : 3 * p + 3]
        away = own_ref.shape[0] * own_ref.shape[1]
        for bits, ref in enumerate(here):
            s_in[mine ^ bits, : rows - away] = ref[:, first_expert + p].reshape(rows - away, 2 * features)
        s_in[mine, rows - away :] = own_ref[...].reshape(away, 2 * features)
        s_in[mine ^ near, rows - away :] = near_ref[...].reshape(away, 2 * features)
        s_in[mine ^ far, rows - away :] = far_ref[0].reshape(away, 2 * features)
        s_in[mine ^ 3, rows - away :] = far_ref[1].reshape(away, 2 * features)
        x = jnp.concatenate([s_in[j, :, :features] for j in range(4)], axis=1)
        g = jnp.concatenate([s_in[j, :, features:] for j in range(4)], axis=1)
        first, second = first_ref[first_expert + p], second_ref[first_expert + p]
        v = jnp.dot(x, first, preferred_element_type=F32)
        grad_hidden = lax.dot_general(g, second, NT, preferred_element_type=F32)
        root = 0.7978845608028654
        square = v * v
        t = jnp.tanh(root * (v + 0.044715 * (v * square)))
        act = (0.5 * v * (1.0 + t)).astype(BF16)
        slope = 0.5 * (1.0 + t) + 0.5 * v * (1.0 - t * t) * (root * (1.0 + 3 * 0.044715 * square))
        grad_pre = (grad_hidden * slope).astype(BF16)
        out = jnp.dot(act, second, preferred_element_type=F32).astype(BF16)
        grad = lax.dot_general(grad_pre, first, NT, preferred_element_type=F32).astype(BF16)
        for j in range(4):
            lanes = slice(j * features, (j + 1) * features)
            s_out[mine ^ j] = jnp.concatenate([out[:, lanes], grad[:, lanes]], axis=1)
        for group, (near, far) in enumerate(UNITS):
            own_ref, far_ref, near_ref = outs[3 * group : 3 * group + 3]
            span = slice(group * rows // len(UNITS), (group + 1) * rows // len(UNITS))
            own_ref[p] = s_out[0, span].reshape(own_ref.shape[1:])
            far_ref[p] = s_out[far, span].reshape(own_ref.shape[1:])
            near_ref[0, p] = s_out[near, span].reshape(own_ref.shape[1:])
            near_ref[1, p] = s_out[3, span].reshape(own_ref.shape[1:])
        for ref, value in zip(saved[4 * p : 4 * p + 4], (x, g, act, grad_pre)):
            ref[...] = value


def run_experts(first_expert, here, pieces, first, second):
    away, capacity, wide = pieces[0].shape
    sources = away + here[0].shape[0]
    _, width, units = first.shape
    rows = sources * capacity
    per = len(WAYS)
    part = (per, sources // len(UNITS), capacity, wide)
    results = pl.pallas_call(
        functools.partial(expert_kernel, first_expert, wide // 2),
        out_shape=[jax.ShapeDtypeStruct(shape, BF16) for shape in (part, part, (2, *part))] * len(UNITS)
        + [jax.ShapeDtypeStruct((rows, n), BF16) for n in (width, width, units, units)] * per,
        in_specs=[VMEM] * (len(here) + len(pieces) + 2),
        out_specs=[VMEM] * (3 * len(UNITS) + 4 * per),
        scratch_shapes=[pltpu.VMEM((4, rows, wide), BF16)] * (2 * per),
        compiler_params=pltpu.CompilerParams(vmem_limit_bytes=16 << 20),
        cost_estimate=pl.CostEstimate(
            flops=8 * per * rows * width * units,
            bytes_accessed=4 * per * width * units,
            transcendentals=per * rows * units,
        ),
        name="experts",
    )(*here, *pieces, first, second)
    parts = [results[3 * group : 3 * group + 3] for group in range(len(UNITS))]
    return parts, results[3 * len(UNITS) :]


def weight_kernel(first_expert, per, *refs):
    saved, rest = refs[: 4 * per], refs[-6:]
    grad_first_hbm, grad_second_hbm, first_buf, second_buf, sems = rest[-5:]
    stores = []
    for p in range(per):
        x, g, act, grad_pre = (ref[...] for ref in saved[4 * p : 4 * p + 4])
        first_buf[p] = lax.dot_general(x, grad_pre, TN, preferred_element_type=F32).astype(BF16)
        stores.append(pltpu.make_async_copy(first_buf.at[p], grad_first_hbm.at[first_expert + p], sems.at[p, 0]))
        stores[-1].start()
        second_buf[p] = lax.dot_general(act, g, TN, preferred_element_type=F32).astype(BF16)
        stores.append(pltpu.make_async_copy(second_buf.at[p], grad_second_hbm.at[first_expert + p], sems.at[p, 1]))
        stores[-1].start()
    for store in stores:
        store.wait()


def weight_grads(chunk, saved, weight_in, weight_out, grads):
    per = len(saved) // 4
    rows, width = saved[0].shape
    units = weight_in.shape[2]
    count = 4 * per
    return pl.pallas_call(
        functools.partial(weight_kernel, chunk * per, per),
        out_shape=[jax.ShapeDtypeStruct(array.shape, BF16) for array in (weight_in, weight_out)],
        in_specs=[VMEM] * count + [HBM] * len(grads),
        out_specs=[HBM] * 2,
        scratch_shapes=[pltpu.VMEM((per, width, units), BF16), pltpu.VMEM((per, units, width), BF16)]
        + [pltpu.SemaphoreType.DMA((per, 2))],
        input_output_aliases={count: 0, count + 1: 1} if grads else {},
        compiler_params=pltpu.CompilerParams(vmem_limit_bytes=20 << 20),
        cost_estimate=pl.CostEstimate(
            flops=4 * per * rows * width * units, bytes_accessed=4 * per * width * units, transcendentals=0
        ),
        name="weight_grads",
    )(*saved, *grads)


def sum_kernel(*refs):
    halves = (len(refs) - 2) // 3
    terms, outs = refs[: 3 * halves], refs[3 * halves :]
    for half in range(halves):
        own, side, passed = terms[3 * half : 3 * half + 3]
        total = own[...].astype(F32) + side[0].astype(F32) + passed[...].astype(F32)
        total = total.astype(BF16)
        for p in range(total.shape[0]):
            for dz, out in enumerate(outs):
                out[0, half * total.shape[0] + p] = total[p, source_of(dz, 0)]
                out[1, half * total.shape[0] + p] = total[p, source_of(dz, 1)]


def sum_rows(terms):
    per, _, capacity, wide = terms[0].shape
    return pl.pallas_call(
        sum_kernel,
        out_shape=[jax.ShapeDtypeStruct((2, len(terms) // 3 * per, capacity, wide), BF16)] * 2,
        in_specs=[VMEM] * len(terms),
        out_specs=[VMEM] * 2,
        compiler_params=pltpu.CompilerParams(vmem_limit_bytes=8 << 20),
        name="sum_rows",
    )(*terms)


def combine_kernel(capacity, exp_dev, picks, place_ref, gate_ref, *refs):
    ins, (out_ref, grad_ref) = refs[:-2], refs[-2:]
    me = lax.axis_index("expert")
    wide = ins[0].shape[-1]
    place = place_ref[...]
    rows, hot = [], []
    for array, index, offset, first_expert in picks:
        rows.append(ins[array][index].reshape(-1, wide))
        first = (me ^ offset) * (exp_dev * capacity) + first_expert * capacity
        hot.append(one_hot(place, first, rows[-1].shape[0]))
    total = lax.dot_general(jnp.concatenate(rows, axis=0), jnp.concatenate(hot, axis=0), TN, preferred_element_type=F32)
    features = out_ref.shape[0]
    out_ref[...] = (gate_ref[...] * total[:features]).astype(BF16)
    grad_ref[...] = total[features:].astype(BF16)


def combine(place, gate, returned, picks, features, exp_dev, capacity):
    count = place.shape[1]
    return pl.pallas_call(
        functools.partial(combine_kernel, capacity, exp_dev, picks),
        out_shape=[jax.ShapeDtypeStruct((features, count), BF16)] * 2,
        in_specs=[VMEM] * (2 + len(returned)),
        out_specs=[VMEM] * 2,
        compiler_params=pltpu.CompilerParams(vmem_limit_bytes=24 << 20),
        name="combine",
    )(place, gate, *returned)


def swap(value, axis, bits):
    size = lax.axis_size(axis)
    return lax.ppermute(value, axis, [(i, i ^ bits) for i in range(size)])


def along_z(buffers):
    direct = [buffers[0]] + [None] * (len(buffers) - 1)
    for dz in reversed(range(1, len(buffers))):
        direct[dz] = swap(buffers[dz], "expert", 2 * dz)
    return direct


def between_cores(direct, *earlier):
    return swap(jnp.stack([rows[1] for rows in after(direct, *earlier)]), "expert", 1)


def after(values, *earlier):
    return lax.optimization_barrier((values, earlier))[0]


def local(tokens, routes, gate_value, weight_in, weight_out, cotangent):
    owners = lax.axis_size("expert")
    exp_dev = weight_in.shape[0]
    count, features = tokens.shape
    capacity = 2 * count // (owners * exp_dev)
    place, gate, buffers = dispatch(
        routes.reshape(1, count), gate_value.reshape(1, count), tokens.T, cotangent.T, owners, exp_dev, capacity
    )
    first, second = load(weight_in, weight_out)
    same, other = buffers[0]
    here = jnp.stack([same, swap(other, "expert", 1)])
    here = [here] + [swap(here, "hidden", bits) for bits in (1, 2, 3)]
    direct = along_z(buffers)[1:]
    rows = pack(direct, between_cores(direct, first, second, *here[1:]))
    per = exp_dev // CHUNKS
    own, near, far = [rows[per * c : per * (c + 1)] for c in range(CHUNKS)], [], []
    for c in range(CHUNKS):
        near.append([swap(rows, "hidden", way[0]) for rows, way in zip(own[c], WAYS)])
    for c in range(CHUNKS):
        pairs = list(zip(own[c], near[c]))
        if c:
            pairs[1] = after(pairs[1], near[c - 1])
        pairs = [jnp.stack(pair) for pair in pairs]
        far.append([swap(pair, "hidden", way[1]) for pair, way in zip(pairs, WAYS)])
    parts, saved = [], []
    for c in range(CHUNKS):
        pieces = [piece for three in zip(own[c], near[c], far[c]) for piece in three]
        part, save = run_experts(per * c, here, pieces, first, second)
        parts.append(part)
        saved.append(save)

    def step_back(c, group):
        mine, other, pair = parts[c][group]
        landed = swap(pair, "hidden", UNITS[group][0])
        return [mine, landed, (other.astype(F32) + landed[1].astype(F32)).astype(BF16)]

    far_terms = [step_back(c, 1) for c in range(CHUNKS)]
    near_terms = [step_back(c, 0) for c in range(CHUNKS)]
    def finish(terms, group):
        passed = [swap(both, "hidden", UNITS[group][1]) for _, _, both in terms]
        totals = sum_rows([rows for (mine, landed, _), last in zip(terms, passed) for rows in (mine, landed, last)])
        return [swap(rows, "expert", 2 * dz) if dz else rows for dz, rows in zip(OFFSETS[group], totals)], totals

    grads = weight_grads(0, saved[0], weight_in, weight_out, [])
    near_terms[1][2] = after(near_terms[1][2], grads)
    homeward = []
    for c in range(CHUNKS):
        if c:
            far_terms[c][2] = after(far_terms[c][2], homeward[-1][-1])
        homeward.append((1, per * c, *finish(far_terms[c : c + 1], 1)))
    near_terms[0][0] = after(near_terms[0][0], homeward[-1][-1])
    homeward.append((0, 0, *finish(near_terms, 0)))
    grads = weight_grads(1, after(saved[1], homeward[-1][-1]), weight_in, weight_out, grads)
    returned, picks = [], []
    for group, first_expert, direct, _ in homeward:
        for j, dz in enumerate(OFFSETS[group]):
            picks.append((len(returned) + j, (0,), 2 * dz, first_expert))
            picks.append((len(returned) + 2, (j,), 2 * dz + 1, first_expert))
        returned.extend([*direct, between_cores(direct, *grads)])
    layer_out, grad_tokens = combine(place, gate, returned, picks, features, exp_dev, capacity)
    return layer_out.T, grad_tokens.T, grads[0], grads[1]


def solution(mesh):
    in_specs = (
        P("expert", "hidden"),
        P("expert", None),
        P("expert", None),
        P("expert", None, "hidden"),
        P("expert", "hidden", None),
        P("expert", "hidden"),
    )
    out_specs = (
        P("expert", "hidden"),
        P("expert", "hidden"),
        P("expert", None, "hidden"),
        P("expert", "hidden", None),
    )

    def whole(*args):
        wide = 2 * args[0].shape[1] // mesh.shape["hidden"]
        capacity = 2 * args[0].shape[0] // args[3].shape[0]
        four = mesh.shape["hidden"] == 4 and args[3].shape[0] == 4 * mesh.shape["expert"]
        fits = four and mesh.shape["expert"] == 8 and wide % 128 == 0 and capacity % 16 == 0
        body = local if fits else general
        return jax.shard_map(body, mesh=mesh, in_specs=in_specs, out_specs=out_specs, check_vma=False)(*args)

    return whole
```

```python
import functools
import jax
import jax.numpy as jnp
from jax import lax
from jax.experimental import pallas as pl
from jax.experimental.pallas import tpu as pltpu
from jax.sharding import PartitionSpec as P

CHUNKS = 2
BF16 = jnp.bfloat16
F32 = jnp.float32


def gelu_tanh(values):
    return jax.nn.gelu(values, approximate=True)


def local_places(routes, experts, capacity):
    chosen = routes[:, 0]
    matches = (chosen[:, None] == jnp.arange(experts, dtype=jnp.int32)[None, :]).astype(jnp.int32)
    before = jnp.cumsum(matches, axis=0) - matches
    return chosen * capacity + jnp.sum(before * matches, axis=1)


def general(tokens, routes, gate_value, weight_in, weight_out, cotangent):
    owners = lax.axis_size("expert")
    blocks = lax.axis_size("hidden")
    exp_dev = weight_in.shape[0]
    experts = owners * exp_dev
    capacity = max(2, 2 * tokens.shape[0] // experts)
    slot_count = experts * capacity
    features = tokens.shape[1]
    full_width = weight_out.shape[2]
    units = weight_in.shape[2]
    line = exp_dev * capacity * features
    placed = local_places(routes, experts, capacity)
    scaled = (gate_value * cotangent.astype(F32)).astype(BF16)
    first_four = weight_in.reshape(exp_dev, blocks, features, units)
    second_four = weight_out.reshape(exp_dev, units, blocks, features)

    def to_slots(values):
        filled = jnp.zeros((slot_count, features), BF16).at[placed].set(values)
        return filled.reshape(owners, line)

    def rows_of(values):
        arrived = lax.all_to_all(to_slots(values), "expert", split_axis=0, concat_axis=0, tiled=True)
        gathered = lax.all_gather(arrived[None], "hidden", axis=0, tiled=True)
        return gathered.reshape(blocks, owners, exp_dev, capacity, features)

    def back(part):
        flat = part.reshape(blocks, owners, line).astype(BF16)
        total = lax.psum_scatter(flat, "hidden", scatter_dimension=0, tiled=True)
        total = total.astype(F32)[0].astype(BF16)
        returned = lax.all_to_all(total, "expert", split_axis=0, concat_axis=0, tiled=True)
        return returned.reshape(slot_count, features)[placed]

    rows_x = rows_of(tokens)
    rows_g = rows_of(scaled)
    preact = jnp.einsum("nsecf,enfh->sech", rows_x, first_four, preferred_element_type=F32)
    activation, pullback = jax.vjp(gelu_tanh, preact)
    hidden_act = activation.astype(BF16)
    out_part = jnp.einsum("sech,ehnf->nsecf", hidden_act, second_four, preferred_element_type=F32)
    grad_hidden = jnp.einsum("nsecf,ehnf->sech", rows_g, second_four, preferred_element_type=F32)
    grad_pre = pullback(grad_hidden)[0].astype(BF16)
    grad_part = jnp.einsum("sech,enfh->nsecf", grad_pre, first_four, preferred_element_type=F32)
    grad_weight_in = jnp.einsum("nsecf,sech->enfh", rows_x, grad_pre, preferred_element_type=F32)
    grad_weight_out = jnp.einsum("sech,nsecf->ehnf", hidden_act, rows_g, preferred_element_type=F32)
    layer_out = (gate_value * back(out_part).astype(F32)).astype(BF16)
    return (
        layer_out,
        back(grad_part),
        grad_weight_in.astype(BF16).reshape(exp_dev, full_width, units),
        grad_weight_out.astype(BF16).reshape(exp_dev, units, full_width),
    )


NT = (((1,), (1,)), ((), ()))
TN = (((0,), (0,)), ((), ()))
VMEM = pl.BlockSpec(memory_space=pltpu.VMEM)
HBM = pl.BlockSpec(memory_space=pltpu.HBM)
WAYS = ((1, 2), (2, 1))
UNITS = ((2, 1), (1, 2))
OFFSETS = ((0, 1), (2, 3))


def one_hot(place, first, count):
    rows = lax.broadcasted_iota(jnp.int32, (count, place.shape[1]), 0)
    return jnp.where(rows == place - first, 1.0, 0.0).astype(BF16)


def dispatch_kernel(exp_dev, capacity, *refs):
    ins, place_ref, gate_ref, rest = refs[:4], refs[4], refs[5], refs[6:]
    buffers, (routes_buf, tok_buf, cot_buf, sems) = rest[:-4], rest[-4:]
    loads = [
        pltpu.make_async_copy(source, target, sems.at[i])
        for i, (source, target) in enumerate(zip(ins, (routes_buf, gate_ref, tok_buf, cot_buf)))
    ]
    for load in loads:
        load.start()
    tokens = routes_buf.shape[1]
    experts = 2 * len(buffers) * exp_dev
    line = exp_dev * capacity
    me = lax.axis_index("expert")
    earlier = lax.broadcasted_iota(jnp.int32, (tokens, tokens), 0) < lax.broadcasted_iota(
        jnp.int32, (tokens, tokens), 1
    )
    earlier = jnp.where(earlier, 1.0, 0.0).astype(BF16)
    loads[0].wait()
    chosen = routes_buf[...]
    matches = lax.broadcasted_iota(jnp.int32, (experts, tokens), 0) == chosen
    before = jnp.dot(jnp.where(matches, 1.0, 0.0).astype(BF16), earlier, preferred_element_type=F32)
    within = jnp.sum(jnp.where(matches, before, 0.0), axis=0, keepdims=True).astype(jnp.int32)
    place = chosen * capacity + within
    place_ref[...] = place
    for load in loads[1:]:
        load.wait()
    scaled = (gate_ref[...] * cot_buf[...].astype(F32)).astype(BF16)
    both = jnp.concatenate([tok_buf[...], scaled], axis=0)
    for dz, ref in enumerate(buffers):
        firsts = [(me ^ offset) * line for offset in (2 * dz, 2 * dz + 1)]
        hot = jnp.concatenate([one_hot(place, first, line) for first in firsts], axis=0)
        filled = lax.dot_general(hot, both, NT, preferred_element_type=F32).astype(BF16)
        ref[...] = filled.reshape(ref.shape)


def in_hbm(*arrays):
    return [pltpu.with_memory_space_constraint(array, pltpu.HBM) for array in arrays]


def dispatch(routes, gate, tokens, cotangent, owners, exp_dev, capacity):
    features, count = tokens.shape
    buffer = jax.ShapeDtypeStruct((2, exp_dev, capacity, 2 * features), BF16)
    buffers = owners // 2
    place, gate, *buffers = pl.pallas_call(
        functools.partial(dispatch_kernel, exp_dev, capacity),
        out_shape=[jax.ShapeDtypeStruct((1, count), jnp.int32), jax.ShapeDtypeStruct((1, count), F32)]
        + [buffer] * buffers,
        in_specs=[HBM] * 4,
        out_specs=[VMEM] * (2 + buffers),
        scratch_shapes=[pltpu.VMEM((1, count), jnp.int32)]
        + [pltpu.VMEM((features, count), BF16)] * 2
        + [pltpu.SemaphoreType.DMA((4,))],
        compiler_params=pltpu.CompilerParams(vmem_limit_bytes=24 << 20),
        name="dispatch",
    )(*in_hbm(routes, gate, tokens, cotangent))
    return place, gate, buffers


def source_of(dz, other_core):
    return 2 * dz + other_core


def pack_kernel(*refs):
    per = refs[0].shape[1]
    direct, passed, outs = refs[: -per - 1], refs[-per - 1], refs[-per:]
    for p, out in enumerate(outs):
        for i, ref in enumerate(direct):
            out[source_of(i, 0)] = ref[0, p]
            out[source_of(i, 1)] = passed[i, p]


def pack(direct, passed):
    _, per, capacity, wide = direct[0].shape
    return pl.pallas_call(
        pack_kernel,
        out_shape=[jax.ShapeDtypeStruct((2 * len(direct), capacity, wide), BF16)] * per,
        in_specs=[VMEM] * (1 + len(direct)),
        out_specs=[VMEM] * per,
        compiler_params=pltpu.CompilerParams(vmem_limit_bytes=8 << 20),
        name="pack",
    )(*direct, passed)


def load_kernel(*refs):
    count = (len(refs) - 1) // 2
    sems = refs[-1]
    loads = [pltpu.make_async_copy(refs[i], refs[count + i], sems.at[i]) for i in range(count)]
    for load in loads:
        load.start()
    for load in loads:
        load.wait()


def load(*arrays):
    return pl.pallas_call(
        load_kernel,
        out_shape=[jax.ShapeDtypeStruct(array.shape, array.dtype) for array in arrays],
        in_specs=[HBM] * len(arrays),
        out_specs=[VMEM] * len(arrays),
        scratch_shapes=[pltpu.SemaphoreType.DMA((len(arrays),))],
        compiler_params=pltpu.CompilerParams(vmem_limit_bytes=16 << 20),
        name="load",
    )(*in_hbm(*arrays))


def in_order(mine, pieces):
    odd, high = mine % 2 == 1, mine // 2 == 1
    pieces = [jnp.where(odd, pieces[k ^ 1], pieces[k]) for k in range(4)]
    return [jnp.where(high, pieces[k ^ 2], pieces[k]) for k in range(4)]


def expert_kernel(first_expert, features, *refs):
    per = len(WAYS)
    here, refs = refs[:4], refs[4:]
    ins, (first_ref, second_ref), refs = refs[: 3 * per], refs[3 * per : 3 * per + 2], refs[3 * per + 2 :]
    outs, saved = refs[: 3 * len(UNITS)], refs[3 * len(UNITS) :]
    mine = lax.axis_index("hidden")
    rows = saved[0].shape[0]
    for p, (near, far) in enumerate(WAYS):
        own_ref, near_ref, far_ref = ins[3 * p : 3 * p + 3]
        away = own_ref.shape[0] * own_ref.shape[1]
        found = {0: own_ref[...], near: near_ref[...], far: far_ref[0], 3: far_ref[1]}
        pieces = [
            jnp.concatenate(
                [here[bits][:, first_expert + p].reshape(rows - away, 2 * features), found[bits].reshape(away, 2 * features)],
                axis=0,
            )
            for bits in range(4)
        ]
        pieces = in_order(mine, pieces)
        x = jnp.concatenate([piece[:, :features] for piece in pieces], axis=1)
        g = jnp.concatenate([piece[:, features:] for piece in pieces], axis=1)
        first, second = first_ref[first_expert + p], second_ref[first_expert + p]
        v = jnp.dot(x, first, preferred_element_type=F32)
        grad_hidden = lax.dot_general(g, second, NT, preferred_element_type=F32)
        root = 0.7978845608028654
        square = v * v
        t = jnp.tanh(root * (v + 0.044715 * (v * square)))
        act = (0.5 * v * (1.0 + t)).astype(BF16)
        slope = 0.5 * (1.0 + t) + 0.5 * v * (1.0 - t * t) * (root * (1.0 + 3 * 0.044715 * square))
        grad_pre = (grad_hidden * slope).astype(BF16)
        out = jnp.dot(act, second, preferred_element_type=F32).astype(BF16)
        grad = lax.dot_general(grad_pre, first, NT, preferred_element_type=F32).astype(BF16)
        pieces = []
        for j in range(4):
            lanes = slice(j * features, (j + 1) * features)
            pieces.append(jnp.concatenate([out[:, lanes], grad[:, lanes]], axis=1))
        pieces = in_order(mine, pieces)
        for group, (near, far) in enumerate(UNITS):
            own_ref, far_ref, near_ref = outs[3 * group : 3 * group + 3]
            span = slice(group * rows // len(UNITS), (group + 1) * rows // len(UNITS))
            own_ref[p] = pieces[0][span].reshape(own_ref.shape[1:])
            far_ref[p] = pieces[far][span].reshape(own_ref.shape[1:])
            near_ref[0, p] = pieces[near][span].reshape(own_ref.shape[1:])
            near_ref[1, p] = pieces[3][span].reshape(own_ref.shape[1:])
        for ref, value in zip(saved[4 * p : 4 * p + 4], (x, g, act, grad_pre)):
            ref[...] = value


def run_experts(first_expert, here, pieces, first, second):
    away, capacity, wide = pieces[0].shape
    sources = away + here[0].shape[0]
    _, width, units = first.shape
    rows = sources * capacity
    per = len(WAYS)
    part = (per, sources // len(UNITS), capacity, wide)
    results = pl.pallas_call(
        functools.partial(expert_kernel, first_expert, wide // 2),
        out_shape=[jax.ShapeDtypeStruct(shape, BF16) for shape in (part, part, (2, *part))] * len(UNITS)
        + [jax.ShapeDtypeStruct((rows, n), BF16) for n in (width, width, units, units)] * per,
        in_specs=[VMEM] * (len(here) + len(pieces) + 2),
        out_specs=[VMEM] * (3 * len(UNITS) + 4 * per),
        compiler_params=pltpu.CompilerParams(vmem_limit_bytes=16 << 20),
        cost_estimate=pl.CostEstimate(
            flops=8 * per * rows * width * units,
            bytes_accessed=4 * per * width * units,
            transcendentals=per * rows * units,
        ),
        name="experts",
    )(*here, *pieces, first, second)
    parts = [results[3 * group : 3 * group + 3] for group in range(len(UNITS))]
    return parts, results[3 * len(UNITS) :]


def weight_kernel(first_expert, per, *refs):
    saved, rest = refs[: 4 * per], refs[-6:]
    grad_first_hbm, grad_second_hbm, first_buf, second_buf, sems = rest[-5:]
    stores = []
    for p in range(per):
        x, g, act, grad_pre = (ref[...] for ref in saved[4 * p : 4 * p + 4])
        first_buf[p] = lax.dot_general(x, grad_pre, TN, preferred_element_type=F32).astype(BF16)
        stores.append(pltpu.make_async_copy(first_buf.at[p], grad_first_hbm.at[first_expert + p], sems.at[p, 0]))
        stores[-1].start()
        second_buf[p] = lax.dot_general(act, g, TN, preferred_element_type=F32).astype(BF16)
        stores.append(pltpu.make_async_copy(second_buf.at[p], grad_second_hbm.at[first_expert + p], sems.at[p, 1]))
        stores[-1].start()
    for store in stores:
        store.wait()


def weight_grads(chunk, saved, weight_in, weight_out, grads):
    per = len(saved) // 4
    rows, width = saved[0].shape
    units = weight_in.shape[2]
    count = 4 * per
    return pl.pallas_call(
        functools.partial(weight_kernel, chunk * per, per),
        out_shape=[jax.ShapeDtypeStruct(array.shape, BF16) for array in (weight_in, weight_out)],
        in_specs=[VMEM] * count + [HBM] * len(grads),
        out_specs=[HBM] * 2,
        scratch_shapes=[pltpu.VMEM((per, width, units), BF16), pltpu.VMEM((per, units, width), BF16)]
        + [pltpu.SemaphoreType.DMA((per, 2))],
        input_output_aliases={count: 0, count + 1: 1} if grads else {},
        compiler_params=pltpu.CompilerParams(vmem_limit_bytes=20 << 20),
        cost_estimate=pl.CostEstimate(
            flops=4 * per * rows * width * units, bytes_accessed=4 * per * width * units, transcendentals=0
        ),
        name="weight_grads",
    )(*saved, *grads)


def sum_kernel(*refs):
    halves = (len(refs) - 2) // 3
    terms, outs = refs[: 3 * halves], refs[3 * halves :]
    for half in range(halves):
        own, side, passed = terms[3 * half : 3 * half + 3]
        total = own[...].astype(F32) + side[0].astype(F32) + passed[...].astype(F32)
        total = total.astype(BF16)
        for p in range(total.shape[0]):
            for dz, out in enumerate(outs):
                out[0, half * total.shape[0] + p] = total[p, source_of(dz, 0)]
                out[1, half * total.shape[0] + p] = total[p, source_of(dz, 1)]


def sum_rows(terms):
    per, _, capacity, wide = terms[0].shape
    return pl.pallas_call(
        sum_kernel,
        out_shape=[jax.ShapeDtypeStruct((2, len(terms) // 3 * per, capacity, wide), BF16)] * 2,
        in_specs=[VMEM] * len(terms),
        out_specs=[VMEM] * 2,
        compiler_params=pltpu.CompilerParams(vmem_limit_bytes=8 << 20),
        name="sum_rows",
    )(*terms)


def combine_kernel(capacity, exp_dev, picks, place_ref, gate_ref, *refs):
    ins, (out_ref, grad_ref) = refs[:-2], refs[-2:]
    me = lax.axis_index("expert")
    wide = ins[0].shape[-1]
    place = place_ref[...]
    rows, hot = [], []
    for array, index, offset, first_expert in picks:
        rows.append(ins[array][index].reshape(-1, wide))
        first = (me ^ offset) * (exp_dev * capacity) + first_expert * capacity
        hot.append(one_hot(place, first, rows[-1].shape[0]))
    total = lax.dot_general(jnp.concatenate(rows, axis=0), jnp.concatenate(hot, axis=0), TN, preferred_element_type=F32)
    features = out_ref.shape[0]
    out_ref[...] = (gate_ref[...] * total[:features]).astype(BF16)
    grad_ref[...] = total[features:].astype(BF16)


def combine(place, gate, returned, picks, features, exp_dev, capacity):
    count = place.shape[1]
    return pl.pallas_call(
        functools.partial(combine_kernel, capacity, exp_dev, picks),
        out_shape=[jax.ShapeDtypeStruct((features, count), BF16)] * 2,
        in_specs=[VMEM] * (2 + len(returned)),
        out_specs=[VMEM] * 2,
        compiler_params=pltpu.CompilerParams(vmem_limit_bytes=24 << 20),
        name="combine",
    )(place, gate, *returned)


def swap(value, axis, bits):
    size = lax.axis_size(axis)
    return lax.ppermute(value, axis, [(i, i ^ bits) for i in range(size)])


def along_z(buffers):
    direct = [buffers[0]] + [None] * (len(buffers) - 1)
    for dz in reversed(range(1, len(buffers))):
        direct[dz] = swap(buffers[dz], "expert", 2 * dz)
    return direct


def between_cores(direct, *earlier):
    return swap(jnp.stack([rows[1] for rows in after(direct, *earlier)]), "expert", 1)


def after(values, *earlier):
    return lax.optimization_barrier((values, earlier))[0]


def local(tokens, routes, gate_value, weight_in, weight_out, cotangent):
    owners = lax.axis_size("expert")
    exp_dev = weight_in.shape[0]
    count, features = tokens.shape
    capacity = 2 * count // (owners * exp_dev)
    place, gate, buffers = dispatch(
        routes.reshape(1, count), gate_value.reshape(1, count), tokens.T, cotangent.T, owners, exp_dev, capacity
    )
    first, second = load(weight_in, weight_out)
    same, other = buffers[0]
    here = jnp.stack([same, swap(other, "expert", 1)])
    here = [here] + [swap(here, "hidden", bits) for bits in (1, 2, 3)]
    direct = along_z(buffers)[1:]
    rows = pack(direct, between_cores(direct, first, second, *here[1:]))
    per = exp_dev // CHUNKS
    own, near, far = [rows[per * c : per * (c + 1)] for c in range(CHUNKS)], [], []
    for c in range(CHUNKS):
        near.append([swap(rows, "hidden", way[0]) for rows, way in zip(own[c], WAYS)])
    for c in range(CHUNKS):
        pairs = list(zip(own[c], near[c]))
        if c:
            pairs[1] = after(pairs[1], near[c - 1])
        pairs = [jnp.stack(pair) for pair in pairs]
        far.append([swap(pair, "hidden", way[1]) for pair, way in zip(pairs, WAYS)])
    parts, saved = [], []
    for c in range(CHUNKS):
        pieces = [piece for three in zip(own[c], near[c], far[c]) for piece in three]
        part, save = run_experts(per * c, here, pieces, first, second)
        parts.append(part)
        saved.append(save)

    def step_back(c, group):
        mine, other, pair = parts[c][group]
        landed = swap(pair, "hidden", UNITS[group][0])
        return [mine, landed, (other.astype(F32) + landed[1].astype(F32)).astype(BF16)]

    far_terms = [step_back(c, 1) for c in range(CHUNKS)]
    near_terms = [step_back(c, 0) for c in range(CHUNKS)]
    def finish(terms, group):
        passed = [swap(both, "hidden", UNITS[group][1]) for _, _, both in terms]
        totals = sum_rows([rows for (mine, landed, _), last in zip(terms, passed) for rows in (mine, landed, last)])
        return [swap(rows, "expert", 2 * dz) if dz else rows for dz, rows in zip(OFFSETS[group], totals)], totals

    grads = weight_grads(0, saved[0], weight_in, weight_out, [])
    near_terms[1][2] = after(near_terms[1][2], grads)
    homeward = []
    for c in range(CHUNKS):
        if c:
            far_terms[c][2] = after(far_terms[c][2], homeward[-1][-1])
        homeward.append((1, per * c, *finish(far_terms[c : c + 1], 1)))
    near_terms[0][0] = after(near_terms[0][0], homeward[-1][-1])
    homeward.append((0, 0, *finish(near_terms, 0)))
    grads = weight_grads(1, after(saved[1], homeward[-1][-1]), weight_in, weight_out, grads)
    returned, picks = [], []
    for group, first_expert, direct, _ in homeward:
        for j, dz in enumerate(OFFSETS[group]):
            picks.append((len(returned) + j, (0,), 2 * dz, first_expert))
            picks.append((len(returned) + 2, (j,), 2 * dz + 1, first_expert))
        returned.extend([*direct, between_cores(direct, *grads)])
    layer_out, grad_tokens = combine(place, gate, returned, picks, features, exp_dev, capacity)
    return layer_out.T, grad_tokens.T, grads[0], grads[1]


def solution(mesh):
    in_specs = (
        P("expert", "hidden"),
        P("expert", None),
        P("expert", None),
        P("expert", None, "hidden"),
        P("expert", "hidden", None),
        P("expert", "hidden"),
    )
    out_specs = (
        P("expert", "hidden"),
        P("expert", "hidden"),
        P("expert", None, "hidden"),
        P("expert", "hidden", None),
    )

    def whole(*args):
        wide = 2 * args[0].shape[1] // mesh.shape["hidden"]
        capacity = 2 * args[0].shape[0] // args[3].shape[0]
        four = mesh.shape["hidden"] == 4 and args[3].shape[0] == 4 * mesh.shape["expert"]
        fits = four and mesh.shape["expert"] == 8 and wide % 128 == 0 and capacity % 16 == 0
        body = local if fits else general
        return jax.shard_map(body, mesh=mesh, in_specs=in_specs, out_specs=out_specs, check_vma=False)(*args)

    return whole
```

```python
import functools
import jax
import jax.numpy as jnp
from jax import lax
from jax.experimental import pallas as pl
from jax.experimental.pallas import tpu as pltpu
from jax.sharding import PartitionSpec as P

CHUNKS = 2
BF16 = jnp.bfloat16
F32 = jnp.float32


def gelu_tanh(values):
    return jax.nn.gelu(values, approximate=True)


def local_places(routes, experts, capacity):
    chosen = routes[:, 0]
    matches = (chosen[:, None] == jnp.arange(experts, dtype=jnp.int32)[None, :]).astype(jnp.int32)
    before = jnp.cumsum(matches, axis=0) - matches
    return chosen * capacity + jnp.sum(before * matches, axis=1)


def general(tokens, routes, gate_value, weight_in, weight_out, cotangent):
    owners = lax.axis_size("expert")
    blocks = lax.axis_size("hidden")
    exp_dev = weight_in.shape[0]
    experts = owners * exp_dev
    capacity = max(2, 2 * tokens.shape[0] // experts)
    slot_count = experts * capacity
    features = tokens.shape[1]
    full_width = weight_out.shape[2]
    units = weight_in.shape[2]
    line = exp_dev * capacity * features
    placed = local_places(routes, experts, capacity)
    scaled = (gate_value * cotangent.astype(F32)).astype(BF16)
    first_four = weight_in.reshape(exp_dev, blocks, features, units)
    second_four = weight_out.reshape(exp_dev, units, blocks, features)

    def to_slots(values):
        filled = jnp.zeros((slot_count, features), BF16).at[placed].set(values)
        return filled.reshape(owners, line)

    def rows_of(values):
        arrived = lax.all_to_all(to_slots(values), "expert", split_axis=0, concat_axis=0, tiled=True)
        gathered = lax.all_gather(arrived[None], "hidden", axis=0, tiled=True)
        return gathered.reshape(blocks, owners, exp_dev, capacity, features)

    def back(part):
        flat = part.reshape(blocks, owners, line).astype(BF16)
        total = lax.psum_scatter(flat, "hidden", scatter_dimension=0, tiled=True)
        total = total.astype(F32)[0].astype(BF16)
        returned = lax.all_to_all(total, "expert", split_axis=0, concat_axis=0, tiled=True)
        return returned.reshape(slot_count, features)[placed]

    rows_x = rows_of(tokens)
    rows_g = rows_of(scaled)
    preact = jnp.einsum("nsecf,enfh->sech", rows_x, first_four, preferred_element_type=F32)
    activation, pullback = jax.vjp(gelu_tanh, preact)
    hidden_act = activation.astype(BF16)
    out_part = jnp.einsum("sech,ehnf->nsecf", hidden_act, second_four, preferred_element_type=F32)
    grad_hidden = jnp.einsum("nsecf,ehnf->sech", rows_g, second_four, preferred_element_type=F32)
    grad_pre = pullback(grad_hidden)[0].astype(BF16)
    grad_part = jnp.einsum("sech,enfh->nsecf", grad_pre, first_four, preferred_element_type=F32)
    grad_weight_in = jnp.einsum("nsecf,sech->enfh", rows_x, grad_pre, preferred_element_type=F32)
    grad_weight_out = jnp.einsum("sech,nsecf->ehnf", hidden_act, rows_g, preferred_element_type=F32)
    layer_out = (gate_value * back(out_part).astype(F32)).astype(BF16)
    return (
        layer_out,
        back(grad_part),
        grad_weight_in.astype(BF16).reshape(exp_dev, full_width, units),
        grad_weight_out.astype(BF16).reshape(exp_dev, units, full_width),
    )


NT = (((1,), (1,)), ((), ()))
TN = (((0,), (0,)), ((), ()))
VMEM = pl.BlockSpec(memory_space=pltpu.VMEM)
HBM = pl.BlockSpec(memory_space=pltpu.HBM)
WAYS = ((1, 2), (2, 1))
UNITS = ((2, 1), (1, 2))
OFFSETS = ((0, 1), (2, 3))


def one_hot(place, first, count):
    rows = lax.broadcasted_iota(jnp.int32, (count, place.shape[1]), 0)
    return jnp.where(rows == place - first, 1.0, 0.0).astype(BF16)


def dispatch_kernel(exp_dev, capacity, *refs):
    ins, place_ref, gate_ref, rest = refs[:4], refs[4], refs[5], refs[6:]
    buffers, (routes_buf, tok_buf, cot_buf, sems) = rest[:-4], rest[-4:]
    loads = [
        pltpu.make_async_copy(source, target, sems.at[i])
        for i, (source, target) in enumerate(zip(ins, (routes_buf, gate_ref, tok_buf, cot_buf)))
    ]
    for load in loads:
        load.start()
    tokens = routes_buf.shape[1]
    experts = 2 * len(buffers) * exp_dev
    line = exp_dev * capacity
    me = lax.axis_index("expert")
    earlier = lax.broadcasted_iota(jnp.int32, (tokens, tokens), 0) < lax.broadcasted_iota(
        jnp.int32, (tokens, tokens), 1
    )
    earlier = jnp.where(earlier, 1.0, 0.0).astype(BF16)
    loads[0].wait()
    chosen = routes_buf[...]
    matches = lax.broadcasted_iota(jnp.int32, (experts, tokens), 0) == chosen
    before = jnp.dot(jnp.where(matches, 1.0, 0.0).astype(BF16), earlier, preferred_element_type=F32)
    within = jnp.sum(jnp.where(matches, before, 0.0), axis=0, keepdims=True).astype(jnp.int32)
    place = chosen * capacity + within
    place_ref[...] = place
    for load in loads[1:]:
        load.wait()
    scaled = (gate_ref[...] * cot_buf[...].astype(F32)).astype(BF16)
    both = jnp.concatenate([tok_buf[...], scaled], axis=0)
    for dz, ref in enumerate(buffers):
        firsts = [(me ^ offset) * line for offset in (2 * dz, 2 * dz + 1)]
        hot = jnp.concatenate([one_hot(place, first, line) for first in firsts], axis=0)
        filled = lax.dot_general(hot, both, NT, preferred_element_type=F32).astype(BF16)
        ref[...] = filled.reshape(ref.shape)


def in_hbm(*arrays):
    return [pltpu.with_memory_space_constraint(array, pltpu.HBM) for array in arrays]


def dispatch(routes, gate, tokens, cotangent, owners, exp_dev, capacity):
    features, count = tokens.shape
    buffer = jax.ShapeDtypeStruct((2, exp_dev, capacity, 2 * features), BF16)
    buffers = owners // 2
    place, gate, *buffers = pl.pallas_call(
        functools.partial(dispatch_kernel, exp_dev, capacity),
        out_shape=[jax.ShapeDtypeStruct((1, count), jnp.int32), jax.ShapeDtypeStruct((1, count), F32)]
        + [buffer] * buffers,
        in_specs=[HBM] * 4,
        out_specs=[VMEM] * (2 + buffers),
        scratch_shapes=[pltpu.VMEM((1, count), jnp.int32)]
        + [pltpu.VMEM((features, count), BF16)] * 2
        + [pltpu.SemaphoreType.DMA((4,))],
        compiler_params=pltpu.CompilerParams(vmem_limit_bytes=24 << 20),
        name="dispatch",
    )(*in_hbm(routes, gate, tokens, cotangent))
    return place, gate, buffers


def source_of(dz, other_core):
    return 2 * dz + other_core


def pack_kernel(*refs):
    per = refs[0].shape[1]
    direct, passed, outs = refs[: -per - 1], refs[-per - 1], refs[-per:]
    for p, out in enumerate(outs):
        for i, ref in enumerate(direct):
            out[source_of(i, 0)] = ref[0, p]
            out[source_of(i, 1)] = passed[i, p]


def pack(direct, passed):
    _, per, capacity, wide = direct[0].shape
    return pl.pallas_call(
        pack_kernel,
        out_shape=[jax.ShapeDtypeStruct((2 * len(direct), capacity, wide), BF16)] * per,
        in_specs=[VMEM] * (1 + len(direct)),
        out_specs=[VMEM] * per,
        compiler_params=pltpu.CompilerParams(vmem_limit_bytes=8 << 20),
        name="pack",
    )(*direct, passed)


def load_kernel(*refs):
    count = (len(refs) - 1) // 2
    sems = refs[-1]
    loads = [pltpu.make_async_copy(refs[i], refs[count + i], sems.at[i]) for i in range(count)]
    for load in loads:
        load.start()
    for load in loads:
        load.wait()


def load(*arrays):
    return pl.pallas_call(
        load_kernel,
        out_shape=[jax.ShapeDtypeStruct(array.shape, array.dtype) for array in arrays],
        in_specs=[HBM] * len(arrays),
        out_specs=[VMEM] * len(arrays),
        scratch_shapes=[pltpu.SemaphoreType.DMA((len(arrays),))],
        compiler_params=pltpu.CompilerParams(vmem_limit_bytes=16 << 20),
        name="load",
    )(*in_hbm(*arrays))


def in_order(mine, pieces):
    odd, high = mine % 2 == 1, mine // 2 == 1
    pieces = [jnp.where(odd, pieces[k ^ 1], pieces[k]) for k in range(4)]
    return [jnp.where(high, pieces[k ^ 2], pieces[k]) for k in range(4)]


def expert_kernel(first_expert, features, *refs):
    per = len(WAYS)
    here, refs = refs[:4], refs[4:]
    ins, (first_ref, second_ref), refs = refs[: 3 * per], refs[3 * per : 3 * per + 2], refs[3 * per + 2 :]
    outs, saved = refs[: 3 * len(UNITS)], refs[3 * len(UNITS) :]
    mine = lax.axis_index("hidden")
    rows = saved[0].shape[0]
    for p, (near, far) in enumerate(WAYS):
        own_ref, near_ref, far_ref = ins[3 * p : 3 * p + 3]
        away = own_ref.shape[0] * own_ref.shape[1]
        found = {0: own_ref[...], near: near_ref[...], far: far_ref[0], 3: far_ref[1]}
        pieces = [
            jnp.concatenate(
                [here[bits][:, first_expert + p].reshape(rows - away, 2 * features), found[bits].reshape(away, 2 * features)],
                axis=0,
            )
            for bits in range(4)
        ]
        pieces = in_order(mine, pieces)
        x = jnp.concatenate([piece[:, :features] for piece in pieces], axis=1)
        g = jnp.concatenate([piece[:, features:] for piece in pieces], axis=1)
        first, second = first_ref[first_expert + p], second_ref[first_expert + p]
        v = jnp.dot(x, first, preferred_element_type=F32)
        grad_hidden = lax.dot_general(g, second, NT, preferred_element_type=F32)
        root = 0.7978845608028654
        square = v * v
        t = jnp.tanh(root * (v + 0.044715 * (v * square)))
        act = (0.5 * v * (1.0 + t)).astype(BF16)
        slope = 0.5 * (1.0 + t) + 0.5 * v * (1.0 - t * t) * (root * (1.0 + 3 * 0.044715 * square))
        grad_pre = (grad_hidden * slope).astype(BF16)
        out = jnp.dot(act, second, preferred_element_type=F32).astype(BF16)
        grad = lax.dot_general(grad_pre, first, NT, preferred_element_type=F32).astype(BF16)
        pieces = []
        for j in range(4):
            lanes = slice(j * features, (j + 1) * features)
            pieces.append(jnp.concatenate([out[:, lanes], grad[:, lanes]], axis=1))
        pieces = in_order(mine, pieces)
        for group, (near, far) in enumerate(UNITS):
            own_ref, far_ref, near_ref = outs[3 * group : 3 * group + 3]
            span = slice(group * rows // len(UNITS), (group + 1) * rows // len(UNITS))
            own_ref[p] = pieces[0][span].reshape(own_ref.shape[1:])
            far_ref[p] = pieces[far][span].reshape(own_ref.shape[1:])
            near_ref[0, p] = pieces[near][span].reshape(own_ref.shape[1:])
            near_ref[1, p] = pieces[3][span].reshape(own_ref.shape[1:])
        for ref, value in zip(saved[4 * p : 4 * p + 4], (x, g, act, grad_pre)):
            ref[...] = value


def run_experts(first_expert, here, pieces, first, second):
    away, capacity, wide = pieces[0].shape
    sources = away + here[0].shape[0]
    _, width, units = first.shape
    rows = sources * capacity
    per = len(WAYS)
    part = (per, sources // len(UNITS), capacity, wide)
    results = pl.pallas_call(
        functools.partial(expert_kernel, first_expert, wide // 2),
        out_shape=[jax.ShapeDtypeStruct(shape, BF16) for shape in (part, part, (2, *part))] * len(UNITS)
        + [jax.ShapeDtypeStruct((rows, n), BF16) for n in (width, width, units, units)] * per,
        in_specs=[VMEM] * (len(here) + len(pieces) + 2),
        out_specs=[VMEM] * (3 * len(UNITS) + 4 * per),
        compiler_params=pltpu.CompilerParams(vmem_limit_bytes=16 << 20),
        cost_estimate=pl.CostEstimate(
            flops=8 * per * rows * width * units,
            bytes_accessed=4 * per * width * units,
            transcendentals=per * rows * units,
        ),
        name="experts",
    )(*here, *pieces, first, second)
    parts = [results[3 * group : 3 * group + 3] for group in range(len(UNITS))]
    return parts, results[3 * len(UNITS) :]


def weight_kernel(first_expert, per, *refs):
    saved, rest = refs[: 4 * per], refs[-6:]
    grad_first_hbm, grad_second_hbm, first_buf, second_buf, sems = rest[-5:]
    stores = []
    for p in range(per):
        x, g, act, grad_pre = (ref[...] for ref in saved[4 * p : 4 * p + 4])
        first_buf[p] = lax.dot_general(x, grad_pre, TN, preferred_element_type=F32).astype(BF16)
        stores.append(pltpu.make_async_copy(first_buf.at[p], grad_first_hbm.at[first_expert + p], sems.at[p, 0]))
        stores[-1].start()
        second_buf[p] = lax.dot_general(act, g, TN, preferred_element_type=F32).astype(BF16)
        stores.append(pltpu.make_async_copy(second_buf.at[p], grad_second_hbm.at[first_expert + p], sems.at[p, 1]))
        stores[-1].start()
    for store in stores:
        store.wait()


def weight_grads(chunk, saved, weight_in, weight_out, grads):
    per = len(saved) // 4
    rows, width = saved[0].shape
    units = weight_in.shape[2]
    count = 4 * per
    return pl.pallas_call(
        functools.partial(weight_kernel, chunk * per, per),
        out_shape=[jax.ShapeDtypeStruct(array.shape, BF16) for array in (weight_in, weight_out)],
        in_specs=[VMEM] * count + [HBM] * len(grads),
        out_specs=[HBM] * 2,
        scratch_shapes=[pltpu.VMEM((per, width, units), BF16), pltpu.VMEM((per, units, width), BF16)]
        + [pltpu.SemaphoreType.DMA((per, 2))],
        input_output_aliases={count: 0, count + 1: 1} if grads else {},
        compiler_params=pltpu.CompilerParams(vmem_limit_bytes=20 << 20),
        cost_estimate=pl.CostEstimate(
            flops=4 * per * rows * width * units, bytes_accessed=4 * per * width * units, transcendentals=0
        ),
        name="weight_grads",
    )(*saved, *grads)


def sum_kernel(*refs):
    halves = (len(refs) - 2) // 3
    terms, outs = refs[: 3 * halves], refs[3 * halves :]
    for half in range(halves):
        own, side, passed = terms[3 * half : 3 * half + 3]
        total = own[...].astype(F32) + side[0].astype(F32) + passed[...].astype(F32)
        total = total.astype(BF16)
        for p in range(total.shape[0]):
            for dz, out in enumerate(outs):
                out[0, half * total.shape[0] + p] = total[p, source_of(dz, 0)]
                out[1, half * total.shape[0] + p] = total[p, source_of(dz, 1)]


def sum_rows(terms):
    per, _, capacity, wide = terms[0].shape
    return pl.pallas_call(
        sum_kernel,
        out_shape=[jax.ShapeDtypeStruct((2, len(terms) // 3 * per, capacity, wide), BF16)] * 2,
        in_specs=[VMEM] * len(terms),
        out_specs=[VMEM] * 2,
        compiler_params=pltpu.CompilerParams(vmem_limit_bytes=8 << 20),
        name="sum_rows",
    )(*terms)


def combine_kernel(capacity, exp_dev, picks, place_ref, gate_ref, *refs):
    ins, (out_ref, grad_ref) = refs[:-2], refs[-2:]
    me = lax.axis_index("expert")
    wide = ins[0].shape[-1]
    place = place_ref[...]
    rows, hot = [], []
    for array, index, offset, first_expert in picks:
        rows.append(ins[array][index].reshape(-1, wide))
        first = (me ^ offset) * (exp_dev * capacity) + first_expert * capacity
        hot.append(one_hot(place, first, rows[-1].shape[0]))
    total = lax.dot_general(jnp.concatenate(rows, axis=0), jnp.concatenate(hot, axis=0), TN, preferred_element_type=F32)
    features = out_ref.shape[0]
    out_ref[...] = (gate_ref[...] * total[:features]).astype(BF16)
    grad_ref[...] = total[features:].astype(BF16)


def combine(place, gate, returned, picks, features, exp_dev, capacity):
    count = place.shape[1]
    return pl.pallas_call(
        functools.partial(combine_kernel, capacity, exp_dev, picks),
        out_shape=[jax.ShapeDtypeStruct((features, count), BF16)] * 2,
        in_specs=[VMEM] * (2 + len(returned)),
        out_specs=[VMEM] * 2,
        compiler_params=pltpu.CompilerParams(vmem_limit_bytes=24 << 20),
        name="combine",
    )(place, gate, *returned)


def swap(value, axis, bits):
    size = lax.axis_size(axis)
    return lax.ppermute(value, axis, [(i, i ^ bits) for i in range(size)])


def along_z(buffers):
    direct = [buffers[0]] + [None] * (len(buffers) - 1)
    for dz in reversed(range(1, len(buffers))):
        direct[dz] = swap(buffers[dz], "expert", 2 * dz)
    return direct


def between_cores(direct, *earlier):
    return swap(jnp.stack([rows[1] for rows in after(direct, *earlier)]), "expert", 1)


def after(values, *earlier):
    return lax.optimization_barrier((values, earlier))[0]


def local(tokens, routes, gate_value, weight_in, weight_out, cotangent):
    owners = lax.axis_size("expert")
    exp_dev = weight_in.shape[0]
    count, features = tokens.shape
    capacity = 2 * count // (owners * exp_dev)
    place, gate, buffers = dispatch(
        routes.reshape(1, count), gate_value.reshape(1, count), tokens.T, cotangent.T, owners, exp_dev, capacity
    )
    first, second = load(weight_in, weight_out)
    same, other = buffers[0]
    here = jnp.stack([same, swap(other, "expert", 1)])
    here = [here] + [swap(here, "hidden", bits) for bits in (1, 2, 3)]
    direct = along_z(buffers)[1:]
    rows = pack(direct, between_cores(direct, first, second, *here[1:]))
    per = exp_dev // CHUNKS
    own, near, far = [rows[per * c : per * (c + 1)] for c in range(CHUNKS)], [], []
    for c in range(CHUNKS):
        near.append([swap(rows, "hidden", way[0]) for rows, way in zip(own[c], WAYS)])
    for c in range(CHUNKS):
        pairs = list(zip(own[c], near[c]))
        if c:
            pairs[1] = after(pairs[1], near[c - 1])
        pairs = [jnp.stack(pair) for pair in pairs]
        far.append([swap(pair, "hidden", way[1]) for pair, way in zip(pairs, WAYS)])
    parts, saved = [], []
    for c in range(CHUNKS):
        pieces = [piece for three in zip(own[c], near[c], far[c]) for piece in three]
        part, save = run_experts(per * c, here, pieces, first, second)
        parts.append(part)
        saved.append(save)

    def step_back(c, group):
        mine, other, pair = parts[c][group]
        landed = swap(pair, "hidden", UNITS[group][0])
        return [mine, landed, (other.astype(F32) + landed[1].astype(F32)).astype(BF16)]

    far_terms = [step_back(c, 1) for c in range(CHUNKS)]
    near_terms = [step_back(c, 0) for c in range(CHUNKS)]
    def finish(terms, group):
        passed = [swap(both, "hidden", UNITS[group][1]) for _, _, both in terms]
        totals = sum_rows([rows for (mine, landed, _), last in zip(terms, passed) for rows in (mine, landed, last)])
        return [swap(rows, "expert", 2 * dz) if dz else rows for dz, rows in zip(OFFSETS[group], totals)], totals

    grads = weight_grads(0, saved[0], weight_in, weight_out, [])
    near_terms[1][2] = after(near_terms[1][2], grads)
    homeward = []
    for c in range(CHUNKS):
        if c:
            far_terms[c][2] = after(far_terms[c][2], homeward[-1][-1])
        homeward.append((1, per * c, *finish(far_terms[c : c + 1], 1)))
    near_terms[0][0] = after(near_terms[0][0], homeward[-1][-1])
    homeward.append((0, 0, *finish(near_terms, 0)))
    grads = weight_grads(1, after(saved[1], homeward[-1][-1]), weight_in, weight_out, grads)
    returned, picks = [], []
    last, taken = [], 0
    for i, (group, first_expert, direct, _) in enumerate(homeward):
        for j, dz in enumerate(OFFSETS[group]):
            picks.append((2 * i + j, (0,), 2 * dz, first_expert))
            index = (j,) if i == 0 else (slice(taken, taken + direct[j].shape[1]),)
            picks.append((2 * len(homeward) + min(i, 1), index, 2 * dz + 1, first_expert))
            taken += direct[j].shape[1] if i else 0
        last += direct if i else []
        returned.extend(direct)
    returned.append(between_cores(homeward[0][2], *grads))
    returned.append(swap(jnp.concatenate([rows[1] for rows in after(last, *grads, returned[-1])]), "expert", 1))
    layer_out, grad_tokens = combine(place, gate, returned, picks, features, exp_dev, capacity)
    return layer_out.T, grad_tokens.T, grads[0], grads[1]


def solution(mesh):
    in_specs = (
        P("expert", "hidden"),
        P("expert", None),
        P("expert", None),
        P("expert", None, "hidden"),
        P("expert", "hidden", None),
        P("expert", "hidden"),
    )
    out_specs = (
        P("expert", "hidden"),
        P("expert", "hidden"),
        P("expert", None, "hidden"),
        P("expert", "hidden", None),
    )

    def whole(*args):
        wide = 2 * args[0].shape[1] // mesh.shape["hidden"]
        capacity = 2 * args[0].shape[0] // args[3].shape[0]
        four = mesh.shape["hidden"] == 4 and args[3].shape[0] == 4 * mesh.shape["expert"]
        fits = four and mesh.shape["expert"] == 8 and wide % 128 == 0 and capacity % 16 == 0
        body = local if fits else general
        return jax.shard_map(body, mesh=mesh, in_specs=in_specs, out_specs=out_specs, check_vma=False)(*args)

    return whole
```

```python
import functools
import jax
import jax.numpy as jnp
from jax import lax
from jax.experimental import pallas as pl
from jax.experimental.pallas import tpu as pltpu
from jax.sharding import PartitionSpec as P

CHUNKS = 2
BF16 = jnp.bfloat16
F32 = jnp.float32


def gelu_tanh(values):
    return jax.nn.gelu(values, approximate=True)


def local_places(routes, experts, capacity):
    chosen = routes[:, 0]
    matches = (chosen[:, None] == jnp.arange(experts, dtype=jnp.int32)[None, :]).astype(jnp.int32)
    before = jnp.cumsum(matches, axis=0) - matches
    return chosen * capacity + jnp.sum(before * matches, axis=1)


def general(tokens, routes, gate_value, weight_in, weight_out, cotangent):
    owners = lax.axis_size("expert")
    blocks = lax.axis_size("hidden")
    exp_dev = weight_in.shape[0]
    experts = owners * exp_dev
    capacity = max(2, 2 * tokens.shape[0] // experts)
    slot_count = experts * capacity
    features = tokens.shape[1]
    full_width = weight_out.shape[2]
    units = weight_in.shape[2]
    line = exp_dev * capacity * features
    placed = local_places(routes, experts, capacity)
    scaled = (gate_value * cotangent.astype(F32)).astype(BF16)
    first_four = weight_in.reshape(exp_dev, blocks, features, units)
    second_four = weight_out.reshape(exp_dev, units, blocks, features)

    def to_slots(values):
        filled = jnp.zeros((slot_count, features), BF16).at[placed].set(values)
        return filled.reshape(owners, line)

    def rows_of(values):
        arrived = lax.all_to_all(to_slots(values), "expert", split_axis=0, concat_axis=0, tiled=True)
        gathered = lax.all_gather(arrived[None], "hidden", axis=0, tiled=True)
        return gathered.reshape(blocks, owners, exp_dev, capacity, features)

    def back(part):
        flat = part.reshape(blocks, owners, line).astype(BF16)
        total = lax.psum_scatter(flat, "hidden", scatter_dimension=0, tiled=True)
        total = total.astype(F32)[0].astype(BF16)
        returned = lax.all_to_all(total, "expert", split_axis=0, concat_axis=0, tiled=True)
        return returned.reshape(slot_count, features)[placed]

    rows_x = rows_of(tokens)
    rows_g = rows_of(scaled)
    preact = jnp.einsum("nsecf,enfh->sech", rows_x, first_four, preferred_element_type=F32)
    activation, pullback = jax.vjp(gelu_tanh, preact)
    hidden_act = activation.astype(BF16)
    out_part = jnp.einsum("sech,ehnf->nsecf", hidden_act, second_four, preferred_element_type=F32)
    grad_hidden = jnp.einsum("nsecf,ehnf->sech", rows_g, second_four, preferred_element_type=F32)
    grad_pre = pullback(grad_hidden)[0].astype(BF16)
    grad_part = jnp.einsum("sech,enfh->nsecf", grad_pre, first_four, preferred_element_type=F32)
    grad_weight_in = jnp.einsum("nsecf,sech->enfh", rows_x, grad_pre, preferred_element_type=F32)
    grad_weight_out = jnp.einsum("sech,nsecf->ehnf", hidden_act, rows_g, preferred_element_type=F32)
    layer_out = (gate_value * back(out_part).astype(F32)).astype(BF16)
    return (
        layer_out,
        back(grad_part),
        grad_weight_in.astype(BF16).reshape(exp_dev, full_width, units),
        grad_weight_out.astype(BF16).reshape(exp_dev, units, full_width),
    )


NT = (((1,), (1,)), ((), ()))
TN = (((0,), (0,)), ((), ()))
VMEM = pl.BlockSpec(memory_space=pltpu.VMEM)
HBM = pl.BlockSpec(memory_space=pltpu.HBM)
WAYS = ((1, 2), (2, 1))
UNITS = ((2, 1), (1, 2))
OFFSETS = ((0, 1), (2, 3))


def one_hot(place, first, count):
    rows = lax.broadcasted_iota(jnp.int32, (count, place.shape[1]), 0)
    return jnp.where(rows == place - first, 1.0, 0.0).astype(BF16)


def dispatch_kernel(exp_dev, capacity, *refs):
    ins, place_ref, gate_ref, rest = refs[:4], refs[4], refs[5], refs[6:]
    buffers, (routes_buf, tok_buf, cot_buf, sems) = rest[:-4], rest[-4:]
    loads = [
        pltpu.make_async_copy(source, target, sems.at[i])
        for i, (source, target) in enumerate(zip(ins, (routes_buf, gate_ref, tok_buf, cot_buf)))
    ]
    for load in loads:
        load.start()
    tokens = routes_buf.shape[1]
    experts = 2 * len(buffers) * exp_dev
    line = exp_dev * capacity
    me = lax.axis_index("expert")
    earlier = lax.broadcasted_iota(jnp.int32, (tokens, tokens), 0) < lax.broadcasted_iota(
        jnp.int32, (tokens, tokens), 1
    )
    earlier = jnp.where(earlier, 1.0, 0.0).astype(BF16)
    loads[0].wait()
    chosen = routes_buf[...]
    matches = lax.broadcasted_iota(jnp.int32, (experts, tokens), 0) == chosen
    before = jnp.dot(jnp.where(matches, 1.0, 0.0).astype(BF16), earlier, preferred_element_type=F32)
    within = jnp.sum(jnp.where(matches, before, 0.0), axis=0, keepdims=True).astype(jnp.int32)
    place = chosen * capacity + within
    place_ref[...] = place
    for load in loads[1:]:
        load.wait()
    scaled = (gate_ref[...] * cot_buf[...].astype(F32)).astype(BF16)
    both = jnp.concatenate([tok_buf[...], scaled], axis=0)
    for dz, ref in enumerate(buffers):
        firsts = [(me ^ offset) * line for offset in (2 * dz, 2 * dz + 1)]
        hot = jnp.concatenate([one_hot(place, first, line) for first in firsts], axis=0)
        filled = lax.dot_general(hot, both, NT, preferred_element_type=F32).astype(BF16)
        ref[...] = filled.reshape(ref.shape)


def in_hbm(*arrays):
    return [pltpu.with_memory_space_constraint(array, pltpu.HBM) for array in arrays]


def dispatch(routes, gate, tokens, cotangent, owners, exp_dev, capacity):
    features, count = tokens.shape
    buffer = jax.ShapeDtypeStruct((2, exp_dev, capacity, 2 * features), BF16)
    buffers = owners // 2
    place, gate, *buffers = pl.pallas_call(
        functools.partial(dispatch_kernel, exp_dev, capacity),
        out_shape=[jax.ShapeDtypeStruct((1, count), jnp.int32), jax.ShapeDtypeStruct((1, count), F32)]
        + [buffer] * buffers,
        in_specs=[HBM] * 4,
        out_specs=[VMEM] * (2 + buffers),
        scratch_shapes=[pltpu.VMEM((1, count), jnp.int32)]
        + [pltpu.VMEM((features, count), BF16)] * 2
        + [pltpu.SemaphoreType.DMA((4,))],
        compiler_params=pltpu.CompilerParams(vmem_limit_bytes=24 << 20),
        name="dispatch",
    )(*in_hbm(routes, gate, tokens, cotangent))
    return place, gate, buffers


def source_of(dz, other_core):
    return 2 * dz + other_core


def pack_kernel(*refs):
    per = refs[0].shape[1]
    direct, passed, outs = refs[: -per - 1], refs[-per - 1], refs[-per:]
    for p, out in enumerate(outs):
        for i, ref in enumerate(direct):
            out[source_of(i, 0)] = ref[0, p]
            out[source_of(i, 1)] = passed[i, p]


def pack(direct, passed):
    _, per, capacity, wide = direct[0].shape
    return pl.pallas_call(
        pack_kernel,
        out_shape=[jax.ShapeDtypeStruct((2 * len(direct), capacity, wide), BF16)] * per,
        in_specs=[VMEM] * (1 + len(direct)),
        out_specs=[VMEM] * per,
        compiler_params=pltpu.CompilerParams(vmem_limit_bytes=8 << 20),
        name="pack",
    )(*direct, passed)


def load_kernel(*refs):
    count = (len(refs) - 1) // 2
    sems = refs[-1]
    loads = [pltpu.make_async_copy(refs[i], refs[count + i], sems.at[i]) for i in range(count)]
    for load in loads:
        load.start()
    for load in loads:
        load.wait()


def load(*arrays):
    return pl.pallas_call(
        load_kernel,
        out_shape=[jax.ShapeDtypeStruct(array.shape, array.dtype) for array in arrays],
        in_specs=[HBM] * len(arrays),
        out_specs=[VMEM] * len(arrays),
        scratch_shapes=[pltpu.SemaphoreType.DMA((len(arrays),))],
        compiler_params=pltpu.CompilerParams(vmem_limit_bytes=16 << 20),
        name="load",
    )(*in_hbm(*arrays))


def in_order(mine, pieces):
    odd, high = mine % 2 == 1, mine // 2 == 1
    pieces = [jnp.where(odd, pieces[k ^ 1], pieces[k]) for k in range(4)]
    return [jnp.where(high, pieces[k ^ 2], pieces[k]) for k in range(4)]


def expert_kernel(first_expert, features, *refs):
    per = len(WAYS)
    here, refs = refs[:4], refs[4:]
    ins, (first_ref, second_ref), refs = refs[: 3 * per], refs[3 * per : 3 * per + 2], refs[3 * per + 2 :]
    outs, saved = refs[: 3 * len(UNITS)], refs[3 * len(UNITS) :]
    mine = lax.axis_index("hidden")
    rows = saved[0].shape[0]
    for p, (near, far) in enumerate(WAYS):
        own_ref, near_ref, far_ref = ins[3 * p : 3 * p + 3]
        away = own_ref.shape[0] * own_ref.shape[1]
        found = {0: own_ref[...], near: near_ref[...], far: far_ref[0], 3: far_ref[1]}
        pieces = [
            jnp.concatenate(
                [here[bits][:, first_expert + p].reshape(rows - away, 2 * features), found[bits].reshape(away, 2 * features)],
                axis=0,
            )
            for bits in range(4)
        ]
        pieces = in_order(mine, pieces)
        x = jnp.concatenate([piece[:, :features] for piece in pieces], axis=1)
        g = jnp.concatenate([piece[:, features:] for piece in pieces], axis=1)
        first, second = first_ref[first_expert + p], second_ref[first_expert + p]
        v = jnp.dot(x, first, preferred_element_type=F32)
        grad_hidden = lax.dot_general(g, second, NT, preferred_element_type=F32)
        root = 0.7978845608028654
        square = v * v
        t = jnp.tanh(root * (v + 0.044715 * (v * square)))
        act = (0.5 * v * (1.0 + t)).astype(BF16)
        slope = 0.5 * (1.0 + t) + 0.5 * v * (1.0 - t * t) * (root * (1.0 + 3 * 0.044715 * square))
        grad_pre = (grad_hidden * slope).astype(BF16)
        out = jnp.dot(act, second, preferred_element_type=F32).astype(BF16)
        grad = lax.dot_general(grad_pre, first, NT, preferred_element_type=F32).astype(BF16)
        pieces = []
        for j in range(4):
            lanes = slice(j * features, (j + 1) * features)
            pieces.append(jnp.concatenate([out[:, lanes], grad[:, lanes]], axis=1))
        pieces = in_order(mine, pieces)
        for group, (near, far) in enumerate(UNITS):
            own_ref, far_ref, near_ref = outs[3 * group : 3 * group + 3]
            span = slice(group * rows // len(UNITS), (group + 1) * rows // len(UNITS))
            own_ref[p] = pieces[0][span].reshape(own_ref.shape[1:])
            far_ref[p] = pieces[far][span].reshape(own_ref.shape[1:])
            near_ref[0, p] = pieces[near][span].reshape(own_ref.shape[1:])
            near_ref[1, p] = pieces[3][span].reshape(own_ref.shape[1:])
        for ref, value in zip(saved[4 * p : 4 * p + 4], (x, g, act, grad_pre)):
            ref[...] = value


def run_experts(first_expert, here, pieces, first, second):
    away, capacity, wide = pieces[0].shape
    sources = away + here[0].shape[0]
    _, width, units = first.shape
    rows = sources * capacity
    per = len(WAYS)
    part = (per, sources // len(UNITS), capacity, wide)
    results = pl.pallas_call(
        functools.partial(expert_kernel, first_expert, wide // 2),
        out_shape=[jax.ShapeDtypeStruct(shape, BF16) for shape in (part, part, (2, *part))] * len(UNITS)
        + [jax.ShapeDtypeStruct((rows, n), BF16) for n in (width, width, units, units)] * per,
        in_specs=[VMEM] * (len(here) + len(pieces) + 2),
        out_specs=[VMEM] * (3 * len(UNITS) + 4 * per),
        compiler_params=pltpu.CompilerParams(vmem_limit_bytes=16 << 20),
        cost_estimate=pl.CostEstimate(
            flops=8 * per * rows * width * units,
            bytes_accessed=4 * per * width * units,
            transcendentals=per * rows * units,
        ),
        name="experts",
    )(*here, *pieces, first, second)
    parts = [results[3 * group : 3 * group + 3] for group in range(len(UNITS))]
    return parts, results[3 * len(UNITS) :]


def weight_kernel(first_expert, per, *refs):
    saved, rest = refs[: 4 * per], refs[-6:]
    grad_first_hbm, grad_second_hbm, first_buf, second_buf, sems = rest[-5:]
    stores = []
    for p in range(per):
        x, g, act, grad_pre = (ref[...] for ref in saved[4 * p : 4 * p + 4])
        first_buf[p] = lax.dot_general(x, grad_pre, TN, preferred_element_type=F32).astype(BF16)
        stores.append(pltpu.make_async_copy(first_buf.at[p], grad_first_hbm.at[first_expert + p], sems.at[p, 0]))
        stores[-1].start()
        second_buf[p] = lax.dot_general(act, g, TN, preferred_element_type=F32).astype(BF16)
        stores.append(pltpu.make_async_copy(second_buf.at[p], grad_second_hbm.at[first_expert + p], sems.at[p, 1]))
        stores[-1].start()
    for store in stores:
        store.wait()


def weight_grads(chunk, saved, weight_in, weight_out, grads):
    per = len(saved) // 4
    rows, width = saved[0].shape
    units = weight_in.shape[2]
    count = 4 * per
    return pl.pallas_call(
        functools.partial(weight_kernel, chunk * per, per),
        out_shape=[jax.ShapeDtypeStruct(array.shape, BF16) for array in (weight_in, weight_out)],
        in_specs=[VMEM] * count + [HBM] * len(grads),
        out_specs=[HBM] * 2,
        scratch_shapes=[pltpu.VMEM((per, width, units), BF16), pltpu.VMEM((per, units, width), BF16)]
        + [pltpu.SemaphoreType.DMA((per, 2))],
        input_output_aliases={count: 0, count + 1: 1} if grads else {},
        compiler_params=pltpu.CompilerParams(vmem_limit_bytes=20 << 20),
        cost_estimate=pl.CostEstimate(
            flops=4 * per * rows * width * units, bytes_accessed=4 * per * width * units, transcendentals=0
        ),
        name="weight_grads",
    )(*saved, *grads)


def sum_kernel(*refs):
    halves = (len(refs) - 2) // 3
    terms, outs = refs[: 3 * halves], refs[3 * halves :]
    for half in range(halves):
        own, side, passed = terms[3 * half : 3 * half + 3]
        total = own[...].astype(F32) + side[0].astype(F32) + passed[...].astype(F32)
        total = total.astype(BF16)
        for p in range(total.shape[0]):
            for dz, out in enumerate(outs):
                out[0, half * total.shape[0] + p] = total[p, source_of(dz, 0)]
                out[1, half * total.shape[0] + p] = total[p, source_of(dz, 1)]


def sum_rows(terms):
    per, _, capacity, wide = terms[0].shape
    return pl.pallas_call(
        sum_kernel,
        out_shape=[jax.ShapeDtypeStruct((2, len(terms) // 3 * per, capacity, wide), BF16)] * 2,
        in_specs=[VMEM] * len(terms),
        out_specs=[VMEM] * 2,
        compiler_params=pltpu.CompilerParams(vmem_limit_bytes=8 << 20),
        name="sum_rows",
    )(*terms)


def combine_kernel(capacity, exp_dev, picks, place_ref, gate_ref, *refs):
    ins, (out_ref, grad_ref) = refs[:-2], refs[-2:]
    me = lax.axis_index("expert")
    wide = ins[0].shape[-1]
    place = place_ref[...]
    rows, hot = [], []
    for array, index, offset, first_expert in picks:
        rows.append(ins[array][index].reshape(-1, wide))
        first = (me ^ offset) * (exp_dev * capacity) + first_expert * capacity
        hot.append(one_hot(place, first, rows[-1].shape[0]))
    total = lax.dot_general(jnp.concatenate(rows, axis=0), jnp.concatenate(hot, axis=0), TN, preferred_element_type=F32)
    features = out_ref.shape[0]
    out_ref[...] = (gate_ref[...] * total[:features]).astype(BF16)
    grad_ref[...] = total[features:].astype(BF16)


def combine(place, gate, returned, picks, features, exp_dev, capacity):
    count = place.shape[1]
    return pl.pallas_call(
        functools.partial(combine_kernel, capacity, exp_dev, picks),
        out_shape=[jax.ShapeDtypeStruct((features, count), BF16)] * 2,
        in_specs=[VMEM] * (2 + len(returned)),
        out_specs=[VMEM] * 2,
        compiler_params=pltpu.CompilerParams(vmem_limit_bytes=24 << 20),
        name="combine",
    )(place, gate, *returned)


def swap(value, axis, bits):
    size = lax.axis_size(axis)
    return lax.ppermute(value, axis, [(i, i ^ bits) for i in range(size)])


def along_z(buffers):
    direct = [buffers[0]] + [None] * (len(buffers) - 1)
    for dz in reversed(range(1, len(buffers))):
        direct[dz] = swap(buffers[dz], "expert", 2 * dz)
    return direct


def between_cores(direct, *earlier):
    return swap(jnp.stack([rows[1] for rows in after(direct, *earlier)]), "expert", 1)


def after(values, *earlier):
    return lax.optimization_barrier((values, earlier))[0]


def local(tokens, routes, gate_value, weight_in, weight_out, cotangent):
    owners = lax.axis_size("expert")
    exp_dev = weight_in.shape[0]
    count, features = tokens.shape
    capacity = 2 * count // (owners * exp_dev)
    place, gate, buffers = dispatch(
        routes.reshape(1, count), gate_value.reshape(1, count), tokens.T, cotangent.T, owners, exp_dev, capacity
    )
    first, second = load(weight_in, weight_out)
    same, other = buffers[0]
    here = jnp.stack([same, swap(other, "expert", 1)])
    here = [here] + [swap(here, "hidden", bits) for bits in (1, 2, 3)]
    direct = along_z(buffers)[1:]
    rows = pack(direct, between_cores(direct, first, second, *here[1:]))
    per = exp_dev // CHUNKS
    own, near, far = [rows[per * c : per * (c + 1)] for c in range(CHUNKS)], [], []
    for c in range(CHUNKS):
        near.append([swap(rows, "hidden", way[0]) for rows, way in zip(own[c], WAYS)])
    for c in range(CHUNKS):
        pairs = list(zip(own[c], near[c]))
        if c:
            pairs[1] = after(pairs[1], near[c - 1])
        pairs = [jnp.stack(pair) for pair in pairs]
        far.append([swap(pair, "hidden", way[1]) for pair, way in zip(pairs, WAYS)])
    parts, saved = [], []
    for c in range(CHUNKS):
        pieces = [piece for three in zip(own[c], near[c], far[c]) for piece in three]
        part, save = run_experts(per * c, here, pieces, first, second)
        parts.append(part)
        saved.append(save)

    def step_back(c, group):
        mine, other, pair = parts[c][group]
        landed = swap(pair, "hidden", UNITS[group][0])
        return [mine, landed, (other.astype(F32) + landed[1].astype(F32)).astype(BF16)]

    far_terms = [step_back(c, 1) for c in range(CHUNKS)]
    near_terms = [step_back(c, 0) for c in range(CHUNKS)]
    def finish(terms, group):
        passed = [swap(both, "hidden", UNITS[group][1]) for _, _, both in terms]
        totals = sum_rows([rows for (mine, landed, _), last in zip(terms, passed) for rows in (mine, landed, last)])
        return [swap(rows, "expert", 2 * dz) if dz else rows for dz, rows in zip(OFFSETS[group], totals)], totals

    grads = weight_grads(0, after(saved[0], far_terms[0][2], near_terms[0][2]), weight_in, weight_out, [])
    far_terms[0][0] = after(far_terms[0][0], grads)
    homeward = []
    for c in range(CHUNKS):
        if c:
            far_terms[c][2] = after(far_terms[c][2], homeward[-1][-1])
        homeward.append((1, per * c, *finish(far_terms[c : c + 1], 1)))
    near_terms[0][0] = after(near_terms[0][0], homeward[-1][-1])
    homeward.append((0, 0, *finish(near_terms, 0)))
    grads = weight_grads(1, after(saved[1], homeward[-1][-1]), weight_in, weight_out, grads)
    returned, picks = [], []
    for group, first_expert, direct, _ in homeward:
        for j, dz in enumerate(OFFSETS[group]):
            picks.append((len(returned) + j, (0,), 2 * dz, first_expert))
            picks.append((len(returned) + 2, (j,), 2 * dz + 1, first_expert))
        returned.extend([*direct, between_cores(direct, *grads)])
    layer_out, grad_tokens = combine(place, gate, returned, picks, features, exp_dev, capacity)
    return layer_out.T, grad_tokens.T, grads[0], grads[1]


def solution(mesh):
    in_specs = (
        P("expert", "hidden"),
        P("expert", None),
        P("expert", None),
        P("expert", None, "hidden"),
        P("expert", "hidden", None),
        P("expert", "hidden"),
    )
    out_specs = (
        P("expert", "hidden"),
        P("expert", "hidden"),
        P("expert", None, "hidden"),
        P("expert", "hidden", None),
    )

    def whole(*args):
        wide = 2 * args[0].shape[1] // mesh.shape["hidden"]
        capacity = 2 * args[0].shape[0] // args[3].shape[0]
        four = mesh.shape["hidden"] == 4 and args[3].shape[0] == 4 * mesh.shape["expert"]
        fits = four and mesh.shape["expert"] == 8 and wide % 128 == 0 and capacity % 16 == 0
        body = local if fits else general
        return jax.shard_map(body, mesh=mesh, in_specs=in_specs, out_specs=out_specs, check_vma=False)(*args)

    return whole
```
